32 devices in a mesh: dp: 4 (over y, x), row: 4 (over z), col: 2 (over core).
Axes of the slice: x: 2, y: 2, z: 4, core: 2. Of those that a mesh axis runs over, the one named last changes fastest.
Arguments:
- hidden_in: bfloat16 [32, 1024, 768], P(('dp', 'row'), None, 'col'), may hold values from -6 to 6
- encoded: bfloat16 [32, 256, 768], P(('dp', 'row'), None, 'col'), may hold values from -6 to 6
- cotangent: bfloat16 [32, 1024, 768], P(('dp', 'row'), None, 'col'), may hold values from -6 to 6
- piece_start: int32 [32, 2], P(('dp', 'row')), may hold values from 0 to 960, as said below
- image_piece_lengths: int32 [32, 2], P(('dp', 'row')), may hold values from 64 to 256, as said below
- bucket_table: int32 [2047], replicated, may hold values from 0 to 31
- self_query: bfloat16 [768, 768], P('row', 'col'), may hold values from -0.0546875 to 0.0546875
- self_key: bfloat16 [768, 768], P('row', 'col'), may hold values from -0.21875 to 0.21875
- self_value: bfloat16 [768, 768], P('row', 'col'), may hold values from -0.21875 to 0.21875
- self_out: bfloat16 [768, 768], P('col', 'row'), may hold values from -0.875 to 0.875
- rel_weight: bfloat16 [32, 12], P('row', 'col'), may hold values from -3 to 3
- cross_query: bfloat16 [768, 768], P('row', 'col'), may hold values from -0.0546875 to 0.0546875
- cross_key: bfloat16 [768, 768], P('row', 'col'), may hold values from -0.21875 to 0.21875
- cross_value: bfloat16 [768, 768], P('row', 'col'), may hold values from -0.21875 to 0.21875
- cross_out: bfloat16 [768, 768], P('col', 'row'), may hold values from -0.875 to 0.875
- ffn_gate: bfloat16 [768, 2048], P('row', 'col'), may hold values from -0.21875 to 0.21875
- ffn_up: bfloat16 [768, 2048], P('row', 'col'), may hold values from -0.21875 to 0.21875
- ffn_down: bfloat16 [2048, 768], P('col', 'row'), may hold values from -0.25 to 0.25
- gain_self: float32 [768], P('col'), may hold values from 0.25 to 1.75
- gain_cross: float32 [768], P('col'), may hold values from 0.25 to 1.75
- gain_ffn: float32 [768], P('col'), may hold values from 0.25 to 1.75
- gain_final: float32 [768], P('col'), may hold values from 0.25 to 1.75
Outputs:
- output: bfloat16 [32, 1024, 768], P(('dp', 'row'), None, 'col')
- hidden_grad: float32 [32, 1024, 768], P(('dp', 'row'), None, 'col')
- encoded_grad: float32 [32, 256, 768], P(('dp', 'row'), None, 'col')
- self_query_grad: float32 [768, 768], P('row', 'col')
- self_key_grad: float32 [768, 768], P('row', 'col')
- self_value_grad: float32 [768, 768], P('row', 'col')
- self_out_grad: float32 [768, 768], P('col', 'row')
- rel_weight_grad: float32 [32, 12], P('row', 'col')
- cross_query_grad: float32 [768, 768], P('row', 'col')
- cross_key_grad: float32 [768, 768], P('row', 'col')
- cross_value_grad: float32 [768, 768], P('row', 'col')
- cross_out_grad: float32 [768, 768], P('col', 'row')
- ffn_gate_grad: float32 [768, 2048], P('row', 'col')
- ffn_up_grad: float32 [768, 2048], P('row', 'col')
- ffn_down_grad: float32 [2048, 768], P('col', 'row')
- gain_self_grad: float32 [768], P('col')
- gain_cross_grad: float32 [768], P('col')
- gain_ffn_grad: float32 [768], P('col')
- gain_final_grad: float32 [768], P('col')
The draws below stay inside these ranges and needn't reach their ends.
Inputs may be any that keep to these rules, and one draw needn't show every extreme that they name: `piece_start`: the p-th piece of a sequence lies inside positions p * 512 to (p + 1) * 512 - 1, so pieces never intersect. `image_piece_lengths`: some piece has exactly 256 tokens. `bucket_table`: entry j - i + 1023 is the bucket of a key at position j seen from a query at position i.
All inputs are finite; a program needn't handle non-finite values.
Results may differ from the reference program's by a relative error of at most 0.03.
The reference program's roundings to bfloat16 on the way count: a program that leaves them out, or rounds other values in their place, can miss the bound.
Values may be sent and summed in bfloat16 or wider, within the bound.
A program may use at most 256 MiB of HBM per device.

```python
import math
import jax
import jax.numpy as jnp
from jax import lax

D = 768
HEADS = 12
HEAD = 64
FF = 2048
BUCKETS = 32
L = 1024
LE = 256
PIECE = 256
PIECES = 2
SEQS = 32


def piece_layout(key):
    base = jax.random.fold_in(key, 11)
    len_key, pick_key, offset_key = jax.random.split(base, 3)
    lengths = jax.random.randint(len_key, (SEQS, PIECES), PIECE // 4, PIECE + 1)
    chosen = jax.random.randint(pick_key, (), 0, SEQS * PIECES)
    flat_ids = jnp.arange(SEQS * PIECES, dtype=jnp.int32).reshape(SEQS, PIECES)
    lengths = jnp.where(flat_ids == chosen, PIECE, lengths)
    slot_len = L // PIECES
    offsets = jax.random.randint(offset_key, (SEQS, PIECES), 0, slot_len - lengths + 1)
    starts = jnp.arange(PIECES, dtype=jnp.int32)[None, :] * slot_len + offsets
    return (starts.astype(jnp.int32), lengths.astype(jnp.int32))


def draw_piece_start(key, part):
    return piece_layout(key)[0]


def draw_image_piece_lengths(key, part):
    return piece_layout(key)[1]


def place_ends(drawn, rng, least, largest):
    longest = drawn.shape.index(max(drawn.shape))
    spots = []
    for shift in (0, 1):
        where = [jax.random.randint(jax.random.fold_in(rng, axis), (), 0, length) for axis, length in enumerate(drawn.shape)]
        where[longest] = (where[longest] + shift) % drawn.shape[longest]
        spots.append(tuple(where))
    return drawn.at[spots[0]].set(least).at[spots[1]].set(largest)


def block_levels(key, dims, cuts, smallest, largest):
    def one(position, parts):
        steps = jax.random.uniform(jax.random.fold_in(jax.random.fold_in(key, 6), position), (parts,), jnp.float32, smallest / len(cuts), largest / len(cuts))
        return jnp.repeat(jnp.exp(steps), dims[position] // parts).reshape((-1,) + (1,) * (len(dims) - position - 1))

    loudness = one(*cuts[0])
    for cut in cuts[1:]:
        loudness = loudness * one(*cut)
    return loudness


def scatter_about(key, dims, spread, limit, shards=(), held_as=jnp.bfloat16):
    drawn = jax.random.normal(key, dims, jnp.float32) * spread
    if len(shards) > 0:
        drawn = block_levels(key, dims, shards, -0.22, 0.18) * drawn
    return jnp.clip(drawn, min=-limit, max=limit).astype(held_as)


def setup_inputs(seed: int = 0) -> dict:
    seeds = jax.random.split(jax.random.key(seed), 23)
    return {
        "hidden_in": scatter_about(seeds[0], (SEQS, L, D), 1.0, 6.0, ((0, 16), (2, 2))),
        "encoded": scatter_about(seeds[1], (SEQS, LE, D), 1.0, 6.0, ((0, 16), (2, 2))),
        "cotangent": scatter_about(seeds[2], (SEQS, L, D), 1.0, 6.0, ((0, 16), (2, 2))),
        "piece_start": draw_piece_start(jax.random.fold_in(seeds[22], 71), 0),
        "image_piece_lengths": draw_image_piece_lengths(jax.random.fold_in(seeds[22], 71), 0),
        "bucket_table": place_ends(jax.random.randint(seeds[5], (2 * L - 1,), 0, BUCKETS), jax.random.fold_in(seeds[5], 1), 0, BUCKETS - 1).astype(jnp.int32),
        "self_query": scatter_about(seeds[6], (D, HEADS * HEAD), (16 * D) ** -0.5, 0.0546875, ((0, 4), (1, 2))),
        "self_key": scatter_about(seeds[7], (D, HEADS * HEAD), D ** -0.5, 0.21875, ((0, 4), (1, 2))),
        "self_value": scatter_about(seeds[8], (D, HEADS * HEAD), D ** -0.5, 0.21875, ((0, 4), (1, 2))),
        "self_out": scatter_about(seeds[9], (HEADS * HEAD, D), (D // 16) ** -0.5, 0.875, ((0, 2), (1, 4))),
        "rel_weight": scatter_about(seeds[10], (BUCKETS, HEADS), 0.5, 3.0, ((0, 4), (1, 2))),
        "cross_query": scatter_about(seeds[11], (D, HEADS * HEAD), (16 * D) ** -0.5, 0.0546875, ((0, 4), (1, 2))),
        "cross_key": scatter_about(seeds[12], (D, HEADS * HEAD), D ** -0.5, 0.21875, ((0, 4), (1, 2))),
        "cross_value": scatter_about(seeds[13], (D, HEADS * HEAD), D ** -0.5, 0.21875, ((0, 4), (1, 2))),
        "cross_out": scatter_about(seeds[14], (HEADS * HEAD, D), (D // 16) ** -0.5, 0.875, ((0, 2), (1, 4))),
        "ffn_gate": scatter_about(seeds[15], (D, FF), D ** -0.5, 0.21875, ((0, 4), (1, 2))),
        "ffn_up": scatter_about(seeds[16], (D, FF), D ** -0.5, 0.21875, ((0, 4), (1, 2))),
        "ffn_down": scatter_about(seeds[17], (FF, D), (FF // 4) ** -0.5, 0.25, ((0, 2), (1, 4))),
        "gain_self": jnp.clip(1.0 + 0.15 * jax.random.normal(seeds[18], (D,), jnp.float32), 0.25, 1.75),
        "gain_cross": jnp.clip(1.0 + 0.15 * jax.random.normal(seeds[19], (D,), jnp.float32), 0.25, 1.75),
        "gain_ffn": jnp.clip(1.0 + 0.15 * jax.random.normal(seeds[20], (D,), jnp.float32), 0.25, 1.75),
        "gain_final": jnp.clip(1.0 + 0.15 * jax.random.normal(seeds[21], (D,), jnp.float32), 0.25, 1.75),
    }


@jax.custom_vjp
def low(v):
    return lax.optimization_barrier(v.astype(jnp.bfloat16)).astype(jnp.float32)

@jax.custom_vjp
def low_back(v):
    return v

def low_keep(v):
    return (low(v), None)

def low_pass(kept, grad):
    return (grad,)

def back_keep(v):
    return (v, None)

def back_low(kept, grad):
    return (low(grad),)
low.defvjp(low_keep, low_pass)
low_back.defvjp(back_keep, back_low)
EPSILON = 1e-06
PRECISE = lax.Precision.HIGHEST
MASKED = -1e+30
ROOT_TWO_PI = math.sqrt(2.0 / math.pi)

def gelu_tanh(inputs):
    return 0.5 * inputs * (1.0 + jnp.tanh(ROOT_TWO_PI * (inputs + 0.044715 * inputs * inputs * inputs)))

def norm_rows(value_vectors, gain_vec):
    return value_vectors * lax.rsqrt(lax.optimization_barrier(jnp.mean(value_vectors * value_vectors, axis=-1, keepdims=True)) + EPSILON) * gain_vec

def project(value_vectors, weight_matrix):
    return jnp.einsum('...d,de->...e', value_vectors, weight_matrix, precision=PRECISE)

def self_bias(scores, start_row, extras):
    rel_weight, bucket_table, starts, lengths = extras
    block_rows = scores.shape[2]
    key_count = scores.shape[3]
    row_ids = start_row + jnp.arange(block_rows, dtype=jnp.int32)
    column_positions = jnp.arange(key_count, dtype=jnp.int32)
    offsets = column_positions[None, :] - row_ids[:, None] + key_count - 1
    rel_bias = jnp.moveaxis(rel_weight[bucket_table[offsets]], 2, 0)
    piece_ends = starts + lengths
    row_in = (row_ids[None, None, :] >= starts[:, :, None]) & (row_ids[None, None, :] < piece_ends[:, :, None])
    col_in = (column_positions[None, None, :] >= starts[:, :, None]) & (column_positions[None, None, :] < piece_ends[:, :, None])
    inside = jnp.any(row_in[:, :, :, None] & col_in[:, :, None, :], axis=1)
    allowed = inside | (column_positions[None, None, :] <= row_ids[None, :, None])
    return jnp.where(allowed[:, None], scores + rel_bias[None], MASKED)

def open_bias(scores, start_row, extras):
    return scores

def attention(queries, key_rows, value_rows, bias_fn, extras):
    groups, length, head_count, head_width = queries.shape
    block_rows = min(512, length)
    block_count = length // block_rows
    blocks = jnp.moveaxis(queries.reshape(groups, block_count, block_rows, head_count, head_width), 1, 0)
    starts = jnp.arange(block_count, dtype=jnp.int32) * block_rows

    def one_block(query_block, start_row, key_inputs, values_in, extras_in):
        scores = low_back(jnp.einsum('gqhd,gkhd->ghqk', query_block, key_inputs, precision=PRECISE))
        scores = bias_fn(scores, start_row, extras_in)
        row_max = lax.optimization_barrier(jnp.max(scores, axis=-1, keepdims=True))
        exp_scores = jnp.exp(scores - row_max)
        softmax_w = exp_scores / lax.optimization_barrier(jnp.sum(exp_scores, axis=-1, keepdims=True))
        return jnp.einsum('ghqk,gkhd->gqhd', low(softmax_w), values_in, precision=PRECISE)
    saved = jax.checkpoint(one_block)
    mixed_rows = lax.map(lambda block_item: saved(block_item[0], block_item[1], key_rows, value_rows, extras), (blocks, starts))
    return jnp.moveaxis(mixed_rows, 0, 1).reshape(groups, length, head_count * head_width)

def layer(weights, gains, inputs, encoded_rows, fixed):
    self_query, self_key, self_value, self_out, rel_weight, cross_query, cross_key, cross_value, cross_out, ffn_gate, ffn_up, ffn_down = weights
    gain_self, gain_cross, gain_ffn, gain_final = gains
    starts, lengths, bucket_table = fixed

    def heads_of(value_vectors, weight_matrix):
        return low_back(low(project(value_vectors, weight_matrix))).reshape(value_vectors.shape[0], value_vectors.shape[1], HEADS, HEAD)
    normed_one = low(norm_rows(inputs, gain_self))
    mixed_one = attention(heads_of(normed_one, self_query), heads_of(normed_one, self_key), heads_of(normed_one, self_value), self_bias, (rel_weight, bucket_table, starts, lengths))
    mixed_one = low_back(low(mixed_one))
    first_sum = inputs + low_back(project(mixed_one, self_out))
    normed_two = low(norm_rows(first_sum, gain_cross))
    mixed_two = attention(heads_of(normed_two, cross_query), heads_of(encoded_rows, cross_key), heads_of(encoded_rows, cross_value), open_bias, ())
    mixed_two = low_back(low(mixed_two))
    second_sum = first_sum + low_back(project(mixed_two, cross_out))
    normed_three = low(norm_rows(second_sum, gain_ffn))
    gate_pre = low_back(project(normed_three, ffn_gate))
    up_pre = low_back(project(normed_three, ffn_up))
    hidden_mid = low_back(low(gelu_tanh(gate_pre) * up_pre))
    third_sum = second_sum + low_back(project(hidden_mid, ffn_down))
    return norm_rows(third_sum, gain_final)

def reference(hidden_in, encoded, cotangent, piece_start, image_piece_lengths, bucket_table, self_query, self_key, self_value, self_out, rel_weight, cross_query, cross_key, cross_value, cross_out, ffn_gate, ffn_up, ffn_down, gain_self, gain_cross, gain_ffn, gain_final):
    weights = tuple((matrix.astype(jnp.float32) for matrix in (self_query, self_key, self_value, self_out, rel_weight, cross_query, cross_key, cross_value, cross_out, ffn_gate, ffn_up, ffn_down)))
    gains = (gain_self.astype(jnp.float32), gain_cross.astype(jnp.float32), gain_ffn.astype(jnp.float32), gain_final.astype(jnp.float32))
    total_seqs = hidden_in.shape[0]
    group_size = math.gcd(total_seqs, max(1, 4096 // hidden_in.shape[1]))
    group_count = total_seqs // group_size

    def by_group(value_vectors):
        return value_vectors.reshape((group_count, group_size) + value_vectors.shape[1:])

    def one_group(carried, group_item):
        inputs, encoded_rows, grad_rows, starts, lengths = group_item

        def run(weights_in, gains_in, inputs_in, encoded_in):
            return layer(weights_in, gains_in, inputs_in, encoded_in, (starts, lengths, bucket_table))
        result, pullback = jax.vjp(run, weights, gains, inputs.astype(jnp.float32), encoded_rows.astype(jnp.float32))
        weight_grads, gain_grads, input_grad, encoded_grad = pullback(grad_rows.astype(jnp.float32))
        carried = jax.tree.map(jnp.add, carried, (weight_grads, gain_grads))
        return (carried, (result.astype(jnp.bfloat16), input_grad, encoded_grad))
    initial = jax.tree.map(jnp.zeros_like, (weights, gains))
    (weight_sums, gain_sums), (outputs, input_grads, encoded_grads) = lax.scan(one_group, initial, (by_group(hidden_in), by_group(encoded), by_group(cotangent), by_group(piece_start), by_group(image_piece_lengths)))
    return (outputs.reshape(hidden_in.shape), input_grads.reshape(hidden_in.shape), encoded_grads.reshape(encoded.shape), weight_sums[0], weight_sums[1], weight_sums[2], weight_sums[3], weight_sums[4], weight_sums[5], weight_sums[6], weight_sums[7], weight_sums[8], weight_sums[9], weight_sums[10], weight_sums[11], gain_sums[0], gain_sums[1], gain_sums[2], gain_sums[3])
```

```python
import math

import jax
import jax.numpy as jnp
from jax import lax
from jax.experimental import pallas as pl
from jax.experimental.pallas import tpu as pltpu
from jax.sharding import PartitionSpec as P

D = 768
HALF = 384
L = 1024
LE = 256
BUCKETS = 32
SPAN = 1536
EPSILON = 1e-06
MASKED = -1e30
ROOT_TWO_PI = math.sqrt(2.0 / math.pi)
MESH = pl.DeviceIdType.MESH
ROWS = 4
QUAD = 4
BLOCK = D // ROWS
PIECE = BLOCK // QUAD
f32 = jnp.float32
bf16 = jnp.bfloat16
NT = (((1,), (1,)), ((), ()))
NN = (((1,), (0,)), ((), ()))
TN = (((0,), (0,)), ((), ()))
VMEM_LIMIT = 60 * 2**20


def dot(a, b, dims):
    return lax.dot_general(a, b, dims, preferred_element_type=f32)


def lanes(offset, rows=L):
    return pl.BlockSpec((rows, 128), lambda h: (0, offset + h))


def qkv_lanes(which):
    return pl.BlockSpec((L, 128), lambda h: (0, (h // 3) * 9 + 3 * which + h % 3))


def kv_lanes(which):
    return pl.BlockSpec((LE, 128), lambda h: (0, (h // 3) * 6 + 3 * which + h % 3))


def head_of(x, h):
    lane = lax.broadcasted_iota(jnp.int32, x.shape, 1)
    return jnp.where((lane >= 64 * h) & (lane < 64 * h + 64), x, jnp.zeros_like(x))


def transposed(x):
    return x.astype(f32).T.astype(bf16)


def spread_bias(t8_ref, table):
    for h in range(2):
        t = t8_ref[h]
        for m in range(16):
            table[h, 8 * m : 8 * m + 8, :] = pltpu.roll(t, 8 * m, 1)


def allowed_rows(piece_ref, base, rows, width):
    s0 = piece_ref[0]
    s1 = piece_ref[1]
    e0 = piece_ref[2]
    e1 = piece_ref[3]
    c = lax.broadcasted_iota(jnp.int32, (1, width), 1) + base
    last = jnp.where(
        (c >= s0) & (c < e0), e0 - 1, jnp.where((c >= s1) & (c < e1), e1 - 1, 0)
    )
    last = jnp.maximum(c, last)
    return lax.broadcasted_iota(jnp.int32, (rows, width), 0) + base <= last


def extent(qb, width):
    return 512 * ((qb * width) // 512 + 1)


def biased_scores(k_ref, q_head, table, h, base, width, ext, ok):
    s = dot(k_ref[:ext, :], q_head, NT)
    bias = jnp.concatenate(
        [table[h, :, pl.ds(base - 128 * g + 512, width)] for g in range(ext // 128)], axis=0
    )
    s = s + bias
    tail = jnp.where(ok, s[base:], MASKED)
    return tail if base == 0 else jnp.concatenate([s[:base], tail], axis=0)


def softmax_cols(s):
    m = jnp.max(s, axis=0, keepdims=True)
    p = jnp.exp(s - m)
    total = jnp.sum(p, axis=0, keepdims=True)
    return (p.astype(bf16), total, m)


def tasks_of(width, group):
    tasks = [(qb, h) for qb in range(L // width) for h in range(2)]
    return [tasks[i : i + group] for i in range(0, len(tasks), group)]


def self_forward_body(piece_ref, q_ref, k_ref, v_ref, t8_ref, o_ref, lse_ref, table):
    width = 256
    vt = transposed(v_ref[...])
    spread_bias(t8_ref, table)
    oks = [
        allowed_rows(piece_ref, qb * width, extent(qb, width) - qb * width, width)
        for qb in range(L // width)
    ]
    outs = {}
    for group in tasks_of(width, 8):
        scored = [
            biased_scores(
                k_ref,
                head_of(q_ref[pl.ds(qb * width, width), :], h),
                table,
                h,
                qb * width,
                width,
                extent(qb, width),
                oks[qb],
            )
            for qb, h in group
        ]
        weights = [softmax_cols(s) for s in scored]
        for (qb, h), (p, total, m) in zip(group, weights):
            mixed = dot(vt[64 * h : 64 * h + 64, : extent(qb, width)], p, NN)
            outs[(qb, h)] = mixed * (1.0 / total)
            lse_ref[0, h : h + 1, pl.ds(qb * width, width)] = m + jnp.log(total)
            if h == 1:
                o_ref[pl.ds(qb * width, width), :] = (
                    jnp.concatenate([outs[(qb, 0)], outs[(qb, 1)]], axis=0).T.astype(bf16)
                )


def self_forward(qkv, t8, piece):
    return pl.pallas_call(
        self_forward_body,
        grid=(6,),
        in_specs=[
            pl.BlockSpec(memory_space=pltpu.SMEM),
            qkv_lanes(0),
            qkv_lanes(1),
            qkv_lanes(2),
            pl.BlockSpec((2, 8, SPAN), lambda h: (h, 0, 0)),
        ],
        out_specs=[lanes(0), pl.BlockSpec((1, 2, L), lambda h: (h, 0, 0))],
        out_shape=[
            jax.ShapeDtypeStruct((L, D), bf16),
            jax.ShapeDtypeStruct((6, 2, L), f32),
        ],
        scratch_shapes=[pltpu.VMEM((2, 128, SPAN), f32)],
        compiler_params=pltpu.CompilerParams(vmem_limit_bytes=VMEM_LIMIT),
        name="self_forward",
    )(piece, qkv, qkv, qkv, t8)


def head_deltas(a_ref, da_ref):
    prod = (a_ref[...].astype(f32) * da_ref[...].astype(f32)).T
    return [jnp.sum(prod[64 * h : 64 * h + 64], axis=0, keepdims=True) for h in range(2)]


def self_backward_body(
    piece_ref,
    q_ref,
    k_ref,
    v_ref,
    t8_ref,
    a_ref,
    da_ref,
    lse_ref,
    dq_ref,
    dk_ref,
    dv_ref,
    diag_ref,
    table,
    spans,
    dk_sum,
    dv_sum,
):
    width = 256
    delta = head_deltas(a_ref, da_ref)
    kt = transposed(k_ref[...])
    spread_bias(t8_ref, table)
    spans[...] = jnp.zeros_like(spans)
    dk_sum[...] = jnp.zeros_like(dk_sum)
    dv_sum[...] = jnp.zeros_like(dv_sum)
    for group in tasks_of(width, 2):
        qb = group[0][0]
        base = qb * width
        ext = extent(qb, width)
        ok = allowed_rows(piece_ref, base, ext - base, width)
        q = q_ref[pl.ds(base, width), :]
        da = da_ref[pl.ds(base, width), :]
        scored = [
            biased_scores(k_ref, head_of(q, h), table, h, base, width, ext, ok) for _, h in group
        ]
        dprobs = [dot(v_ref[:ext, :], head_of(da, h), NT) for _, h in group]
        low = []
        for h in range(2):
            p = jnp.exp(scored[h] - lse_ref[0, h : h + 1, pl.ds(base, width)])
            ds = p * (dprobs[h] - delta[h][:, base : base + width])
            for g in range(ext // 128):
                spans[h, :, pl.ds(base - 128 * g + 512, width)] += ds[128 * g : 128 * g + 128]
            low.append((p.astype(bf16), ds.astype(bf16)))
        dks = [dot(ds, q, NN) for _, ds in low]
        dvs = [dot(p, da, NN) for p, _ in low]
        dqs = [dot(kt[64 * h : 64 * h + 64, :ext], low[h][1], NN) for h in range(2)]
        lane = lax.broadcasted_iota(jnp.int32, (ext, 128), 1)
        dk_sum[:ext] += jnp.where(lane < 64, dks[0], dks[1])
        dv_sum[:ext] += jnp.where(lane < 64, dvs[0], dvs[1])
        dq_ref[pl.ds(base, width), :] = jnp.concatenate(dqs, axis=0).T.astype(bf16)
    dk_ref[...] = dk_sum[...].astype(bf16)
    dv_ref[...] = dv_sum[...].astype(bf16)
    for h in range(2):
        total = spans[h, 0:8, :]
        for m in range(1, 16):
            total = total + pltpu.roll(spans[h, 8 * m : 8 * m + 8, :], SPAN - 8 * m, 1)
        diag_ref[h] = total


def self_backward(qkv, t8, piece, mixed, dmixed, lse):
    return pl.pallas_call(
        self_backward_body,
        grid=(6,),
        in_specs=[
            pl.BlockSpec(memory_space=pltpu.SMEM),
            qkv_lanes(0),
            qkv_lanes(1),
            qkv_lanes(2),
            pl.BlockSpec((2, 8, SPAN), lambda h: (h, 0, 0)),
            lanes(0),
            lanes(0),
            pl.BlockSpec((1, 2, L), lambda h: (h, 0, 0)),
        ],
        out_specs=[
            lanes(0),
            lanes(0),
            lanes(0),
            pl.BlockSpec((2, 8, SPAN), lambda h: (h, 0, 0)),
        ],
        out_shape=[jax.ShapeDtypeStruct((L, D), bf16)] * 3
        + [jax.ShapeDtypeStruct((12, 8, SPAN), f32)],
        scratch_shapes=[
            pltpu.VMEM((2, 128, SPAN), f32),
            pltpu.VMEM((2, 128, SPAN), f32),
            pltpu.VMEM((L, 128), f32),
            pltpu.VMEM((L, 128), f32),
        ],
        compiler_params=pltpu.CompilerParams(vmem_limit_bytes=VMEM_LIMIT),
        name="self_backward",
    )(piece, qkv, qkv, qkv, t8, mixed, dmixed, lse)


def cross_forward_body(q_ref, k_ref, v_ref, o_ref, lse_ref):
    width = 256
    vt = transposed(v_ref[...])
    outs = {}
    for group in tasks_of(width, 8):
        scored = [
            dot(k_ref[...], head_of(q_ref[pl.ds(qb * width, width), :], h), NT) for qb, h in group
        ]
        weights = [softmax_cols(s) for s in scored]
        for (qb, h), (p, total, m) in zip(group, weights):
            outs[(qb, h)] = dot(vt[64 * h : 64 * h + 64, :], p, NN) * (1.0 / total)
            lse_ref[0, h : h + 1, pl.ds(qb * width, width)] = m + jnp.log(total)
            if h == 1:
                o_ref[pl.ds(qb * width, width), :] = (
                    jnp.concatenate([outs[(qb, 0)], outs[(qb, 1)]], axis=0).T.astype(bf16)
                )


def cross_forward(queries, key_values):
    return pl.pallas_call(
        cross_forward_body,
        grid=(6,),
        in_specs=[lanes(0), kv_lanes(0), kv_lanes(1)],
        out_specs=[lanes(0), pl.BlockSpec((1, 2, L), lambda h: (h, 0, 0))],
        out_shape=[
            jax.ShapeDtypeStruct((L, D), bf16),
            jax.ShapeDtypeStruct((6, 2, L), f32),
        ],
        compiler_params=pltpu.CompilerParams(vmem_limit_bytes=VMEM_LIMIT),
        name="cross_forward",
    )(queries, key_values, key_values)


def cross_backward_body(q_ref, k_ref, v_ref, a_ref, da_ref, lse_ref, dq_ref, dk_ref, dv_ref):
    width = 256
    delta = head_deltas(a_ref, da_ref)
    kt = transposed(k_ref[...])
    lane = lax.broadcasted_iota(jnp.int32, (LE, 128), 1)
    outs = {}
    dks = [None, None]
    dvs = [None, None]
    for group in tasks_of(width, 4):
        scored = [
            dot(k_ref[...], head_of(q_ref[pl.ds(qb * width, width), :], h), NT) for qb, h in group
        ]
        dprobs = [
            dot(v_ref[...], head_of(da_ref[pl.ds(qb * width, width), :], h), NT) for qb, h in group
        ]
        low = []
        for (qb, h), s, dp in zip(group, scored, dprobs):
            p = jnp.exp(s - lse_ref[0, h : h + 1, pl.ds(qb * width, width)])
            ds = p * (dp - delta[h][:, qb * width : (qb + 1) * width])
            low.append((p.astype(bf16), ds.astype(bf16)))
        for (qb, h), (p, ds) in zip(group, low):
            dk = dot(ds, q_ref[pl.ds(qb * width, width), :], NN)
            dv = dot(p, da_ref[pl.ds(qb * width, width), :], NN)
            dks[h] = dk if dks[h] is None else dks[h] + dk
            dvs[h] = dv if dvs[h] is None else dvs[h] + dv
            outs[(qb, h)] = dot(kt[64 * h : 64 * h + 64, :], ds, NN)
            if h == 1:
                dq_ref[pl.ds(qb * width, width), :] = (
                    jnp.concatenate([outs[(qb, 0)], outs[(qb, 1)]], axis=0).T.astype(bf16)
                )
    dk_ref[...] = jnp.where(lane < 64, dks[0], dks[1]).astype(bf16)
    dv_ref[...] = jnp.where(lane < 64, dvs[0], dvs[1]).astype(bf16)


def cross_backward(queries, key_values, mixed, dmixed, lse):
    return pl.pallas_call(
        cross_backward_body,
        grid=(6,),
        in_specs=[
            lanes(0),
            kv_lanes(0),
            kv_lanes(1),
            lanes(0),
            lanes(0),
            pl.BlockSpec((1, 2, L), lambda h: (h, 0, 0)),
        ],
        out_specs=[lanes(0), lanes(0, LE), lanes(0, LE)],
        out_shape=[jax.ShapeDtypeStruct((L, D), bf16)] + [jax.ShapeDtypeStruct((LE, D), bf16)] * 2,
        compiler_params=pltpu.CompilerParams(vmem_limit_bytes=VMEM_LIMIT),
        name="cross_backward",
    )(queries, key_values, key_values, mixed, dmixed, lse)


def place():
    dp = lax.axis_index("dp")
    return (dp, dp % QUAD, lax.axis_index("row"), lax.axis_index("col"))


def quad_mate(dp, quarter, flip):
    return dp - quarter + (quarter ^ flip)


def greet_all(dp, quarter, row, col):
    barrier = pltpu.get_barrier_semaphore()
    for s in range(1, ROWS):
        pl.semaphore_signal(
            barrier, inc=1, device_id=(dp, (row + s) % ROWS, col), device_id_type=MESH
        )
    for k in range(1, QUAD):
        pl.semaphore_signal(
            barrier, inc=1, device_id=(quad_mate(dp, quarter, k), row, col), device_id_type=MESH
        )
    pl.semaphore_signal(barrier, inc=1, device_id=(dp, row, 1 - col), device_id_type=MESH)
    pl.semaphore_wait(barrier, ROWS + QUAD - 1)


def gather_body(count, *refs):
    blocks = refs[:count]
    wholes = refs[count : 2 * count]
    z_send, z_recv, q_send, q_recv, c_send, c_recv, local_sem = refs[2 * count :]
    dp, quarter, row, col = place()
    greet_all(dp, quarter, row, col)
    partner = (dp, row, 1 - col)
    started = []

    def begin(copy):
        copy.start()
        started.append(copy)
        return copy

    def part(i, r, q):
        wide = blocks[i].shape[1]
        at = pl.multiple_of(r * BLOCK + q * PIECE, PIECE)
        return wholes[i].at[pl.ds(at, PIECE), pl.ds(pl.multiple_of(col * wide, 128), wide)]

    z_copies = {}
    own = []
    c_copies = []
    for i in range(count):
        wide = blocks[i].shape[1]
        whole_block = wholes[i].at[
            pl.ds(pl.multiple_of(row * BLOCK, BLOCK), BLOCK),
            pl.ds(pl.multiple_of(col * wide, 128), wide),
        ]
        for s in range(1, ROWS):
            z_copies[(i, s)] = begin(
                pltpu.make_async_remote_copy(
                    src_ref=blocks[i].at[pl.ds(pl.multiple_of(quarter * PIECE, PIECE), PIECE), :],
                    dst_ref=part(i, row, quarter),
                    send_sem=z_send.at[i, s - 1],
                    recv_sem=z_recv.at[i, s - 1],
                    device_id=(dp, (row + s) % ROWS, col),
                    device_id_type=MESH,
                )
            )
        c_copies.append(
            begin(
                pltpu.make_async_remote_copy(
                    src_ref=blocks[i],
                    dst_ref=whole_block,
                    send_sem=c_send.at[i, 0, 0],
                    recv_sem=c_recv.at[i, 0, 0],
                    device_id=partner,
                    device_id_type=MESH,
                )
            )
        )
        local = pltpu.make_async_copy(blocks[i], whole_block, local_sem.at[i])
        local.start()
        own.append(local)
    q_copies = {}

    def hand_over(i, s, k, r):
        ref = part(i, r, quarter ^ k)
        c_copies.append(
            begin(
                pltpu.make_async_remote_copy(
                    src_ref=ref,
                    dst_ref=ref,
                    send_sem=c_send.at[i, s, k],
                    recv_sem=c_recv.at[i, s, k],
                    device_id=partner,
                    device_id_type=MESH,
                )
            )
        )

    def spread(i):
        for s in range(1, ROWS):
            z_copies[(i, s)].wait_recv()
            r = (row - s + ROWS) % ROWS
            ref = part(i, r, quarter)
            for k in range(1, QUAD):
                q_copies[(i, s, k)] = begin(
                    pltpu.make_async_remote_copy(
                        src_ref=ref,
                        dst_ref=ref,
                        send_sem=q_send.at[i, s - 1, k - 1],
                        recv_sem=q_recv.at[i, s - 1, k - 1],
                        device_id=(quad_mate(dp, quarter, k), row, col),
                        device_id_type=MESH,
                    )
                )
            hand_over(i, s, 0, r)

    def share(i):
        for s in range(1, ROWS):
            for k in range(1, QUAD):
                q_copies[(i, s, k)].wait_recv()
                hand_over(i, s, k, (row - s + ROWS) % ROWS)

    for i in range(count):
        spread(i)
        if i > 0:
            share(i - 1)
    share(count - 1)
    for copy in own:
        copy.wait()
    for copy in c_copies:
        copy.wait_recv()
    for copy in started:
        copy.wait_send()


def gather_weights(blocks, number):
    count = len(blocks)
    wholes = [jax.ShapeDtypeStruct((D, 2 * b.shape[1]), b.dtype) for b in blocks]
    dma = pltpu.SemaphoreType.DMA
    return pl.pallas_call(
        lambda *refs: gather_body(count, *refs),
        out_shape=wholes,
        in_specs=[pl.BlockSpec(memory_space=pl.ANY)] * count,
        out_specs=[pl.BlockSpec(memory_space=pl.ANY)] * count,
        scratch_shapes=[
            dma((count, ROWS - 1)),
            dma((count, ROWS - 1)),
            dma((count, ROWS - 1, QUAD - 1)),
            dma((count, ROWS - 1, QUAD - 1)),
            dma((count, ROWS, QUAD)),
            dma((count, ROWS, QUAD)),
            dma((count,)),
        ],
        compiler_params=pltpu.CompilerParams(collective_id=number, has_side_effects=True),
        name="gather_weights",
    )(*blocks)


def swap_features(x, col):
    own = lax.dynamic_index_in_dim(x, col, 0, keepdims=False)
    other = lax.dynamic_index_in_dim(x, 1 - col, 0, keepdims=False)
    came = lax.ppermute(other, "col", [(0, 1), (1, 0)])
    return jnp.where(
        col == 0, jnp.concatenate([own, came], axis=1), jnp.concatenate([came, own], axis=1)
    )


def swap_back(y, col):
    own = lax.dynamic_slice_in_dim(y, col * HALF, HALF, 1)
    other = lax.dynamic_slice_in_dim(y, (1 - col) * HALF, HALF, 1)
    came = lax.ppermute(other, "col", [(0, 1), (1, 0)])
    return jnp.where(col == 0, jnp.stack([own, came]), jnp.stack([came, own]))


def inverse_rms(v):
    return lax.rsqrt(jnp.mean(v * v, axis=-1, keepdims=True) + EPSILON)


def norm_backward(v, r, gain, dn):
    inner = jnp.sum(dn * gain * v, axis=-1, keepdims=True)
    dv = dn * gain * r - v * (r * r * r) * (inner / D)
    return (dv, jnp.sum(dn * v * r, axis=0))


def gelu_parts(t):
    inner = ROOT_TWO_PI * (t + 0.044715 * t * t * t)
    th = jnp.tanh(inner)
    value = 0.5 * t * (1.0 + th)
    slope = 0.5 * (1.0 + th) + 0.5 * t * (1.0 - th * th) * ROOT_TWO_PI * (
        1.0 + 3.0 * 0.044715 * t * t
    )
    return (value, slope)


def body(
    hidden_in,
    encoded,
    cotangent,
    piece_start,
    image_piece_lengths,
    bucket_table,
    self_query,
    self_key,
    self_value,
    self_out,
    rel_weight,
    cross_query,
    cross_key,
    cross_value,
    cross_out,
    ffn_gate,
    ffn_up,
    ffn_down,
    gain_self,
    gain_cross,
    gain_ffn,
    gain_final,
):
    col = lax.axis_index("col")
    row = lax.axis_index("row")
    blocks = (
        jnp.concatenate([self_query, self_key, self_value], axis=1),
        self_out.T,
        cross_query,
        jnp.concatenate([cross_key, cross_value], axis=1),
        cross_out.T,
        jnp.concatenate([ffn_gate, ffn_up], axis=1),
        ffn_down.T,
    )
    w_qkv, w_out_t, c_query, c_kv, c_out_t, f_gu, f_down_t = gather_weights(blocks, 0)
    small = lax.all_gather(
        jnp.concatenate([gain_self, gain_cross, gain_ffn, gain_final]), "col", axis=0
    )
    gains = small.reshape(2, 4, HALF).transpose(1, 0, 2).reshape(4, D)
    g_self, g_cross, g_ffn, g_final = gains[0], gains[1], gains[2], gains[3]
    w_rel = lax.all_gather(
        lax.all_gather(rel_weight, "row", axis=0, tiled=True), "col", axis=1, tiled=True
    )
    onehot = (
        bucket_table[:SPAN, None] == jnp.arange(BUCKETS, dtype=jnp.int32)[None, :]
    ).astype(f32)
    bias_of = jnp.dot(onehot, w_rel.astype(f32), precision=lax.Precision.HIGHEST).T
    flipped = bias_of[:, ::-1]
    t8 = jnp.stack([jnp.roll(flipped, s, axis=1) for s in range(8)], axis=1)
    starts = lax.dynamic_index_in_dim(piece_start, col, 0, keepdims=False)
    lengths = lax.dynamic_index_in_dim(image_piece_lengths, col, 0, keepdims=False)
    piece = jnp.concatenate([starts, starts + lengths])

    x = swap_features(hidden_in, col).astype(f32)
    enc = swap_features(encoded, col)
    grad_out = swap_features(cotangent, col).astype(f32)

    r1 = inverse_rms(x)
    n1 = (x * r1 * g_self).astype(bf16)
    qkv = dot(n1, w_qkv, NN).astype(bf16)
    a1, lse1 = self_forward(qkv, t8, piece)
    h1 = x + dot(a1, w_out_t, NT)
    r2 = inverse_rms(h1)
    n2 = (h1 * r2 * g_cross).astype(bf16)
    q2 = dot(n2, c_query, NN).astype(bf16)
    kv2 = dot(enc, c_kv, NN).astype(bf16)
    a2, lse2 = cross_forward(q2, kv2)
    h2 = h1 + dot(a2, c_out_t, NT)
    r3 = inverse_rms(h2)
    n3 = (h2 * r3 * g_ffn).astype(bf16)
    gu = dot(n3, f_gu, NN).reshape(L, 2, 2, 1024)
    gate, up = gu[:, :, 0], gu[:, :, 1]
    act, slope = gelu_parts(gate)
    mid = (act * up).astype(bf16).reshape(L, 2048)
    h3 = h2 + dot(mid, f_down_t, NT)
    r4 = inverse_rms(h3)
    output = (h3 * r4 * g_final).astype(bf16)

    dh3, dg_final = norm_backward(h3, r4, g_final, grad_out)
    e3 = dh3.astype(bf16)
    gr_down = dot(e3, mid, TN)
    dmid = dot(e3, f_down_t, NN).astype(bf16).astype(f32).reshape(L, 2, 1024)
    dgu = jnp.stack([dmid * up * slope, dmid * act], axis=2).astype(bf16).reshape(L, 4096)
    gr_gu = dot(n3, dgu, TN)
    dn3 = dot(dgu, f_gu, NT)
    back3, dg_ffn = norm_backward(h2, r3, g_ffn, dn3)
    dh2 = dh3 + back3
    e2 = dh2.astype(bf16)
    gr_co = dot(e2, a2, TN)
    da2 = dot(e2, c_out_t, NN).astype(bf16)
    dq2, dk2, dv2 = cross_backward(q2, kv2, a2, da2, lse2)
    gr_cq = dot(n2, dq2, TN)
    dkv2 = jnp.concatenate([dk2[:, :HALF], dv2[:, :HALF], dk2[:, HALF:], dv2[:, HALF:]], axis=1)
    gr_ckv = dot(enc, dkv2, TN)
    enc_grad = dot(dkv2, c_kv, NT)
    dn2 = dot(dq2, c_query, NT)
    back2, dg_cross = norm_backward(h1, r2, g_cross, dn2)
    dh1 = dh2 + back2
    e1 = dh1.astype(bf16)
    gr_out = dot(e1, a1, TN)
    da1 = dot(e1, w_out_t, NN).astype(bf16)
    dq1, dk1, dv1, diag = self_backward(qkv, t8, piece, a1, da1, lse1)
    dqkv = jnp.concatenate(
        [part[:, HALF * c : HALF * (c + 1)] for c in range(2) for part in (dq1, dk1, dv1)], axis=1
    )
    gr_qkv = dot(n1, dqkv, TN)
    dn1 = dot(dqkv, w_qkv, NT)
    back1, dg_self = norm_backward(x, r1, g_self, dn1)
    hidden_grad = dh1 + back1

    spans = sum(jnp.roll(diag[:, s], -s, axis=1) for s in range(8))[:, ::-1]
    gr_rel = jnp.dot(onehot.T, spans.T, precision=lax.Precision.HIGHEST)

    def reduced(g):
        g = g.astype(bf16)
        g = lax.psum_scatter(g, "col", scatter_dimension=1, tiled=True)
        g = lax.psum_scatter(g, "row", scatter_dimension=0, tiled=True)
        return lax.psum(g, "dp").astype(f32)

    gr_qkv = reduced(gr_qkv)
    gr_out = reduced(gr_out).T
    gr_cq = reduced(gr_cq)
    gr_ckv = reduced(gr_ckv)
    gr_co = reduced(gr_co).T
    gr_gu = reduced(gr_gu)
    gr_down = reduced(gr_down).T
    gain_sums = jnp.stack([dg_self, dg_cross, dg_ffn, dg_final])
    gain_sums, gr_rel = lax.psum((gain_sums, gr_rel), ("dp", "row", "col"))
    gain_sums = lax.dynamic_slice_in_dim(gain_sums, col * HALF, HALF, 1)
    gr_rel = lax.dynamic_slice(gr_rel, (row * 8, col * 6), (8, 6))
    return (
        swap_back(output, col),
        swap_back(hidden_grad, col),
        swap_back(enc_grad, col),
        gr_qkv[:, :HALF],
        gr_qkv[:, HALF : 2 * HALF],
        gr_qkv[:, 2 * HALF :],
        gr_out,
        gr_rel,
        gr_cq,
        gr_ckv[:, :HALF],
        gr_ckv[:, HALF:],
        gr_co,
        gr_gu[:, :1024],
        gr_gu[:, 1024:],
        gr_down,
        gain_sums[0],
        gain_sums[1],
        gain_sums[2],
        gain_sums[3],
    )


def solution(mesh):
    batch = P(("dp", "row"), None, "col")
    inward = P("row", "col")
    outward = P("col", "row")
    gain = P("col")
    weights = (
        (inward,) * 3 + (outward, inward) + (inward,) * 3 + (outward,) + (inward,) * 2 + (outward,)
    )
    placed = (batch,) * 3 + (P(("dp", "row"), None),) * 2 + (P(),) + weights + (gain,) * 4
    return jax.shard_map(
        body,
        mesh=mesh,
        in_specs=placed,
        out_specs=(batch,) * 3 + weights + (gain,) * 4,
        check_vma=False,
    )
```

```python
import math

import jax
import jax.numpy as jnp
from jax import lax
from jax.experimental import pallas as pl
from jax.experimental.pallas import tpu as pltpu
from jax.sharding import PartitionSpec as P

D = 768
HALF = 384
L = 1024
LE = 256
BUCKETS = 32
SPAN = 1536
EPSILON = 1e-06
MASKED = -1e30
ROOT_TWO_PI = math.sqrt(2.0 / math.pi)
MESH = pl.DeviceIdType.MESH
ROWS = 4
QUAD = 4
BLOCK = D // ROWS
PIECE = BLOCK // QUAD
f32 = jnp.float32
bf16 = jnp.bfloat16
NT = (((1,), (1,)), ((), ()))
NN = (((1,), (0,)), ((), ()))
TN = (((0,), (0,)), ((), ()))
VMEM_LIMIT = 60 * 2**20


def dot(a, b, dims):
    return lax.dot_general(a, b, dims, preferred_element_type=f32)


def lanes(offset, rows=L):
    return pl.BlockSpec((rows, 128), lambda h: (0, offset + h))


def qkv_lanes(which):
    return pl.BlockSpec((L, 128), lambda h: (0, (h // 3) * 9 + 3 * which + h % 3))


def kv_lanes(which):
    return pl.BlockSpec((LE, 128), lambda h: (0, (h // 3) * 6 + 3 * which + h % 3))


def head_of(x, h):
    lane = lax.broadcasted_iota(jnp.int32, x.shape, 1)
    return jnp.where((lane >= 64 * h) & (lane < 64 * h + 64), x, jnp.zeros_like(x))


def transposed(x):
    return x.astype(f32).T.astype(bf16)


def spread_bias(t8_ref, table):
    for h in range(2):
        t = t8_ref[h]
        for m in range(16):
            table[h, 8 * m : 8 * m + 8, :] = pltpu.roll(t, 8 * m, 1)


def allowed_rows(piece_ref, base, rows, width):
    s0 = piece_ref[0]
    s1 = piece_ref[1]
    e0 = piece_ref[2]
    e1 = piece_ref[3]
    c = lax.broadcasted_iota(jnp.int32, (1, width), 1) + base
    last = jnp.where(
        (c >= s0) & (c < e0), e0 - 1, jnp.where((c >= s1) & (c < e1), e1 - 1, 0)
    )
    last = jnp.maximum(c, last)
    return lax.broadcasted_iota(jnp.int32, (rows, width), 0) + base <= last


def extent(qb, width):
    return 512 * ((qb * width) // 512 + 1)


def biased_scores(k_ref, q_head, table, h, base, width, ext, ok):
    s = dot(k_ref[:ext, :], q_head, NT)
    bias = jnp.concatenate(
        [table[h, :, pl.ds(base - 128 * g + 512, width)] for g in range(ext // 128)], axis=0
    )
    s = s + bias
    tail = jnp.where(ok, s[base:], MASKED)
    return tail if base == 0 else jnp.concatenate([s[:base], tail], axis=0)


def softmax_cols(s):
    m = jnp.max(s, axis=0, keepdims=True)
    p = jnp.exp(s - m)
    total = jnp.sum(p, axis=0, keepdims=True)
    return (p.astype(bf16), total, m)


def tasks_of(width, group):
    tasks = [(qb, h) for qb in range(L // width) for h in range(2)]
    return [tasks[i : i + group] for i in range(0, len(tasks), group)]


def self_forward_body(piece_ref, q_ref, k_ref, v_ref, t8_ref, o_ref, lse_ref, table):
    width = 256
    vt = transposed(v_ref[...])
    spread_bias(t8_ref, table)
    oks = [
        allowed_rows(piece_ref, qb * width, extent(qb, width) - qb * width, width)
        for qb in range(L // width)
    ]
    outs = {}
    for group in tasks_of(width, 8):
        scored = [
            biased_scores(
                k_ref,
                head_of(q_ref[pl.ds(qb * width, width), :], h),
                table,
                h,
                qb * width,
                width,
                extent(qb, width),
                oks[qb],
            )
            for qb, h in group
        ]
        weights = [softmax_cols(s) for s in scored]
        for (qb, h), (p, total, m) in zip(group, weights):
            mixed = dot(vt[64 * h : 64 * h + 64, : extent(qb, width)], p, NN)
            outs[(qb, h)] = mixed * (1.0 / total)
            lse_ref[0, h : h + 1, pl.ds(qb * width, width)] = m + jnp.log(total)
            if h == 1:
                o_ref[pl.ds(qb * width, width), :] = (
                    jnp.concatenate([outs[(qb, 0)], outs[(qb, 1)]], axis=0).T.astype(bf16)
                )


def head_deltas(a_ref, da_ref):
    prod = (a_ref[...].astype(f32) * da_ref[...].astype(f32)).T
    return [jnp.sum(prod[64 * h : 64 * h + 64], axis=0, keepdims=True) for h in range(2)]


def self_backward_body(
    piece_ref,
    q_ref,
    k_ref,
    v_ref,
    t8_ref,
    a_ref,
    da_ref,
    lse_ref,
    dq_ref,
    dk_ref,
    dv_ref,
    diag_ref,
    table,
    spans,
    dk_sum,
    dv_sum,
):
    width = 256
    delta = head_deltas(a_ref, da_ref)
    kt = transposed(k_ref[...])
    spread_bias(t8_ref, table)
    spans[...] = jnp.zeros_like(spans)
    dk_sum[...] = jnp.zeros_like(dk_sum)
    dv_sum[...] = jnp.zeros_like(dv_sum)
    for group in tasks_of(width, 2):
        qb = group[0][0]
        base = qb * width
        ext = extent(qb, width)
        ok = allowed_rows(piece_ref, base, ext - base, width)
        q = q_ref[pl.ds(base, width), :]
        da = da_ref[pl.ds(base, width), :]
        scored = [
            biased_scores(k_ref, head_of(q, h), table, h, base, width, ext, ok) for _, h in group
        ]
        dprobs = [dot(v_ref[:ext, :], head_of(da, h), NT) for _, h in group]
        low = []
        for h in range(2):
            p = jnp.exp(scored[h] - lse_ref[0, h : h + 1, pl.ds(base, width)])
            ds = p * (dprobs[h] - delta[h][:, base : base + width])
            for g in range(ext // 128):
                spans[h, :, pl.ds(base - 128 * g + 512, width)] += ds[128 * g : 128 * g + 128]
            low.append((p.astype(bf16), ds.astype(bf16)))
        dks = [dot(ds, q, NN) for _, ds in low]
        dvs = [dot(p, da, NN) for p, _ in low]
        dqs = [dot(kt[64 * h : 64 * h + 64, :ext], low[h][1], NN) for h in range(2)]
        lane = lax.broadcasted_iota(jnp.int32, (ext, 128), 1)
        dk_sum[:ext] += jnp.where(lane < 64, dks[0], dks[1])
        dv_sum[:ext] += jnp.where(lane < 64, dvs[0], dvs[1])
        dq_ref[pl.ds(base, width), :] = jnp.concatenate(dqs, axis=0).T.astype(bf16)
    dk_ref[...] = dk_sum[...].astype(bf16)
    dv_ref[...] = dv_sum[...].astype(bf16)
    for h in range(2):
        total = spans[h, 0:8, :]
        for m in range(1, 16):
            total = total + pltpu.roll(spans[h, 8 * m : 8 * m + 8, :], SPAN - 8 * m, 1)
        diag_ref[h] = total


def self_backward(qkv, t8, piece, mixed, dmixed, lse):
    return pl.pallas_call(
        self_backward_body,
        grid=(6,),
        in_specs=[
            pl.BlockSpec(memory_space=pltpu.SMEM),
            qkv_lanes(0),
            qkv_lanes(1),
            qkv_lanes(2),
            pl.BlockSpec((2, 8, SPAN), lambda h: (h, 0, 0)),
            lanes(0),
            lanes(0),
            pl.BlockSpec((1, 2, L), lambda h: (h, 0, 0)),
        ],
        out_specs=[
            lanes(0),
            lanes(0),
            lanes(0),
            pl.BlockSpec((2, 8, SPAN), lambda h: (h, 0, 0)),
        ],
        out_shape=[jax.ShapeDtypeStruct((L, D), bf16)] * 3
        + [jax.ShapeDtypeStruct((12, 8, SPAN), f32)],
        scratch_shapes=[
            pltpu.VMEM((2, 128, SPAN), f32),
            pltpu.VMEM((2, 128, SPAN), f32),
            pltpu.VMEM((L, 128), f32),
            pltpu.VMEM((L, 128), f32),
        ],
        compiler_params=pltpu.CompilerParams(vmem_limit_bytes=VMEM_LIMIT),
        name="self_backward",
    )(piece, qkv, qkv, qkv, t8, mixed, dmixed, lse)


def cross_forward_body(q_ref, k_ref, v_ref, o_ref, lse_ref):
    width = 256
    vt = transposed(v_ref[...])
    outs = {}
    for group in tasks_of(width, 8):
        scored = [
            dot(k_ref[...], head_of(q_ref[pl.ds(qb * width, width), :], h), NT) for qb, h in group
        ]
        weights = [softmax_cols(s) for s in scored]
        for (qb, h), (p, total, m) in zip(group, weights):
            outs[(qb, h)] = dot(vt[64 * h : 64 * h + 64, :], p, NN) * (1.0 / total)
            lse_ref[0, h : h + 1, pl.ds(qb * width, width)] = m + jnp.log(total)
            if h == 1:
                o_ref[pl.ds(qb * width, width), :] = (
                    jnp.concatenate([outs[(qb, 0)], outs[(qb, 1)]], axis=0).T.astype(bf16)
                )


def cross_backward_body(q_ref, k_ref, v_ref, a_ref, da_ref, lse_ref, dq_ref, dk_ref, dv_ref):
    width = 256
    delta = head_deltas(a_ref, da_ref)
    kt = transposed(k_ref[...])
    lane = lax.broadcasted_iota(jnp.int32, (LE, 128), 1)
    outs = {}
    dks = [None, None]
    dvs = [None, None]
    for group in tasks_of(width, 4):
        scored = [
            dot(k_ref[...], head_of(q_ref[pl.ds(qb * width, width), :], h), NT) for qb, h in group
        ]
        dprobs = [
            dot(v_ref[...], head_of(da_ref[pl.ds(qb * width, width), :], h), NT) for qb, h in group
        ]
        low = []
        for (qb, h), s, dp in zip(group, scored, dprobs):
            p = jnp.exp(s - lse_ref[0, h : h + 1, pl.ds(qb * width, width)])
            ds = p * (dp - delta[h][:, qb * width : (qb + 1) * width])
            low.append((p.astype(bf16), ds.astype(bf16)))
        for (qb, h), (p, ds) in zip(group, low):
            dk = dot(ds, q_ref[pl.ds(qb * width, width), :], NN)
            dv = dot(p, da_ref[pl.ds(qb * width, width), :], NN)
            dks[h] = dk if dks[h] is None else dks[h] + dk
            dvs[h] = dv if dvs[h] is None else dvs[h] + dv
            outs[(qb, h)] = dot(kt[64 * h : 64 * h + 64, :], ds, NN)
            if h == 1:
                dq_ref[pl.ds(qb * width, width), :] = (
                    jnp.concatenate([outs[(qb, 0)], outs[(qb, 1)]], axis=0).T.astype(bf16)
                )
    dk_ref[...] = jnp.where(lane < 64, dks[0], dks[1]).astype(bf16)
    dv_ref[...] = jnp.where(lane < 64, dvs[0], dvs[1]).astype(bf16)


def cross_backward(queries, key_values, mixed, dmixed, lse):
    return pl.pallas_call(
        cross_backward_body,
        grid=(6,),
        in_specs=[
            lanes(0),
            kv_lanes(0),
            kv_lanes(1),
            lanes(0),
            lanes(0),
            pl.BlockSpec((1, 2, L), lambda h: (h, 0, 0)),
        ],
        out_specs=[lanes(0), lanes(0, LE), lanes(0, LE)],
        out_shape=[jax.ShapeDtypeStruct((L, D), bf16)] + [jax.ShapeDtypeStruct((LE, D), bf16)] * 2,
        compiler_params=pltpu.CompilerParams(vmem_limit_bytes=VMEM_LIMIT),
        name="cross_backward",
    )(queries, key_values, key_values, mixed, dmixed, lse)


def place():
    dp = lax.axis_index("dp")
    return (dp, dp % QUAD, lax.axis_index("row"), lax.axis_index("col"))


def quad_mate(dp, quarter, flip):
    return dp - quarter + (quarter ^ flip)


def greet_all(dp, quarter, row, col):
    barrier = pltpu.get_barrier_semaphore()
    for s in range(1, ROWS):
        pl.semaphore_signal(
            barrier, inc=1, device_id=(dp, (row + s) % ROWS, col), device_id_type=MESH
        )
    for k in range(1, QUAD):
        pl.semaphore_signal(
            barrier, inc=1, device_id=(quad_mate(dp, quarter, k), row, col), device_id_type=MESH
        )
    pl.semaphore_signal(barrier, inc=1, device_id=(dp, row, 1 - col), device_id_type=MESH)
    pl.semaphore_wait(barrier, ROWS + QUAD - 1)


class Gathering:
    AHEAD = 3

    def __init__(self, blocks, wholes, apart, joined, gain_pair, rel_pair, own_blocks, sems):
        self.blocks, self.wholes, self.own_blocks = blocks, wholes, own_blocks
        self.dp, self.quarter, self.row, self.col = place()
        self.partner = (self.dp, self.row, 1 - self.col)
        (
            self.z_send,
            self.z_recv,
            self.q_send,
            self.q_recv,
            self.c_send,
            self.c_recv,
            local_sem,
            s_send,
            s_recv,
        ) = sems
        self.started = []
        count, swaps = len(blocks), len(apart)
        row, col, quarter = self.row, self.col, self.quarter
        greet_all(self.dp, quarter, row, col)
        self.own = {}
        self.from_partner = {}

        def keep(src, dst, slot):
            local = pltpu.make_async_copy(src, dst, local_sem.at[slot])
            local.start()
            self.own[slot] = local

        def half(ref):
            return ref.at[col]

        def rel_at(r):
            return rel_pair[1].at[
                pl.ds(pl.multiple_of(r * 8, 8), 8), pl.ds(pl.multiple_of(col * 128, 128), 128)
            ]

        self.rel_at = rel_at
        self.swap = []
        for j in range(swaps):
            self.swap.append(
                self.remote(
                    apart[j].at[1 - col], half(joined[j]), s_send.at[j], s_recv.at[j], self.partner
                )
            )
            keep(apart[j].at[col], half(joined[j]), count + j)
        self.swap.append(
            self.remote(
                gain_pair[0], half(gain_pair[1]), s_send.at[swaps], s_recv.at[swaps], self.partner
            )
        )
        keep(gain_pair[0], half(gain_pair[1]), count + swaps)
        keep(rel_pair[0], rel_at(row), count + swaps + 1)
        self.rel_sems = (s_send, s_recv, swaps + 1)
        self.rel_copies = [
            self.remote(
                rel_pair[0],
                rel_at(row),
                s_send.at[swaps + 1 + s],
                s_recv.at[swaps + 1 + s],
                self.partner if s == 0 else (self.dp, (row + s) % ROWS, col),
            )
            for s in range(ROWS)
        ]
        self.z_copies = {}
        self.q_copies = {}
        self.local_sem = local_sem
        for i in range(self.AHEAD):
            self.offer(i)
        for i in range(count):
            keep(blocks[i], own_blocks[i], i)

    def offer(self, i):
        row, col = self.row, self.col
        whole_block = self.wholes[i].at[col, pl.ds(pl.multiple_of(row * BLOCK, BLOCK), BLOCK)]
        for s in range(1, ROWS):
            self.z_copies[(i, s)] = self.remote(
                self.blocks[i].at[pl.ds(pl.multiple_of(self.quarter * PIECE, PIECE), PIECE), :],
                self.part(i, row, self.quarter),
                self.z_send.at[i, s - 1],
                self.z_recv.at[i, s - 1],
                (self.dp, (row + s) % ROWS, col),
            )
        self.from_partner[(i, 0, 0)] = self.remote(
            self.blocks[i],
            whole_block,
            self.c_send.at[i, 0, 0],
            self.c_recv.at[i, 0, 0],
            self.partner,
        )

    def remote(self, src, dst, send_sem, recv_sem, device):
        copy = pltpu.make_async_remote_copy(
            src_ref=src,
            dst_ref=dst,
            send_sem=send_sem,
            recv_sem=recv_sem,
            device_id=device,
            device_id_type=MESH,
        )
        copy.start()
        self.started.append(copy)
        return copy

    def part(self, i, r, q):
        at = pl.multiple_of(r * BLOCK + q * PIECE, PIECE)
        return self.wholes[i].at[self.col, pl.ds(at, PIECE)]

    def rel_onward(self):
        s_send, s_recv, base = self.rel_sems
        for s in range(1, ROWS):
            self.rel_copies[s].wait_recv()
            ref = self.rel_at((self.row - s + ROWS) % ROWS)
            slot = base + ROWS - 1 + s
            self.rel_copies.append(
                self.remote(ref, ref, s_send.at[slot], s_recv.at[slot], self.partner)
            )

    def rel_arrived(self, slot):
        self.own[slot].wait()
        self.rel_copies[0].wait_recv()
        for copy in self.rel_copies[ROWS:]:
            copy.wait_recv()

    def hand_over(self, i, s, k, r):
        ref = self.part(i, r, self.quarter ^ k)
        self.from_partner[(i, s, k)] = self.remote(
            ref, ref, self.c_send.at[i, s, k], self.c_recv.at[i, s, k], self.partner
        )

    def to_mate(self, i, s, k, slot, ref):
        self.q_copies[(i, s, slot)] = self.remote(
            ref,
            ref,
            self.q_send.at[i, s - 1, slot - 1],
            self.q_recv.at[i, s - 1, slot - 1],
            (quad_mate(self.dp, self.quarter, k), self.row, self.col),
        )

    def spread(self, i):
        for s in range(1, ROWS):
            self.z_copies[(i, s)].wait_recv()
            r = (self.row - s + ROWS) % ROWS
            ref = self.part(i, r, self.quarter)
            for k in (1, 2):
                self.to_mate(i, s, k, k, ref)
            self.hand_over(i, s, 0, r)
        if i + self.AHEAD < len(self.blocks):
            self.offer(i + self.AHEAD)
        self.own[i].wait()
        self.own[i] = pltpu.make_async_copy(
            self.own_blocks[i],
            self.wholes[i].at[self.col, pl.ds(pl.multiple_of(self.row * BLOCK, BLOCK), BLOCK)],
            self.local_sem.at[i],
        )
        self.own[i].start()

    def share(self, i):
        for s in range(1, ROWS):
            r = (self.row - s + ROWS) % ROWS
            onward = 1 + (i + s) % 2
            for k in (onward, 3 - onward):
                self.q_copies[(i, s, k)].wait_recv()
                if k == onward:
                    self.to_mate(i, s, 3 - k, 3, self.part(i, r, self.quarter ^ k))
                self.hand_over(i, s, k, r)

    def close(self, i):
        for s in range(1, ROWS):
            self.q_copies[(i, s, 3)].wait_recv()
            self.hand_over(i, s, 3, (self.row - s + ROWS) % ROWS)

    def arrived(self, i):
        self.own[i].wait()
        for s in range(ROWS):
            for k in range(QUAD if s else 1):
                self.from_partner[(i, s, k)].wait_recv()

    def finish(self):
        for copy in self.started:
            copy.wait_send()


def forward_body(count, swaps, *refs):
    blocks = refs[:count]
    apart = refs[count : count + swaps]
    gain_in, rel_in, onehot_ref, piece_ref = refs[count + swaps : count + swaps + 4]
    refs = refs[count + swaps + 4 :]
    wholes = refs[:count]
    outs = refs[count : count + 9 + swaps + 1]
    refs = refs[count + 9 + swaps + 1 :]
    h2, rel_all, gains, rows_in, enc, cot, w_qkv, w_out, w_cq, w_ckv, w_co = refs[:11]
    qkv, a1, h1, q2, kv2, a2, t8, lse1, lse2, table, load_sem, save_sem = refs[11:23]
    own_blocks = refs[23 : 23 + count]
    joined = (rows_in, enc, cot)
    comm = Gathering(
        blocks,
        wholes,
        apart,
        joined,
        (gain_in, gains),
        (rel_in, rel_all),
        own_blocks,
        refs[23 + count :],
    )
    saving = []

    class Loads(list):
        def wait(self):
            for copy in self:
                copy.wait()

    def load(src, dst, slot):
        wide = src.shape[2]
        copies = Loads()
        for c in range(2):
            copies.append(
                pltpu.make_async_copy(
                    src.at[c], dst.at[:, c * wide : (c + 1) * wide], load_sem.at[slot, c]
                )
            )
            copies[-1].start()
        return copies

    def save(slot, src):
        copy = pltpu.make_async_copy(src, outs[slot], save_sem.at[slot])
        copy.start()
        saving.append(copy)

    def weight(i, dst):
        comm.arrived(i)
        return load(wholes[i], dst, 3 + i)

    def swapped(j, slot, ref):
        comm.swap[j].wait_recv()
        comm.own[count + j].wait()
        save(slot, ref)

    comm.rel_onward()
    comm.spread(0)
    comm.spread(1)
    swapped(0, 9, rows_in)
    swapped(swaps, 9 + swaps, gains)
    g_self = jnp.concatenate([gains[0, 0:1, :], gains[1, 0:1, :]], axis=1)
    g_cross = jnp.concatenate([gains[0, 1:2, :], gains[1, 1:2, :]], axis=1)
    comm.share(0)
    comm.spread(2)
    step = 256
    blocks_of = [slice(step * b, step * (b + 1)) for b in range(L // step)]
    comm.rel_arrived(count + swaps + 1)
    rel16 = jnp.concatenate([rel_all[:, :6], rel_all[:, 128:134]], axis=1).astype(bf16)
    bias = dot(rel16, onehot_ref[...], TN)
    for n in range(8):
        moved = pltpu.roll(bias, n, 1) if n else bias
        for h in range(12):
            t8[h, n : n + 1, :] = moved[h : h + 1]
    save(0, t8)
    comm.share(1)
    comm.close(0)
    loading = weight(0, w_qkv)
    comm.share(2)
    loading.wait()
    for n, at in enumerate(blocks_of):
        xb = jnp.concatenate([rows_in[0, at, :], rows_in[1, at, :]], axis=1).astype(f32)
        n1 = (xb * rms_of(xb) * g_self).astype(bf16)
        qkv[at, :] = dot(n1, w_qkv[...], NN).astype(bf16)
        if n == 0:
            comm.close(1)
        if n == 1:
            comm.spread(3)
        if n == 2:
            comm.close(2)
        if n == 3:
            comm.share(3)
    save(1, qkv)

    def lane(block):
        return pl.ds(pl.multiple_of(block * 128, 128), 128)

    def self_heads(hp, carry):
        base = (hp // 3) * 9 + hp % 3
        self_forward_body(
            piece_ref,
            qkv.at[:, lane(base)],
            qkv.at[:, lane(base + 3)],
            qkv.at[:, lane(base + 6)],
            t8.at[pl.ds(2 * hp, 2)],
            a1.at[:, lane(hp)],
            lse1.at[pl.ds(hp, 1)],
            table,
        )
        return carry

    lax.fori_loop(0, 2, self_heads, 0)
    comm.spread(4)
    comm.close(3)
    loadings = [weight(1, w_out), weight(2, w_cq)]
    swapped(1, 10, enc)
    swapped(2, 11, cot)
    lax.fori_loop(2, 4, self_heads, 0)
    comm.share(4)
    loadings.append(weight(3, w_ckv))
    lax.fori_loop(4, 6, self_heads, 0)
    save(2, a1)
    save(3, lse1)
    comm.close(4)
    comm.spread(5)
    for copy in loadings:
        copy.wait()
    loading = weight(4, w_co)
    kv2[...] = dot(jnp.concatenate([enc[0], enc[1]], axis=1), w_ckv[...], NN).astype(bf16)
    save(6, kv2)
    for n, at in enumerate(blocks_of):
        xb = jnp.concatenate([rows_in[0, at, :], rows_in[1, at, :]], axis=1).astype(f32)
        h1b = xb + dot(a1[at, :], w_out[...], NT)
        h1[at, :] = h1b
        n2 = (h1b * rms_of(h1b) * g_cross).astype(bf16)
        q2[at, :] = dot(n2, w_cq[...], NN).astype(bf16)
    save(4, h1)
    save(5, q2)

    def cross_heads(hp, carry):
        base = (hp // 3) * 6 + hp % 3
        cross_forward_body(
            q2.at[:, lane(hp)],
            kv2.at[:, lane(base)],
            kv2.at[:, lane(base + 3)],
            a2.at[:, lane(hp)],
            lse2.at[pl.ds(hp, 1)],
        )
        return carry

    lax.fori_loop(0, 2, cross_heads, 0)
    comm.spread(6)
    comm.share(5)
    lax.fori_loop(2, 6, cross_heads, 0)
    save(7, a2)
    save(8, lse2)
    comm.close(5)
    loading.wait()
    for at in blocks_of:
        h2[at, :] = h1[at, :] + dot(a2[at, :], w_co[...], NT)
    comm.share(6)
    comm.close(6)
    comm.arrived(5)
    comm.arrived(6)
    for copy in saving:
        copy.wait()
    comm.finish()


def forward(blocks, apart, gains, rel, onehot, piece, number):
    count = len(blocks)
    swaps = len(apart)
    shape = jax.ShapeDtypeStruct
    saved = [
        shape((12, 8, SPAN), f32),
        shape((L, 3 * D), bf16),
        shape((L, D), bf16),
        shape((6, 2, L), f32),
        shape((L, D), f32),
        shape((L, D), bf16),
        shape((LE, 2 * D), bf16),
        shape((L, D), bf16),
        shape((6, 2, L), f32),
    ]
    saved += [shape(x.shape, x.dtype) for x in apart] + [shape((2, 8, HALF), f32)]
    wholes = [shape((2, D, b.shape[1]), b.dtype) for b in blocks]
    dma = pltpu.SemaphoreType.DMA
    any_spec = pl.BlockSpec(memory_space=pl.ANY)
    vmem = pl.BlockSpec(memory_space=pltpu.VMEM)
    scratch = [
        pltpu.VMEM((BUCKETS, 256), f32),
        pltpu.VMEM((2, 8, HALF), f32),
        pltpu.VMEM((2, L, HALF), bf16),
        pltpu.VMEM((2, LE, HALF), bf16),
        pltpu.VMEM((2, L, HALF), bf16),
        pltpu.VMEM((D, 3 * D), bf16),
        pltpu.VMEM((D, D), bf16),
        pltpu.VMEM((D, D), bf16),
        pltpu.VMEM((D, 2 * D), bf16),
        pltpu.VMEM((D, D), bf16),
        pltpu.VMEM((L, 3 * D), bf16),
        pltpu.VMEM((L, D), bf16),
        pltpu.VMEM((L, D), f32),
        pltpu.VMEM((L, D), bf16),
        pltpu.VMEM((LE, 2 * D), bf16),
        pltpu.VMEM((L, D), bf16),
        pltpu.VMEM((12, 8, SPAN), f32),
        pltpu.VMEM((6, 2, L), f32),
        pltpu.VMEM((6, 2, L), f32),
        pltpu.VMEM((2, 128, SPAN), f32),
        dma((8, 2)),
        dma((9 + swaps + 1,)),
    ]
    scratch += [pltpu.VMEM(b.shape, b.dtype) for b in blocks]
    scratch += [
        dma((count, ROWS - 1)),
        dma((count, ROWS - 1)),
        dma((count, ROWS - 1, QUAD - 1)),
        dma((count, ROWS - 1, QUAD - 1)),
        dma((count, ROWS, QUAD)),
        dma((count, ROWS, QUAD)),
        dma((count + swaps + 2,)),
        dma((swaps + 8,)),
        dma((swaps + 8,)),
    ]
    out = pl.pallas_call(
        lambda *refs: forward_body(count, swaps, *refs),
        out_shape=wholes + saved + [shape((L, D), f32)],
        in_specs=[any_spec] * (count + swaps + 2)
        + [vmem, pl.BlockSpec(memory_space=pltpu.SMEM)],
        out_specs=[any_spec] * (len(wholes) + len(saved)) + [vmem],
        scratch_shapes=scratch,
        compiler_params=pltpu.CompilerParams(
            collective_id=number, has_side_effects=True, vmem_limit_bytes=VMEM_LIMIT
        ),
        name="forward",
    )(*blocks, *apart, gains, rel, onehot, piece)
    return (out[:count], out[count + 9 : -1], out[count : count + 9] + out[-1:])


def swap_back(y, col):
    own = lax.dynamic_slice_in_dim(y, col * HALF, HALF, 1)
    other = lax.dynamic_slice_in_dim(y, (1 - col) * HALF, HALF, 1)
    came = lax.ppermute(other, "col", [(0, 1), (1, 0)])
    return jnp.where(col == 0, jnp.stack([own, came]), jnp.stack([came, own]))


def rms_of(v):
    return lax.rsqrt(jnp.sum(v * v, axis=-1, keepdims=True) * (1.0 / D) + EPSILON)


def norm_back_rows(v, r, gain, dn):
    inner = jnp.sum(dn * gain * v, axis=-1, keepdims=True)
    dv = dn * gain * r - v * (r * r * r) * (inner * (1.0 / D))
    return (dv, jnp.sum(dn * v * r, axis=0, keepdims=True))


def ffn_body(
    h2_ref,
    cot_ref,
    gain_ref,
    wgu_ref,
    wd_ref,
    out_ref,
    dh2_ref,
    ggu_ref,
    gd_ref,
    dgain_ref,
    n3t,
    mid_all,
    e3t,
    dgu_all,
):
    step = pl.program_id(0)
    rows = h2_ref.shape[0]
    here = pl.ds(pl.multiple_of(step * rows, rows), rows)
    g_ffn = jnp.concatenate([gain_ref[0, 2:3, :], gain_ref[1, 2:3, :]], axis=1)
    g_final = jnp.concatenate([gain_ref[0, 3:4, :], gain_ref[1, 3:4, :]], axis=1)
    h2 = h2_ref[...]
    r3 = rms_of(h2)
    n3 = (h2 * r3 * g_ffn).astype(bf16)
    n3t[:, here] = transposed(n3)
    kept = []
    for c in range(4):
        at = (c % 2) * 512
        gate = dot(n3, wgu_ref[c // 2, :, at : at + 512], NN)
        up = dot(n3, wgu_ref[c // 2, :, at + 1024 : at + 1536], NN)
        act, slope = gelu_parts(gate)
        mid = (act * up).astype(bf16)
        mid_all[here, 512 * c : 512 * (c + 1)] = mid
        kept.append((act, up * slope))
    h3 = h2 + dot(mid_all[here, :1024], wd_ref[0], NT) + dot(mid_all[here, 1024:], wd_ref[1], NT)
    r4 = rms_of(h3)
    out_ref[...] = (h3 * r4 * g_final).astype(bf16)
    dh3, dg_final = norm_back_rows(h3, r4, g_final, jnp.concatenate([cot_ref[0], cot_ref[1]], axis=1).astype(f32))
    e3 = dh3.astype(bf16)
    e3t[:, here] = transposed(e3)
    for c in range(4):
        at = (c // 2) * 2048 + (c % 2) * 512
        act, slope = kept[c]
        low = 512 * (c % 2)
        dmid = dot(e3, wd_ref[c // 2, :, low : low + 512], NN).astype(bf16).astype(f32)
        dgu_all[here, at : at + 512] = (dmid * slope).astype(bf16)
        dgu_all[here, at + 1024 : at + 1536] = (dmid * act).astype(bf16)
    dn3 = dot(dgu_all[here, :2048], wgu_ref[0], NT) + dot(dgu_all[here, 2048:], wgu_ref[1], NT)
    back, dg_ffn = norm_back_rows(h2, r3, g_ffn, dn3)
    dh2_ref[...] = dh3 + back

    @pl.when(step == 0)
    def _():
        dgain_ref[...] = jnp.zeros_like(dgain_ref)

    dgain_ref[2:3, :] += dg_ffn
    dgain_ref[3:4, :] += dg_final

    @pl.when(step == pl.num_programs(0) - 1)
    def _():
        for c in range(8):
            span = slice(512 * c, 512 * (c + 1))
            low = slice(512 * (c % 4), 512 * (c % 4 + 1))
            ggu_ref[c // 4, :, low] = dot(n3t[...], dgu_all[:, span], NN).astype(bf16)
        for c in range(4):
            span = slice(512 * c, 512 * (c + 1))
            low = slice(512 * (c % 2), 512 * (c % 2 + 1))
            gd_ref[c // 2, :, low] = dot(e3t[...], mid_all[:, span], NN).astype(bf16)


def feed_forward(h2, cot, gains, wgu, wd):
    rows = 256
    def whole(*shape):
        return pl.BlockSpec(shape, lambda i: (0,) * len(shape), pipeline_mode=pl.Buffered(1))

    block = pl.BlockSpec((rows, D), lambda i: (i, 0))
    return pl.pallas_call(
        ffn_body,
        grid=(L // rows,),
        in_specs=[
            block,
            pl.BlockSpec((2, rows, HALF), lambda i: (0, i, 0)),
            whole(2, 8, HALF),
            whole(2, D, 2048),
            whole(2, D, 1024),
        ],
        out_specs=[block, block, whole(2, D, 2048), whole(2, D, 1024), whole(8, D)],
        out_shape=[
            jax.ShapeDtypeStruct((L, D), bf16),
            jax.ShapeDtypeStruct((L, D), f32),
            jax.ShapeDtypeStruct((2, D, 2048), bf16),
            jax.ShapeDtypeStruct((2, D, 1024), bf16),
            jax.ShapeDtypeStruct((8, D), f32),
        ],
        scratch_shapes=[
            pltpu.VMEM((D, L), bf16),
            pltpu.VMEM((L, 2048), bf16),
            pltpu.VMEM((D, L), bf16),
            pltpu.VMEM((L, 4096), bf16),
        ],
        compiler_params=pltpu.CompilerParams(vmem_limit_bytes=VMEM_LIMIT),
        name="feed_forward",
    )(h2, cot, gains, wgu, wd)


def reduce_body(arrays, chunks, *refs):
    grads = refs[:arrays]
    small_in = refs[arrays]
    outs = refs[arrays + 1 : 2 * arrays + 1]
    small_out = refs[2 * arrays + 1]
    scratch = refs[2 * arrays + 2 :]
    count = len(chunks)
    pair = scratch[:count]
    first = scratch[count : 2 * count]
    second = scratch[2 * count : 3 * count]
    third = scratch[3 * count : 4 * count]
    fourth = scratch[4 * count : 5 * count]
    small_buf, sends, recvs, small_send, small_recv = scratch[5 * count :]
    dp, quarter, row, col = place()
    greet_all(dp, quarter, row, col)
    begun = []
    pending = {}

    def send(i, slot, src, dst, device):
        copy = pltpu.make_async_remote_copy(
            src_ref=src,
            dst_ref=dst,
            send_sem=sends.at[i, slot],
            recv_sem=recvs.at[i, slot],
            device_id=device,
            device_id_type=MESH,
        )
        copy.start()
        begun.append(copy)
        pending[(i, slot)] = copy

    def mate(k):
        return (quad_mate(dp, quarter, k), row, col)

    def half(i, c):
        a, offset, wide = chunks[i]
        return (c, slice(None), slice(None), slice(None), pl.ds(offset, wide))

    def stage0(i):
        a = chunks[i][0]
        send(i, 0, grads[a].at[half(i, 1 - col)], pair[i], (dp, row, 1 - col))

    def stage1(i):
        pending[(i, 0)].wait_recv()
        for r in range(ROWS):
            a, offset, wide = chunks[i]
            pair[i][r] = pair[i][r] + grads[a][col, r, :, :, pl.ds(offset, wide)]
            if r % 2 == 1:
                k = 1 if r == 1 else 2
                for j, q in enumerate((quarter ^ k, quarter ^ 3)):
                    send(
                        i,
                        1 + r - 1 + j,
                        pair[i].at[pl.ds(r - 1, 2), q],
                        first[i].at[pl.ds(r - 1, 2), j],
                        mate(k),
                    )

    def stage2(i):
        for h in range(2):
            k = 1 if h == 0 else 2
            pending[(i, 1 + 2 * h)].wait_recv()
            pending[(i, 2 + 2 * h)].wait_recv()
            for r in (2 * h, 2 * h + 1):
                first[i][r, 1] = first[i][r, 1] + pair[i][r, quarter ^ 3 ^ k]
            send(
                i,
                5 + h,
                first[i].at[pl.ds(2 * h, 2), 1],
                second[i].at[pl.ds(2 * h, 2)],
                mate(3 ^ k),
            )
            for r in (2 * h, 2 * h + 1):
                first[i][r, 0] = first[i][r, 0] + pair[i][r, quarter]

    def stage3(i):
        for h in range(2):
            pending[(i, 5 + h)].wait_recv()
            for r in (2 * h, 2 * h + 1):
                second[i][r] = second[i][r] + first[i][r, 0]
        for s in range(1, ROWS):
            send(
                i,
                6 + s,
                second[i].at[(row + s) % ROWS],
                third[i].at[s - 1],
                (dp, (row + s) % ROWS, col),
            )

    def stage4(i):
        for s in range(1, ROWS):
            pending[(i, 6 + s)].wait_recv()
        total = second[i][row].astype(f32)
        for s in range(1, ROWS):
            total = total + third[i][s - 1].astype(f32)
        fourth[i][quarter] = total.astype(bf16)
        for k in range(1, QUAD):
            send(i, 9 + k, fourth[i].at[quarter], fourth[i].at[quarter], mate(k))

    def stage5(i):
        for k in range(1, QUAD):
            pending[(i, 9 + k)].wait_recv()
        a, offset, wide = chunks[i]
        outs[a][:, :, offset : offset + wide] = fourth[i][...].astype(f32)

    def small_send_to(slot, src, dst, device):
        copy = pltpu.make_async_remote_copy(
            src_ref=small_buf.at[src],
            dst_ref=small_buf.at[dst],
            send_sem=small_send.at[slot],
            recv_sem=small_recv.at[slot],
            device_id=device,
            device_id_type=MESH,
        )
        copy.start()
        begun.append(copy)
        pending[("small", slot)] = copy

    small_buf[0] = small_in[...]
    small_send_to(0, 0, 1, (dp, row, 1 - col))
    stages = (stage0, stage1, stage2, stage3, stage4, stage5)
    for i in range(count):
        stage0(i)
    for t in range(count + 4):
        for n in range(1, 6):
            i = t - n + 1
            if 0 <= i < count:
                stages[n](i)
        if t == 0:
            pending[("small", 0)].wait_recv()
            small_buf[2] = small_buf[0] + small_buf[1]
            small_send_to(1, 2, 3, mate(1))
        if t == 1:
            pending[("small", 1)].wait_recv()
            small_buf[4] = small_buf[2] + small_buf[3]
            small_send_to(2, 4, 5, mate(2))
        if t == 2:
            pending[("small", 2)].wait_recv()
            small_buf[6 + row] = small_buf[4] + small_buf[5]
            for s in range(1, ROWS):
                small_send_to(2 + s, 6 + row, 6 + row, (dp, (row + s) % ROWS, col))
        if t == 3:
            for s in range(1, ROWS):
                pending[("small", 2 + s)].wait_recv()
            small_out[...] = (small_buf[6] + small_buf[7]) + (small_buf[8] + small_buf[9])
    for copy in begun:
        copy.wait_send()


def reduce_gradients(grads, small, number):
    arrays = len(grads)
    halves = [g.shape[2] for g in grads]
    chunks = []
    for a, w in enumerate(halves):
        pieces = 2 if w > 1100 else 1
        chunks += [(a, p * (w // pieces) // 128 * 128, 0) for p in range(pieces)]
    chunks = tuple(
        (a, o, (chunks[n + 1][1] if n + 1 < len(chunks) and chunks[n + 1][0] == a else halves[a]) - o)
        for n, (a, o, _) in enumerate(chunks)
    )
    count = len(chunks)
    widths = [w for _, _, w in chunks]
    dma = pltpu.SemaphoreType.DMA
    vmem = pl.BlockSpec(memory_space=pltpu.VMEM)
    out = pl.pallas_call(
        lambda *refs: reduce_body(arrays, chunks, *refs),
        out_shape=[jax.ShapeDtypeStruct((QUAD, PIECE, w), f32) for w in halves]
        + [jax.ShapeDtypeStruct(small.shape, f32)],
        in_specs=[vmem] * (arrays + 1),
        out_specs=[vmem] * (arrays + 1),
        scratch_shapes=[pltpu.VMEM((ROWS, QUAD, PIECE, w), bf16) for w in widths]
        + [pltpu.VMEM((ROWS, 2, PIECE, w), bf16) for w in widths]
        + [pltpu.VMEM((ROWS, PIECE, w), bf16) for w in widths]
        + [pltpu.VMEM((ROWS - 1, PIECE, w), bf16) for w in widths]
        + [pltpu.VMEM((QUAD, PIECE, w), bf16) for w in widths]
        + [
            pltpu.VMEM((6 + ROWS,) + small.shape, f32),
            dma((count, 13)),
            dma((count, 13)),
            dma((6,)),
            dma((6,)),
        ],
        compiler_params=pltpu.CompilerParams(
            collective_id=number, has_side_effects=True, vmem_limit_bytes=VMEM_LIMIT
        ),
        name="reduce_gradients",
    )(*[g.reshape(2, ROWS, QUAD, PIECE, g.shape[2]) for g in grads], small)
    return ([o.reshape(BLOCK, o.shape[2]) for o in out[:arrays]], out[arrays])


def inverse_rms(v):
    return lax.rsqrt(jnp.mean(v * v, axis=-1, keepdims=True) + EPSILON)


def norm_backward(v, r, gain, dn):
    inner = jnp.sum(dn * gain * v, axis=-1, keepdims=True)
    dv = dn * gain * r - v * (r * r * r) * (inner / D)
    return (dv, jnp.sum(dn * v * r, axis=0))


def gelu_parts(t):
    inner = ROOT_TWO_PI * (t + 0.044715 * t * t * t)
    th = jnp.tanh(inner)
    value = 0.5 * t * (1.0 + th)
    slope = 0.5 * (1.0 + th) + 0.5 * t * (1.0 - th * th) * ROOT_TWO_PI * (
        1.0 + 3.0 * 0.044715 * t * t
    )
    return (value, slope)


def body(
    quads,
    hidden_in,
    encoded,
    cotangent,
    piece_start,
    image_piece_lengths,
    bucket_table,
    self_query,
    self_key,
    self_value,
    self_out,
    rel_weight,
    cross_query,
    cross_key,
    cross_value,
    cross_out,
    ffn_gate,
    ffn_up,
    ffn_down,
    gain_self,
    gain_cross,
    gain_ffn,
    gain_final,
):
    col = lax.axis_index("col")
    row = lax.axis_index("row")
    blocks = (
        jnp.concatenate([self_query, self_key, self_value], axis=1),
        self_out.T,
        cross_query,
        jnp.concatenate([cross_key, cross_value], axis=1),
        cross_out.T,
        jnp.concatenate([ffn_gate, ffn_up], axis=1),
        ffn_down.T,
    )
    gain_block = jnp.stack([gain_self, gain_cross, gain_ffn, gain_final])
    gain_block = jnp.concatenate([gain_block, jnp.zeros_like(gain_block)])
    rel_block = jnp.pad(rel_weight.astype(f32), ((0, 0), (0, 122)))
    onehot = (
        bucket_table[None, :SPAN] == jnp.arange(BUCKETS, dtype=jnp.int32)[:, None]
    ).astype(f32)
    starts = lax.dynamic_index_in_dim(piece_start, col, 0, keepdims=False)
    lengths = lax.dynamic_index_in_dim(image_piece_lengths, col, 0, keepdims=False)
    piece = jnp.concatenate([starts, starts + lengths])
    wholes, (x, enc, cot, gains), saved = forward(
        blocks,
        (hidden_in, encoded, cotangent),
        gain_block,
        rel_block,
        onehot.astype(bf16)[:, ::-1],
        piece,
        0,
    )
    w_qkv, w_out_t, c_query, c_kv, c_out_t = [
        jnp.concatenate([w[0], w[1]], axis=1) for w in wholes[:5]
    ]
    f_gu, f_down_t = wholes[5:]
    t8, qkv, a1, lse1, h1, q2, kv2, a2, lse2, h2 = saved
    g_self, g_cross = jnp.concatenate([gains[0, :2], gains[1, :2]], axis=1)
    x = jnp.concatenate([x[0], x[1]], axis=1).astype(f32)
    enc = jnp.concatenate([enc[0], enc[1]], axis=1)
    r1 = inverse_rms(x)
    n1 = (x * r1 * g_self).astype(bf16)
    r2 = inverse_rms(h1)
    n2 = (h1 * r2 * g_cross).astype(bf16)
    output, dh2, gr_gu, gr_down, ffn_gains = feed_forward(h2, cot, gains, f_gu, f_down_t)
    e2 = dh2.astype(bf16)
    gr_co = dot(e2, a2, TN)
    da2 = dot(e2, c_out_t, NN).astype(bf16)
    dq2, dk2, dv2 = cross_backward(q2, kv2, a2, da2, lse2)
    gr_cq = dot(n2, dq2, TN)
    dkv2 = jnp.concatenate([dk2[:, :HALF], dv2[:, :HALF], dk2[:, HALF:], dv2[:, HALF:]], axis=1)
    gr_ckv = dot(enc, dkv2, TN)
    enc_grad = dot(dkv2, c_kv, NT)
    dn2 = dot(dq2, c_query, NT)
    back2, dg_cross = norm_backward(h1, r2, g_cross, dn2)
    dh1 = dh2 + back2
    e1 = dh1.astype(bf16)
    gr_out = dot(e1, a1, TN)
    da1 = dot(e1, w_out_t, NN).astype(bf16)
    dq1, dk1, dv1, diag = self_backward(qkv, t8, piece, a1, da1, lse1)
    dqkv = jnp.concatenate(
        [part[:, HALF * c : HALF * (c + 1)] for c in range(2) for part in (dq1, dk1, dv1)], axis=1
    )
    gr_qkv = dot(n1, dqkv, TN)
    dn1 = dot(dqkv, w_qkv, NT)
    back1, dg_self = norm_backward(x, r1, g_self, dn1)
    hidden_grad = dh1 + back1

    spans = sum(jnp.roll(diag[:, s], -s, axis=1) for s in range(8))[:, ::-1]
    gr_rel = jnp.dot(onehot, spans.T, precision=lax.Precision.HIGHEST)

    small = jnp.concatenate(
        [
            jnp.stack([dg_self, dg_cross]),
            ffn_gains[2:4],
            jnp.pad(gr_rel.reshape(1, BUCKETS * 12), ((0, 3), (0, D - BUCKETS * 12))),
        ]
    )
    grads = [gr_gu, gr_down, gr_co, gr_cq, gr_ckv, gr_out, gr_qkv]
    grads, small = reduce_gradients([
            g if g.ndim == 3 else jnp.moveaxis(g.astype(bf16).reshape(D, 2, -1), 1, 0)
            for g in grads
        ], small, 1)
    if quads > 1:
        grads, small = jax.tree.map(lambda t: lax.psum(t, "dp") * (1.0 / QUAD), (grads, small))
    gr_gu, gr_down, gr_co, gr_cq, gr_ckv, gr_out, gr_qkv = grads
    gr_down, gr_co, gr_out = gr_down.T, gr_co.T, gr_out.T
    gain_sums = lax.dynamic_slice_in_dim(small[:4], col * HALF, HALF, 1)
    gr_rel = small[4, : BUCKETS * 12].reshape(BUCKETS, 12)
    gr_rel = lax.dynamic_slice(gr_rel, (row * 8, col * 6), (8, 6))
    return (
        swap_back(output, col),
        swap_back(hidden_grad, col),
        swap_back(enc_grad, col),
        gr_qkv[:, :HALF],
        gr_qkv[:, HALF : 2 * HALF],
        gr_qkv[:, 2 * HALF :],
        gr_out,
        gr_rel,
        gr_cq,
        gr_ckv[:, :HALF],
        gr_ckv[:, HALF:],
        gr_co,
        gr_gu[:, :1024],
        gr_gu[:, 1024:],
        gr_down,
        gain_sums[0],
        gain_sums[1],
        gain_sums[2],
        gain_sums[3],
    )


def solution(mesh):
    batch = P(("dp", "row"), None, "col")
    inward = P("row", "col")
    outward = P("col", "row")
    gain = P("col")
    weights = (
        (inward,) * 3 + (outward, inward) + (inward,) * 3 + (outward,) + (inward,) * 2 + (outward,)
    )
    placed = (batch,) * 3 + (P(("dp", "row"), None),) * 2 + (P(),) + weights + (gain,) * 4
    return jax.shard_map(
        lambda *args: body(mesh.shape["dp"] // QUAD, *args),
        mesh=mesh,
        in_specs=placed,
        out_specs=(batch,) * 3 + weights + (gain,) * 4,
        check_vma=False,
    )
```

```python
import math

import jax
import jax.numpy as jnp
from jax import lax
from jax.experimental import pallas as pl
from jax.experimental.pallas import tpu as pltpu
from jax.sharding import PartitionSpec as P

D = 768
HALF = 384
L = 1024
LE = 256
BUCKETS = 32
SPAN = 1536
EPSILON = 1e-06
MASKED = -1e30
ROOT_TWO_PI = math.sqrt(2.0 / math.pi)
MESH = pl.DeviceIdType.MESH
ROWS = 4
QUAD = 4
BLOCK = D // ROWS
PIECE = BLOCK // QUAD
f32 = jnp.float32
bf16 = jnp.bfloat16
NT = (((1,), (1,)), ((), ()))
NN = (((1,), (0,)), ((), ()))
TN = (((0,), (0,)), ((), ()))
VMEM_LIMIT = 60 * 2**20


def dot(a, b, dims):
    return lax.dot_general(a, b, dims, preferred_element_type=f32)


def head_of(x, h):
    lane = lax.broadcasted_iota(jnp.int32, x.shape, 1)
    return jnp.where((lane >= 64 * h) & (lane < 64 * h + 64), x, jnp.zeros_like(x))


def transposed(x):
    return x.astype(f32).T.astype(bf16)


def spread_bias(t8_ref, table):
    for h in range(2):
        t = t8_ref[h]
        for m in range(16):
            table[h][8 * m : 8 * m + 8, :] = pltpu.roll(t, 8 * m, 1)


def allowed_rows(piece_ref, base, rows, width):
    s0 = piece_ref[0]
    s1 = piece_ref[1]
    e0 = piece_ref[2]
    e1 = piece_ref[3]
    c = lax.broadcasted_iota(jnp.int32, (1, width), 1) + base
    last = jnp.where(
        (c >= s0) & (c < e0), e0 - 1, jnp.where((c >= s1) & (c < e1), e1 - 1, 0)
    )
    last = jnp.maximum(c, last)
    return lax.broadcasted_iota(jnp.int32, (rows, width), 0) + base <= last


def extent(qb, width):
    return 512 * ((qb * width) // 512 + 1)


def biased_scores(k_ref, q_head, table, h, base, width, ext, ok):
    s = dot(k_ref[:ext, :], q_head, NT)
    bias = jnp.concatenate(
        [table[h][:, pl.ds(base - 128 * g + 512, width)] for g in range(ext // 128)], axis=0
    )
    s = s + bias
    tail = jnp.where(ok, s[base:], MASKED)
    return tail if base == 0 else jnp.concatenate([s[:base], tail], axis=0)


def softmax_cols(s):
    m = jnp.max(s, axis=0, keepdims=True)
    p = jnp.exp(s - m)
    total = jnp.sum(p, axis=0, keepdims=True)
    return (p.astype(bf16), total, m)


def tasks_of(width, group):
    tasks = [(qb, h) for qb in range(L // width) for h in range(2)]
    return [tasks[i : i + group] for i in range(0, len(tasks), group)]


def self_forward_body(piece_ref, q_ref, k_ref, v_ref, t8_ref, o_ref, lse_ref, table):
    width = 256
    vt = transposed(v_ref[...])
    spread_bias(t8_ref, table)
    oks = [
        allowed_rows(piece_ref, qb * width, extent(qb, width) - qb * width, width)
        for qb in range(L // width)
    ]
    outs = {}
    for group in tasks_of(width, 8):
        scored = [
            biased_scores(
                k_ref,
                head_of(q_ref[pl.ds(qb * width, width), :], h),
                table,
                h,
                qb * width,
                width,
                extent(qb, width),
                oks[qb],
            )
            for qb, h in group
        ]
        weights = [softmax_cols(s) for s in scored]
        for (qb, h), (p, total, m) in zip(group, weights):
            mixed = dot(vt[64 * h : 64 * h + 64, : extent(qb, width)], p, NN)
            outs[(qb, h)] = mixed * (1.0 / total)
            lse_ref[0, h : h + 1, pl.ds(qb * width, width)] = m + jnp.log(total)
            if h == 1:
                o_ref[pl.ds(qb * width, width), :] = (
                    jnp.concatenate([outs[(qb, 0)], outs[(qb, 1)]], axis=0).T.astype(bf16)
                )


def head_deltas(a_ref, da_ref):
    prod = (a_ref[...].astype(f32) * da_ref[...].astype(f32)).T
    return [jnp.sum(prod[64 * h : 64 * h + 64], axis=0, keepdims=True) for h in range(2)]


def self_backward_body(
    piece_ref,
    q_ref,
    k_ref,
    v_ref,
    t8_ref,
    a_ref,
    da_ref,
    lse_ref,
    dq_ref,
    dk_ref,
    dv_ref,
    diag_ref,
    table,
    spans,
    dk_sum,
    dv_sum,
):
    width = 256
    delta = head_deltas(a_ref, da_ref)
    kt = transposed(k_ref[...])
    spread_bias(t8_ref, table)
    for h in range(2):
        spans[h][...] = jnp.zeros(spans[h].shape, f32)
    dk_sum[...] = jnp.zeros_like(dk_sum)
    dv_sum[...] = jnp.zeros_like(dv_sum)
    for group in tasks_of(width, 2):
        qb = group[0][0]
        base = qb * width
        ext = extent(qb, width)
        ok = allowed_rows(piece_ref, base, ext - base, width)
        q = q_ref[pl.ds(base, width), :]
        da = da_ref[pl.ds(base, width), :]
        scored = [
            biased_scores(k_ref, head_of(q, h), table, h, base, width, ext, ok) for _, h in group
        ]
        dprobs = [dot(v_ref[:ext, :], head_of(da, h), NT) for _, h in group]
        low = []
        for h in range(2):
            p = jnp.exp(scored[h] - lse_ref[0, h : h + 1, pl.ds(base, width)])
            ds = p * (dprobs[h] - delta[h][:, base : base + width])
            for g in range(ext // 128):
                spans[h][:, pl.ds(base - 128 * g + 512, width)] += ds[128 * g : 128 * g + 128]
            low.append((p.astype(bf16), ds.astype(bf16)))
        dks = [dot(ds, q, NN) for _, ds in low]
        dvs = [dot(p, da, NN) for p, _ in low]
        dqs = [dot(kt[64 * h : 64 * h + 64, :ext], low[h][1], NN) for h in range(2)]
        lane = lax.broadcasted_iota(jnp.int32, (ext, 128), 1)
        dk_sum[:ext] += jnp.where(lane < 64, dks[0], dks[1])
        dv_sum[:ext] += jnp.where(lane < 64, dvs[0], dvs[1])
        dq_ref[pl.ds(base, width), :] = jnp.concatenate(dqs, axis=0).T.astype(bf16)
    dk_ref[...] = dk_sum[...].astype(bf16)
    dv_ref[...] = dv_sum[...].astype(bf16)
    for h in range(2):
        total = spans[h][0:8, :]
        for m in range(1, 16):
            total = total + pltpu.roll(spans[h][8 * m : 8 * m + 8, :], SPAN - 8 * m, 1)
        diag_ref[h] = total


def cross_forward_body(q_ref, k_ref, v_ref, o_ref, lse_ref):
    width = 256
    vt = transposed(v_ref[...])
    outs = {}
    for group in tasks_of(width, 8):
        scored = [
            dot(k_ref[...], head_of(q_ref[pl.ds(qb * width, width), :], h), NT) for qb, h in group
        ]
        weights = [softmax_cols(s) for s in scored]
        for (qb, h), (p, total, m) in zip(group, weights):
            outs[(qb, h)] = dot(vt[64 * h : 64 * h + 64, :], p, NN) * (1.0 / total)
            lse_ref[0, h : h + 1, pl.ds(qb * width, width)] = m + jnp.log(total)
            if h == 1:
                o_ref[pl.ds(qb * width, width), :] = (
                    jnp.concatenate([outs[(qb, 0)], outs[(qb, 1)]], axis=0).T.astype(bf16)
                )


def cross_backward_body(q_ref, k_ref, v_ref, a_ref, da_ref, lse_ref, dq_ref, dk_ref, dv_ref):
    width = 256
    delta = head_deltas(a_ref, da_ref)
    kt = transposed(k_ref[...])
    lane = lax.broadcasted_iota(jnp.int32, (LE, 128), 1)
    outs = {}
    dks = [None, None]
    dvs = [None, None]
    for group in tasks_of(width, 4):
        scored = [
            dot(k_ref[...], head_of(q_ref[pl.ds(qb * width, width), :], h), NT) for qb, h in group
        ]
        dprobs = [
            dot(v_ref[...], head_of(da_ref[pl.ds(qb * width, width), :], h), NT) for qb, h in group
        ]
        low = []
        for (qb, h), s, dp in zip(group, scored, dprobs):
            p = jnp.exp(s - lse_ref[0, h : h + 1, pl.ds(qb * width, width)])
            ds = p * (dp - delta[h][:, qb * width : (qb + 1) * width])
            low.append((p.astype(bf16), ds.astype(bf16)))
        for (qb, h), (p, ds) in zip(group, low):
            dk = dot(ds, q_ref[pl.ds(qb * width, width), :], NN)
            dv = dot(p, da_ref[pl.ds(qb * width, width), :], NN)
            dks[h] = dk if dks[h] is None else dks[h] + dk
            dvs[h] = dv if dvs[h] is None else dvs[h] + dv
            outs[(qb, h)] = dot(kt[64 * h : 64 * h + 64, :], ds, NN)
            if h == 1:
                dq_ref[pl.ds(qb * width, width), :] = (
                    jnp.concatenate([outs[(qb, 0)], outs[(qb, 1)]], axis=0).T.astype(bf16)
                )
    dk_ref[...] = jnp.where(lane < 64, dks[0], dks[1]).astype(bf16)
    dv_ref[...] = jnp.where(lane < 64, dvs[0], dvs[1]).astype(bf16)


def place():
    dp = lax.axis_index("dp")
    return (dp, dp % QUAD, lax.axis_index("row"), lax.axis_index("col"))


def quad_mate(dp, quarter, flip):
    return dp - quarter + (quarter ^ flip)


def greet_all(dp, quarter, row, col):
    barrier = pltpu.get_barrier_semaphore()
    for s in range(1, ROWS):
        pl.semaphore_signal(
            barrier, inc=1, device_id=(dp, (row + s) % ROWS, col), device_id_type=MESH
        )
    for k in range(1, QUAD):
        pl.semaphore_signal(
            barrier, inc=1, device_id=(quad_mate(dp, quarter, k), row, col), device_id_type=MESH
        )
    pl.semaphore_signal(barrier, inc=1, device_id=(dp, row, 1 - col), device_id_type=MESH)
    pl.semaphore_wait(barrier, ROWS + QUAD - 1)


class Gathering:
    AHEAD = 3

    def __init__(self, blocks, wholes, apart, joined, gain_pair, rel_pair, own_blocks, sems):
        self.blocks, self.wholes, self.own_blocks = blocks, wholes, own_blocks
        self.dp, self.quarter, self.row, self.col = place()
        self.partner = (self.dp, self.row, 1 - self.col)
        (
            self.z_send,
            self.z_recv,
            self.q_send,
            self.q_recv,
            self.c_send,
            self.c_recv,
            local_sem,
            s_send,
            s_recv,
        ) = sems
        self.started = []
        count, swaps = len(blocks), len(apart)
        row, col, quarter = self.row, self.col, self.quarter
        greet_all(self.dp, quarter, row, col)
        self.own = {}
        self.from_partner = {}

        def keep(src, dst, slot):
            local = pltpu.make_async_copy(src, dst, local_sem.at[slot])
            local.start()
            self.own[slot] = local

        def half(ref):
            return ref.at[col]

        def rel_at(r):
            return rel_pair[1].at[
                pl.ds(pl.multiple_of(r * 8, 8), 8), pl.ds(pl.multiple_of(col * 128, 128), 128)
            ]

        self.rel_at = rel_at
        self.swap = []
        for j in range(swaps):
            self.swap.append(
                self.remote(
                    apart[j].at[1 - col], half(joined[j]), s_send.at[j], s_recv.at[j], self.partner
                )
            )
            keep(apart[j].at[col], half(joined[j]), count + j)
        self.swap.append(
            self.remote(
                gain_pair[0], half(gain_pair[1]), s_send.at[swaps], s_recv.at[swaps], self.partner
            )
        )
        keep(gain_pair[0], half(gain_pair[1]), count + swaps)
        keep(rel_pair[0], rel_at(row), count + swaps + 1)
        self.rel_sems = (s_send, s_recv, swaps + 1)
        self.rel_copies = [
            self.remote(
                rel_pair[0],
                rel_at(row),
                s_send.at[swaps + 1 + s],
                s_recv.at[swaps + 1 + s],
                self.partner if s == 0 else (self.dp, (row + s) % ROWS, col),
            )
            for s in range(ROWS)
        ]
        self.z_copies = {}
        self.q_copies = {}
        self.local_sem = local_sem
        for i in range(self.AHEAD):
            self.offer(i)
        for i in range(count):
            keep(blocks[i], own_blocks[i], i)

    def offer(self, i):
        row, col = self.row, self.col
        whole_block = self.wholes[i].at[col, pl.ds(pl.multiple_of(row * BLOCK, BLOCK), BLOCK)]
        for s in range(1, ROWS):
            self.z_copies[(i, s)] = self.remote(
                self.blocks[i].at[pl.ds(pl.multiple_of(self.quarter * PIECE, PIECE), PIECE), :],
                self.part(i, row, self.quarter),
                self.z_send.at[i, s - 1],
                self.z_recv.at[i, s - 1],
                (self.dp, (row + s) % ROWS, col),
            )
        self.from_partner[(i, 0, 0)] = self.remote(
            self.blocks[i],
            whole_block,
            self.c_send.at[i, 0, 0],
            self.c_recv.at[i, 0, 0],
            self.partner,
        )

    def remote(self, src, dst, send_sem, recv_sem, device):
        copy = pltpu.make_async_remote_copy(
            src_ref=src,
            dst_ref=dst,
            send_sem=send_sem,
            recv_sem=recv_sem,
            device_id=device,
            device_id_type=MESH,
        )
        copy.start()
        self.started.append(copy)
        return copy

    def part(self, i, r, q):
        at = pl.multiple_of(r * BLOCK + q * PIECE, PIECE)
        return self.wholes[i].at[self.col, pl.ds(at, PIECE)]

    def rel_onward(self):
        s_send, s_recv, base = self.rel_sems
        for s in range(1, ROWS):
            self.rel_copies[s].wait_recv()
            ref = self.rel_at((self.row - s + ROWS) % ROWS)
            slot = base + ROWS - 1 + s
            self.rel_copies.append(
                self.remote(ref, ref, s_send.at[slot], s_recv.at[slot], self.partner)
            )

    def rel_arrived(self, slot):
        self.own[slot].wait()
        self.rel_copies[0].wait_recv()
        for copy in self.rel_copies[ROWS:]:
            copy.wait_recv()

    def hand_over(self, i, s, k, r):
        ref = self.part(i, r, self.quarter ^ k)
        self.from_partner[(i, s, k)] = self.remote(
            ref, ref, self.c_send.at[i, s, k], self.c_recv.at[i, s, k], self.partner
        )

    def to_mate(self, i, s, k, slot, ref):
        self.q_copies[(i, s, slot)] = self.remote(
            ref,
            ref,
            self.q_send.at[i, s - 1, slot - 1],
            self.q_recv.at[i, s - 1, slot - 1],
            (quad_mate(self.dp, self.quarter, k), self.row, self.col),
        )

    def spread(self, i):
        for s in range(1, ROWS):
            self.z_copies[(i, s)].wait_recv()
            r = (self.row - s + ROWS) % ROWS
            ref = self.part(i, r, self.quarter)
            for k in (1, 2):
                self.to_mate(i, s, k, k, ref)
            self.hand_over(i, s, 0, r)
        if i + self.AHEAD < len(self.blocks):
            self.offer(i + self.AHEAD)
        self.own[i].wait()
        self.own[i] = pltpu.make_async_copy(
            self.own_blocks[i],
            self.wholes[i].at[self.col, pl.ds(pl.multiple_of(self.row * BLOCK, BLOCK), BLOCK)],
            self.local_sem.at[i],
        )
        self.own[i].start()

    def share(self, i):
        for s in range(1, ROWS):
            r = (self.row - s + ROWS) % ROWS
            onward = 1 + (i + s) % 2
            for k in (onward, 3 - onward):
                self.q_copies[(i, s, k)].wait_recv()
                if k == onward:
                    self.to_mate(i, s, 3 - k, 3, self.part(i, r, self.quarter ^ k))
                self.hand_over(i, s, k, r)

    def close(self, i):
        for s in range(1, ROWS):
            self.q_copies[(i, s, 3)].wait_recv()
            self.hand_over(i, s, 3, (self.row - s + ROWS) % ROWS)

    def arrived(self, i):
        self.own[i].wait()
        for s in range(ROWS):
            for k in range(QUAD if s else 1):
                self.from_partner[(i, s, k)].wait_recv()

    def finish(self):
        for copy in self.started:
            copy.wait_send()


def forward_body(count, swaps, *refs):
    blocks = refs[:count]
    apart = refs[count : count + swaps]
    gain_in, rel_in, onehot_ref, piece_ref = refs[count + swaps : count + swaps + 4]
    refs = refs[count + swaps + 4 :]
    wholes = refs[:count]
    outs = refs[count : count + 9 + swaps + 1]
    refs = refs[count + 9 + swaps + 1 :]
    h2, rel_all, gains, rows_in, enc, cot, w_qkv, w_out, w_cq, w_ckv, w_co = refs[:11]
    qkv, a1, h1, q2, kv2, a2, t8, lse1, lse2, table, load_sem, save_sem = refs[11:23]
    own_blocks = refs[23 : 23 + count]
    joined = (rows_in, enc, cot)
    comm = Gathering(
        blocks,
        wholes,
        apart,
        joined,
        (gain_in, gains),
        (rel_in, rel_all),
        own_blocks,
        refs[23 + count :],
    )
    saving = []

    class Loads(list):
        def wait(self):
            for copy in self:
                copy.wait()

    def load(src, dst, slot):
        wide = src.shape[2]
        copies = Loads()
        for c in range(2):
            copies.append(
                pltpu.make_async_copy(
                    src.at[c], dst.at[:, c * wide : (c + 1) * wide], load_sem.at[slot, c]
                )
            )
            copies[-1].start()
        return copies

    def save(slot, src):
        copy = pltpu.make_async_copy(src, outs[slot], save_sem.at[slot])
        copy.start()
        saving.append(copy)

    def weight(i, dst):
        comm.arrived(i)
        return load(wholes[i], dst, 3 + i)

    def swapped(j, slot, ref):
        comm.swap[j].wait_recv()
        comm.own[count + j].wait()
        save(slot, ref)

    comm.rel_onward()
    comm.spread(0)
    comm.spread(1)
    swapped(0, 9, rows_in)
    swapped(swaps, 9 + swaps, gains)
    g_self = jnp.concatenate([gains[0, 0:1, :], gains[1, 0:1, :]], axis=1)
    g_cross = jnp.concatenate([gains[0, 1:2, :], gains[1, 1:2, :]], axis=1)
    comm.share(0)
    comm.spread(2)
    step = 256
    blocks_of = [slice(step * b, step * (b + 1)) for b in range(L // step)]
    comm.rel_arrived(count + swaps + 1)
    rel16 = jnp.concatenate([rel_all[:, :6], rel_all[:, 128:134]], axis=1).astype(bf16)
    bias = dot(rel16, onehot_ref[...], TN)
    for n in range(8):
        moved = pltpu.roll(bias, n, 1) if n else bias
        for h in range(12):
            t8[h, n : n + 1, :] = moved[h : h + 1]
    save(0, t8)
    comm.share(1)
    comm.close(0)
    loading = weight(0, w_qkv)
    comm.share(2)
    loading.wait()
    for n, at in enumerate(blocks_of):
        xb = jnp.concatenate([rows_in[0, at, :], rows_in[1, at, :]], axis=1).astype(f32)
        n1 = (xb * rms_of(xb) * g_self).astype(bf16)
        qkv[at, :] = dot(n1, w_qkv[...], NN).astype(bf16)
        if n == 0:
            comm.close(1)
        if n == 1:
            comm.spread(3)
        if n == 2:
            comm.close(2)
        if n == 3:
            comm.share(3)
    save(1, qkv)

    def lane(block):
        return pl.ds(pl.multiple_of(block * 128, 128), 128)

    def self_heads(hp, carry):
        base = (hp // 3) * 9 + (hp % 3) * 3
        self_forward_body(
            piece_ref,
            qkv.at[:, lane(base)],
            qkv.at[:, lane(base + 1)],
            qkv.at[:, lane(base + 2)],
            t8.at[pl.ds(2 * hp, 2)],
            a1.at[:, lane(hp)],
            lse1.at[pl.ds(hp, 1)],
            [table.at[0], table.at[1]],
        )
        return carry

    lax.fori_loop(0, 2, self_heads, 0)
    comm.spread(4)
    comm.close(3)
    loadings = [weight(1, w_out), weight(2, w_cq)]
    swapped(1, 10, enc)
    swapped(2, 11, cot)
    lax.fori_loop(2, 4, self_heads, 0)
    comm.share(4)
    loadings.append(weight(3, w_ckv))
    lax.fori_loop(4, 6, self_heads, 0)
    save(2, a1)
    save(3, lse1)
    comm.close(4)
    comm.spread(5)
    for copy in loadings:
        copy.wait()
    loading = weight(4, w_co)
    kv2[...] = dot(jnp.concatenate([enc[0], enc[1]], axis=1), w_ckv[...], NN).astype(bf16)
    save(6, kv2)
    for n, at in enumerate(blocks_of):
        xb = jnp.concatenate([rows_in[0, at, :], rows_in[1, at, :]], axis=1).astype(f32)
        h1b = xb + dot(a1[at, :], w_out[...], NT)
        h1[at, :] = h1b
        n2 = (h1b * rms_of(h1b) * g_cross).astype(bf16)
        q2[at, :] = dot(n2, w_cq[...], NN).astype(bf16)
    save(4, h1)
    save(5, q2)

    def cross_heads(hp, carry):
        base = (hp // 3) * 6 + hp % 3
        cross_forward_body(
            q2.at[:, lane(hp)],
            kv2.at[:, lane(base)],
            kv2.at[:, lane(base + 3)],
            a2.at[:, lane(hp)],
            lse2.at[pl.ds(hp, 1)],
        )
        return carry

    lax.fori_loop(0, 2, cross_heads, 0)
    comm.spread(6)
    comm.share(5)
    lax.fori_loop(2, 6, cross_heads, 0)
    save(7, a2)
    save(8, lse2)
    comm.close(5)
    loading.wait()
    for at in blocks_of:
        h2[at, :] = h1[at, :] + dot(a2[at, :], w_co[...], NT)
    comm.share(6)
    comm.close(6)
    comm.arrived(5)
    comm.arrived(6)
    for copy in saving:
        copy.wait()
    comm.finish()


def forward(blocks, apart, gains, rel, onehot, piece, number):
    count = len(blocks)
    swaps = len(apart)
    shape = jax.ShapeDtypeStruct
    saved = [
        shape((12, 8, SPAN), f32),
        shape((L, 3 * D), bf16),
        shape((L, D), bf16),
        shape((6, 2, L), f32),
        shape((L, D), f32),
        shape((L, D), bf16),
        shape((LE, 2 * D), bf16),
        shape((L, D), bf16),
        shape((6, 2, L), f32),
    ]
    saved += [shape(x.shape, x.dtype) for x in apart] + [shape((2, 8, HALF), f32)]
    wholes = [shape((2, D, b.shape[1]), b.dtype) for b in blocks]
    dma = pltpu.SemaphoreType.DMA
    any_spec = pl.BlockSpec(memory_space=pl.ANY)
    vmem = pl.BlockSpec(memory_space=pltpu.VMEM)
    scratch = [
        pltpu.VMEM((BUCKETS, 256), f32),
        pltpu.VMEM((2, 8, HALF), f32),
        pltpu.VMEM((2, L, HALF), bf16),
        pltpu.VMEM((2, LE, HALF), bf16),
        pltpu.VMEM((2, L, HALF), bf16),
        pltpu.VMEM((D, 3 * D), bf16),
        pltpu.VMEM((D, D), bf16),
        pltpu.VMEM((D, D), bf16),
        pltpu.VMEM((D, 2 * D), bf16),
        pltpu.VMEM((D, D), bf16),
        pltpu.VMEM((L, 3 * D), bf16),
        pltpu.VMEM((L, D), bf16),
        pltpu.VMEM((L, D), f32),
        pltpu.VMEM((L, D), bf16),
        pltpu.VMEM((LE, 2 * D), bf16),
        pltpu.VMEM((L, D), bf16),
        pltpu.VMEM((12, 8, SPAN), f32),
        pltpu.VMEM((6, 2, L), f32),
        pltpu.VMEM((6, 2, L), f32),
        pltpu.VMEM((2, 128, SPAN), f32),
        dma((8, 2)),
        dma((9 + swaps + 1,)),
    ]
    scratch += [pltpu.VMEM(b.shape, b.dtype) for b in blocks]
    scratch += [
        dma((count, ROWS - 1)),
        dma((count, ROWS - 1)),
        dma((count, ROWS - 1, QUAD - 1)),
        dma((count, ROWS - 1, QUAD - 1)),
        dma((count, ROWS, QUAD)),
        dma((count, ROWS, QUAD)),
        dma((count + swaps + 2,)),
        dma((swaps + 8,)),
        dma((swaps + 8,)),
    ]
    out = pl.pallas_call(
        lambda *refs: forward_body(count, swaps, *refs),
        out_shape=wholes + saved + [shape((L, D), f32)],
        in_specs=[any_spec] * (count + swaps + 2)
        + [vmem, pl.BlockSpec(memory_space=pltpu.SMEM)],
        out_specs=[any_spec] * (len(wholes) + len(saved)) + [vmem],
        scratch_shapes=scratch,
        compiler_params=pltpu.CompilerParams(
            collective_id=number, has_side_effects=True, vmem_limit_bytes=VMEM_LIMIT
        ),
        name="forward",
    )(*blocks, *apart, gains, rel, onehot, piece)
    return (out[:count], out[count + 9 : -1], out[count : count + 9] + out[-1:])


def rms_of(v):
    return lax.rsqrt(jnp.sum(v * v, axis=-1, keepdims=True) * (1.0 / D) + EPSILON)


def norm_back_rows(v, r, gain, dn):
    inner = jnp.sum(dn * gain * v, axis=-1, keepdims=True)
    dv = dn * gain * r - v * (r * r * r) * (inner * (1.0 / D))
    return (dv, jnp.sum(dn * v * r, axis=0, keepdims=True))


def ffn_body(
    h2_ref,
    cot_ref,
    gain_ref,
    wgu_ref,
    wd_ref,
    out_ref,
    dh2_ref,
    ggu_ref,
    gd_ref,
    dgain_ref,
    n3t,
    mid_all,
    e3t,
    dgu_all,
):
    step = pl.program_id(0)
    rows = h2_ref.shape[0]
    here = pl.ds(pl.multiple_of(step * rows, rows), rows)
    g_ffn = jnp.concatenate([gain_ref[0, 2:3, :], gain_ref[1, 2:3, :]], axis=1)
    g_final = jnp.concatenate([gain_ref[0, 3:4, :], gain_ref[1, 3:4, :]], axis=1)
    h2 = h2_ref[...]
    r3 = rms_of(h2)
    n3 = (h2 * r3 * g_ffn).astype(bf16)
    n3t[:, here] = transposed(n3)
    kept = []
    for c in range(4):
        at = (c % 2) * 512
        gate = dot(n3, wgu_ref[c // 2, :, at : at + 512], NN)
        up = dot(n3, wgu_ref[c // 2, :, at + 1024 : at + 1536], NN)
        act, slope = gelu_parts(gate)
        mid = (act * up).astype(bf16)
        mid_all[here, 512 * c : 512 * (c + 1)] = mid
        kept.append((act, up * slope))
    h3 = h2 + dot(mid_all[here, :1024], wd_ref[0], NT) + dot(mid_all[here, 1024:], wd_ref[1], NT)
    r4 = rms_of(h3)
    normed = (h3 * r4 * g_final).astype(bf16)
    out_ref[0] = normed[:, :HALF]
    out_ref[1] = normed[:, HALF:]
    dh3, dg_final = norm_back_rows(h3, r4, g_final, jnp.concatenate([cot_ref[0], cot_ref[1]], axis=1).astype(f32))
    e3 = dh3.astype(bf16)
    e3t[:, here] = transposed(e3)
    for c in range(4):
        at = (c // 2) * 2048 + (c % 2) * 512
        act, slope = kept[c]
        low = 512 * (c % 2)
        dmid = dot(e3, wd_ref[c // 2, :, low : low + 512], NN).astype(bf16).astype(f32)
        dgu_all[here, at : at + 512] = (dmid * slope).astype(bf16)
        dgu_all[here, at + 1024 : at + 1536] = (dmid * act).astype(bf16)
    dn3 = dot(dgu_all[here, :2048], wgu_ref[0], NT) + dot(dgu_all[here, 2048:], wgu_ref[1], NT)
    back, dg_ffn = norm_back_rows(h2, r3, g_ffn, dn3)
    dh2_ref[...] = dh3 + back

    @pl.when(step == 0)
    def _():
        dgain_ref[...] = jnp.zeros_like(dgain_ref)

    dgain_ref[2:3, :] += dg_ffn
    dgain_ref[3:4, :] += dg_final

    @pl.when(step == pl.num_programs(0) - 1)
    def _():
        for c in range(8):
            span = slice(512 * c, 512 * (c + 1))
            low = slice(512 * (c % 4), 512 * (c % 4 + 1))
            ggu_ref[c // 4, :, low] = dot(n3t[...], dgu_all[:, span], NN).astype(bf16)
        for c in range(4):
            span = slice(512 * c, 512 * (c + 1))
            low = slice(512 * (c % 2), 512 * (c % 2 + 1))
            gd_ref[c // 2, :, low] = dot(e3t[...], mid_all[:, span], NN).astype(bf16)


def feed_forward(h2, cot, gains, wgu, wd):
    rows = 256
    def whole(*shape):
        return pl.BlockSpec(shape, lambda i: (0,) * len(shape), pipeline_mode=pl.Buffered(1))

    block = pl.BlockSpec((rows, D), lambda i: (i, 0))
    return pl.pallas_call(
        ffn_body,
        grid=(L // rows,),
        in_specs=[
            block,
            pl.BlockSpec((2, rows, HALF), lambda i: (0, i, 0)),
            whole(2, 8, HALF),
            whole(2, D, 2048),
            whole(2, D, 1024),
        ],
        out_specs=[
            pl.BlockSpec((2, rows, HALF), lambda i: (0, i, 0)),
            block,
            whole(2, D, 2048),
            whole(2, D, 1024),
            whole(8, D),
        ],
        out_shape=[
            jax.ShapeDtypeStruct((2, L, HALF), bf16),
            jax.ShapeDtypeStruct((L, D), f32),
            jax.ShapeDtypeStruct((2, D, 2048), bf16),
            jax.ShapeDtypeStruct((2, D, 1024), bf16),
            jax.ShapeDtypeStruct((8, D), f32),
        ],
        scratch_shapes=[
            pltpu.VMEM((D, L), bf16),
            pltpu.VMEM((L, 2048), bf16),
            pltpu.VMEM((D, L), bf16),
            pltpu.VMEM((L, 4096), bf16),
        ],
        compiler_params=pltpu.CompilerParams(vmem_limit_bytes=VMEM_LIMIT),
        name="feed_forward",
    )(h2, cot, gains, wgu, wd)


class Summing:
    def __init__(self, widths, pair, first, second, third, final, outs, sems):
        self.widths = widths
        self.pair, self.first, self.second, self.third = pair, first, second, third
        self.final, self.outs = final, outs
        self.sends, self.recvs, self.local_sem = sems
        self.dp, self.quarter, self.row, self.col = place()
        self.partner = (self.dp, self.row, 1 - self.col)
        self.begun = []
        self.pending = {}
        self.kept = []
        greet_all(self.dp, self.quarter, self.row, self.col)

    def remote(self, src, dst, send_sem, recv_sem, device):
        copy = pltpu.make_async_remote_copy(
            src_ref=src,
            dst_ref=dst,
            send_sem=send_sem,
            recv_sem=recv_sem,
            device_id=device,
            device_id_type=MESH,
        )
        copy.start()
        self.begun.append(copy)
        return copy

    def send(self, i, slot, src, dst, device):
        self.pending[(i, slot)] = self.remote(
            src, dst, self.sends.at[i, slot], self.recvs.at[i, slot], device
        )

    def mate(self, k):
        return (quad_mate(self.dp, self.quarter, k), self.row, self.col)

    def offer(self, i, src):
        self.send(i, 0, src, self.pair[i], self.partner)

    def stage1(self, i, own):
        self.pending[(i, 0)].wait_recv()
        pair = self.pair[i]
        for r in range(ROWS):
            pair[r] = pair[r] + own(r)
            if r % 2 == 1:
                k = 1 if r == 1 else 2
                for j, q in enumerate((self.quarter ^ k, self.quarter ^ 3)):
                    self.send(
                        i,
                        r + j,
                        pair.at[pl.ds(r - 1, 2), q],
                        self.first[i].at[pl.ds(r - 1, 2), j],
                        self.mate(k),
                    )

    def stage2(self, i):
        first, pair = self.first[i], self.pair[i]
        for h in range(2):
            k = 1 if h == 0 else 2
            self.pending[(i, 1 + 2 * h)].wait_recv()
            self.pending[(i, 2 + 2 * h)].wait_recv()
            for r in (2 * h, 2 * h + 1):
                first[r, 1] = first[r, 1] + pair[r, self.quarter ^ 3 ^ k]
            self.send(
                i,
                5 + h,
                first.at[pl.ds(2 * h, 2), 1],
                self.second[i].at[pl.ds(2 * h, 2)],
                self.mate(3 ^ k),
            )
            for r in (2 * h, 2 * h + 1):
                first[r, 0] = first[r, 0] + pair[r, self.quarter]

    def stage3(self, i):
        second = self.second[i]
        for h in range(2):
            self.pending[(i, 5 + h)].wait_recv()
            for r in (2 * h, 2 * h + 1):
                second[r] = second[r] + self.first[i][r, 0]
        for s in range(1, ROWS):
            to = (self.row + s) % ROWS
            self.send(i, 6 + s, second.at[to], self.third[i].at[s - 1], (self.dp, to, self.col))

    def stage4(self, i):
        for s in range(1, ROWS):
            self.pending[(i, 6 + s)].wait_recv()
        total = self.second[i][self.row].astype(f32)
        for s in range(1, ROWS):
            total = total + self.third[i][s - 1].astype(f32)
        self.final[i][...] = total.astype(bf16)
        there = self.outs[i].at[self.quarter]
        for k in (1, 2):
            self.send(i, 9 + k, self.final[i], there, self.mate(k))
        copy = pltpu.make_async_copy(self.final[i], there, self.local_sem.at[i])
        copy.start()
        self.kept.append(copy)

    def stage5(self, i):
        onward = 1 + i % 2
        for k in (onward, 3 - onward):
            self.pending[(i, 9 + k)].wait_recv()
            if k == onward:
                ref = self.outs[i].at[self.quarter ^ k]
                self.send(i, 12, ref, ref, self.mate(3 - k))

    def finish(self):
        for i in range(len(self.widths)):
            self.pending[(i, 12)].wait_recv()
        for copy in self.kept:
            copy.wait()
        for copy in self.begun:
            copy.wait_send()


CHUNKS = (1024, 1024, 1024, HALF, HALF, 2 * HALF, HALF, HALF, HALF, HALF)
(F0, F1, F2, CO, CQ, CKV, SO, QA, QB, QC) = range(10)
SMALL = (16, 896)


def backward_body(*refs):
    (
        dh2_in,
        g_gu,
        g_down,
        t8_in,
        qkv_in,
        a1_in,
        lse1_in,
        h1_in,
        q2_in,
        kv2_in,
        a2_in,
        lse2_in,
        x_in,
        enc_in,
        w_qkv_in,
        w_out_in,
        w_cq_in,
        w_ckv_in,
        w_co_in,
        made,
        gains,
        ffn_gains,
        onehot_ref,
        piece_ref,
    ) = refs[:24]
    count = len(CHUNKS)
    output, hidden_grad, enc_grad = refs[24:27]
    sums = refs[27 : 27 + count]
    small_out = refs[27 + count]
    refs = refs[28 + count :]
    pair = refs[:count]
    first = refs[count : 2 * count]
    second = refs[2 * count : 3 * count]
    third = refs[3 * count : 4 * count]
    final = refs[4 * count : 5 * count]
    refs = refs[5 * count :]
    gr_co, gr_cq, gr_ckv, gr_out, gr_qkv = refs[:5]
    total, turned, mixed, dmixed, w_big, w_cq, w_out, enc, rows, qkv, t8, lse1, lse2, x = refs[5:19]
    dk_sum, dv_sum, diag, spans_all, eg, small = refs[19:25]
    load_sem, ex_send, ex_recv, ex_local, small_send, small_recv = refs[25:31]
    comm = Summing(CHUNKS, pair, first, second, third, final, sums, refs[31:34])
    col, row, partner = comm.col, comm.row, comm.partner

    def load(slot, *pairs):
        copies = []
        for n, (src, dst) in enumerate(pairs):
            copies.append(pltpu.make_async_copy(src, dst, load_sem.at[slot, n]))
            copies[-1].start()
        return copies

    def wait(copies):
        for copy in copies:
            copy.wait()

    def halves(src, dst, offset=0):
        wide = src.shape[2]
        return [
            (src.at[c], dst.at[:, offset + c * wide : offset + (c + 1) * wide]) for c in range(2)
        ]

    def own_ffn(i):
        src = (g_gu, g_gu, g_down)[i]
        lanes_of = pl.ds(1024 if i == 1 else 0, 1024)
        slot = i % 2
        return load(
            12 + i,
            *[
                (
                    src.at[col, r, :, :, lanes_of],
                    gr_qkv.at[slot * 4 + r, :, :, pl.ds(0, 1024)],
                )
                for r in range(ROWS)
            ],
        )

    bouncing = load(0, (made.at[col], dmixed.at[:, :HALF]))
    ex_out = comm.remote(
        made.at[1 - col], output.at[col], ex_send.at[0], ex_recv.at[0], partner
    )
    comm.offer(F0, g_gu.at[1 - col, :, :, :, pl.ds(0, 1024)])
    comm.offer(F1, g_gu.at[1 - col, :, :, :, pl.ds(1024, 1024)])
    comm.offer(F2, g_down.at[1 - col])
    l_total = load(1, (dh2_in, total))
    l_co = load(2, *halves(w_co_in, w_big, 2 * D))
    l_a2 = load(3, (a2_in, mixed))
    l_own = [own_ffn(0), own_ffn(1)]
    l_q2 = load(4, (q2_in, qkv.at[:, :D]), (kv2_in, qkv.at[:LE, D:]), (lse2_in, lse2))
    l_h1 = load(
        5, *[(h1_in.at[pl.ds(512 * n, 512)], rows.at[:, D * n : D * (n + 1)]) for n in range(2)]
    )
    l_ckv = load(6, *halves(w_ckv_in, w_big))
    l_cq = load(7, *halves(w_cq_in, w_cq))
    l_enc = load(8, *halves(enc_in, enc))
    l_out = load(9, *halves(w_out_in, w_out))
    l_x = load(10, *halves(x_in, x))
    l_t8 = load(11, (t8_in, t8), (lse1_in, lse1))

    step = 256
    blocks_of = [slice(step * b, step * (b + 1)) for b in range(L // step)]
    g_self = jnp.concatenate([gains[0, 0:1, :], gains[1, 0:1, :]], axis=1)
    g_cross = jnp.concatenate([gains[0, 1:2, :], gains[1, 1:2, :]], axis=1)

    def lane(block):
        if isinstance(block, int):
            return pl.ds(block * 128, 128)
        return pl.ds(pl.multiple_of(block * 128, 128), 128)

    def put(dst, value):
        dst[...] = value.astype(bf16).reshape(dst.shape)

    def own_of(ref):
        return lambda r: ref[col, r]

    def own_loaded(i):
        slot = i % 2
        return lambda r: gr_qkv[slot * 4 + r, :, :, pl.ds(0, 1024)]

    wait(bouncing)
    keep_out = pltpu.make_async_copy(dmixed.at[:, :HALF], output.at[col], ex_local.at[0])
    keep_out.start()
    wait(l_total)
    for at in blocks_of:
        turned[:, at] = transposed(total[at, :])
    wait(l_co)
    keep_out.wait()
    for at in blocks_of:
        dmixed[at, :] = dot(total[at, :].astype(bf16), w_big[:, 2 * D :], NN).astype(bf16)
    wait(l_a2)
    for c in range(2):
        put(gr_co.at[c], dot(turned[...], mixed[:, HALF * c : HALF * (c + 1)], NN))
    comm.offer(CO, gr_co.at[1 - col])
    wait(l_own[0])
    comm.stage1(F0, own_loaded(0))
    wait(l_q2)

    def cross_heads(hp, carry):
        base = 6 + (hp // 3) * 6 + hp % 3
        queries = qkv.at[:, lane(hp)]
        keys = qkv.at[pl.ds(0, LE), lane(base)]
        values = qkv.at[pl.ds(0, LE), lane(base + 3)]
        cross_backward_body(
            queries,
            keys,
            values,
            mixed.at[:, lane(hp)],
            dmixed.at[:, lane(hp)],
            lse2.at[pl.ds(hp, 1)],
            queries,
            keys,
            values,
        )
        return carry

    lax.fori_loop(0, 2, cross_heads, 0)
    wait(l_own[1])
    comm.stage1(F1, own_loaded(1))
    l_own.append(own_ffn(2))
    lax.fori_loop(2, 4, cross_heads, 0)
    comm.stage2(F0)
    wait(l_own[2])
    comm.stage1(F2, own_loaded(2))
    comm.stage1(CO, own_of(gr_co))
    lax.fori_loop(4, 6, cross_heads, 0)
    l_a1 = load(3, (a1_in, mixed))
    comm.stage2(F1)
    wait(l_h1)

    def h1_rows(b):
        return rows[256 * (b % 2) : 256 * (b % 2 + 1), D * (b // 2) : D * (b // 2 + 1)]

    for b, at in enumerate(blocks_of):
        h1b = h1_rows(b)
        turned[:, at] = transposed((h1b * rms_of(h1b) * g_cross).astype(bf16))
    for c in range(2):
        put(gr_cq.at[c], dot(turned[...], qkv[:, HALF * c : HALF * (c + 1)], NN))
    comm.offer(CQ, gr_cq.at[1 - col])
    wait(l_enc)
    enct = transposed(enc[...])
    for c in range(2):
        put(gr_ckv.at[c], dot(enct, qkv[:LE, D + D * c : D + D * (c + 1)], NN))
    comm.offer(CKV, gr_ckv.at[1 - col])
    comm.stage2(F2)
    comm.stage3(F0)
    wait(l_ckv)
    back = dot(qkv[:LE, D:], w_big[:, : 2 * D], NT)
    eg[0] = back[:, :HALF]
    eg[1] = back[:, HALF:]
    ex_eg = comm.remote(eg.at[1 - col], enc_grad.at[col], ex_send.at[1], ex_recv.at[1], partner)
    keep_eg = pltpu.make_async_copy(eg.at[col], enc_grad.at[col], ex_local.at[1])
    keep_eg.start()
    l_qkv = load(2, *halves(w_qkv_in, w_big))
    wait(l_cq)
    wait(l_out)
    comm.stage2(CO)
    dg_cross = jnp.zeros((1, D), f32)
    for b, at in enumerate(blocks_of):
        h1b = h1_rows(b)
        dn2 = dot(qkv[at, :D], w_cq[...], NT)
        dv, dg = norm_back_rows(h1b, rms_of(h1b), g_cross, dn2)
        dg_cross = dg_cross + dg
        dh1 = total[at, :] + dv
        total[at, :] = dh1
        e1 = dh1.astype(bf16)
        turned[:, at] = transposed(e1)
        dmixed[at, :] = dot(e1, w_out[...], NN).astype(bf16)
        if b == 1:
            comm.stage3(F1)
            comm.stage1(CQ, own_of(gr_cq))
    l_q1 = load(4, (qkv_in, qkv))
    comm.stage1(CKV, own_of(gr_ckv))
    wait(l_a1)
    for c in range(2):
        put(gr_out.at[c], dot(turned[...], mixed[:, HALF * c : HALF * (c + 1)], NN))
    comm.offer(SO, gr_out.at[1 - col])
    comm.stage3(F2)
    comm.stage3(CO)
    wait(l_x)
    for at in blocks_of:
        xb = x[at, :].astype(f32)
        turned[:, at] = transposed((xb * rms_of(xb) * g_self).astype(bf16))
    wait(l_t8)
    wait(l_q1)
    table = [rows.at[pl.ds(128 * h, 128)] for h in range(2)]
    spans = [rows.at[pl.ds(256 + 128 * h, 128)] for h in range(2)]
    spans_all[...] = jnp.zeros_like(spans_all)

    def self_heads(hp):
        base = 9 * (hp // 3) + 3 * (hp % 3)
        queries, keys, values = [qkv.at[:, lane(base + n)] for n in range(3)]
        self_backward_body(
            piece_ref,
            queries,
            keys,
            values,
            t8.at[pl.ds(2 * hp, 2)],
            mixed.at[:, lane(hp)],
            dmixed.at[:, lane(hp)],
            lse1.at[pl.ds(hp, 1)],
            queries,
            keys,
            values,
            diag,
            table,
            spans,
            dk_sum,
            dv_sum,
        )
        for h in range(2):
            lined = diag[h, 0:1, :]
            for n in range(1, 8):
                lined = lined + pltpu.roll(diag[h, n : n + 1, :], SPAN - n, 1)
            spans_all[pl.ds(2 * hp + h, 1), :] = lined

    def qkv_grad(j, c):
        return gr_qkv.at[pl.ds(4 * c, 4), :, :, pl.ds(HALF * j, HALF)]

    def grads_of(j):
        for c in range(2):
            at = 3 * HALF * c + HALF * j
            put(qkv_grad(j, c), dot(turned[...], qkv[:, at : at + HALF], NN))
        comm.offer(QA + j, qkv_grad(j, 1 - col))

    def own_qkv(j):
        return lambda r: gr_qkv[4 * col + r, :, :, pl.ds(HALF * j, HALF)]

    self_heads(0)
    comm.stage1(SO, own_of(gr_out))
    comm.stage2(CQ)
    comm.stage4(F0)
    self_heads(3)
    comm.stage2(CKV)
    comm.stage4(F1)
    grads_of(0)
    self_heads(1)
    comm.stage1(QA, own_qkv(0))
    comm.stage2(SO)
    comm.stage3(CQ)
    comm.stage3(CKV)
    comm.stage4(F2)
    comm.stage4(CO)
    comm.stage5(F0)
    self_heads(4)
    comm.stage2(QA)
    comm.stage3(SO)
    comm.stage4(CQ)
    comm.stage5(F1)
    grads_of(1)
    self_heads(2)
    comm.stage1(QB, own_qkv(1))
    comm.stage3(QA)
    comm.stage4(CKV)
    comm.stage5(F2)
    comm.stage5(CO)
    self_heads(5)
    comm.stage2(QB)
    comm.stage4(QA)
    comm.stage4(SO)
    comm.stage5(CQ)
    comm.stage5(CKV)
    grads_of(2)
    comm.stage3(QB)

    wait(l_qkv)
    left = spans_all[...]
    rel = jnp.zeros((16, BUCKETS), f32)
    for _ in range(3):
        high = left.astype(bf16)
        rel = rel + dot(high, onehot_ref[...], NT)
        left = left - high.astype(f32)
    dg_self = jnp.zeros((1, D), f32)
    leaving = []

    def half_of(c):
        return pl.ds(pl.multiple_of(c * HALF, 128), HALF)

    for b, at in enumerate(blocks_of):
        xb = x[at, :].astype(f32)
        dn1 = dot(qkv[at, :], w_big[...], NT)
        dv, dg = norm_back_rows(xb, rms_of(xb), g_self, dn1)
        dg_self = dg_self + dg
        total[at, :] = total[at, :] + dv
        leaving.append(
            comm.remote(
                total.at[at, half_of(1 - col)],
                hidden_grad.at[col, at],
                ex_send.at[2 + b],
                ex_recv.at[2 + b],
                partner,
            )
        )
        kept = pltpu.make_async_copy(
            total.at[at, half_of(col)], hidden_grad.at[col, at], ex_local.at[2 + b]
        )
        kept.start()
        comm.kept.append(kept)
        if b == 0:
            comm.stage1(QC, own_qkv(2))
            comm.stage5(QA)
        if b == 1:
            comm.stage4(QB)
        if b == 2:
            comm.stage2(QC)
            comm.stage5(SO)

    small[0] = jnp.zeros(SMALL, f32)
    small[0, 0:1, :D] = dg_self
    small[0, 1:2, :D] = dg_cross
    small[0, 2:4, :D] = ffn_gains[2:4, :]
    small[0, :, D : D + BUCKETS] = rel
    passing = {}

    def pass_on(slot, src, dst, device):
        passing[slot] = comm.remote(
            small.at[src], small.at[dst], small_send.at[slot], small_recv.at[slot], device
        )

    pass_on(0, 0, 1, partner)
    comm.stage3(QC)
    passing[0].wait_recv()
    small[2] = small[0] + small[1]
    pass_on(1, 2, 3, comm.mate(1))
    comm.stage5(QB)
    passing[1].wait_recv()
    small[4] = small[2] + small[3]
    pass_on(2, 4, 5, comm.mate(2))
    comm.stage4(QC)
    passing[2].wait_recv()
    small[6 + row] = small[4] + small[5]
    for s in range(1, ROWS):
        pass_on(2 + s, 6 + row, 6 + row, (comm.dp, (row + s) % ROWS, col))
    comm.stage5(QC)
    for s in range(1, ROWS):
        passing[2 + s].wait_recv()
    small_out[...] = (small[6] + small[7]) + (small[8] + small[9])
    keep_eg.wait()
    ex_out.wait_recv()
    ex_eg.wait_recv()
    for copy in leaving:
        copy.wait_recv()
    comm.finish()


def backward(args, onehot, piece, number):
    shape = jax.ShapeDtypeStruct
    dma = pltpu.SemaphoreType.DMA
    any_spec = pl.BlockSpec(memory_space=pl.ANY)
    vmem = pl.BlockSpec(memory_space=pltpu.VMEM)
    count = len(CHUNKS)
    quarters = (ROWS, QUAD, PIECE)
    scratch = [pltpu.VMEM(quarters + (w,), bf16) for w in CHUNKS]
    scratch += [pltpu.VMEM((ROWS, 2, PIECE, w), bf16) for w in CHUNKS]
    scratch += [pltpu.VMEM((ROWS, PIECE, w), bf16) for w in CHUNKS]
    scratch += [pltpu.VMEM((ROWS - 1, PIECE, w), bf16) for w in CHUNKS]
    scratch += [pltpu.VMEM((PIECE, w), bf16) for w in CHUNKS]
    scratch += [
        pltpu.VMEM((2,) + quarters + (HALF,), bf16),
        pltpu.VMEM((2,) + quarters + (HALF,), bf16),
        pltpu.VMEM((2,) + quarters + (2 * HALF,), bf16),
        pltpu.VMEM((2,) + quarters + (HALF,), bf16),
        pltpu.VMEM((2 * ROWS, QUAD, PIECE, 3 * HALF), bf16),
        pltpu.VMEM((L, D), f32),
        pltpu.VMEM((D, L), bf16),
        pltpu.VMEM((L, D), bf16),
        pltpu.VMEM((L, D), bf16),
        pltpu.VMEM((D, 3 * D), bf16),
        pltpu.VMEM((D, D), bf16),
        pltpu.VMEM((D, D), bf16),
        pltpu.VMEM((LE, D), bf16),
        pltpu.VMEM((L // 2, 2 * D), f32),
        pltpu.VMEM((L, 3 * D), bf16),
        pltpu.VMEM((12, 8, SPAN), f32),
        pltpu.VMEM((6, 2, L), f32),
        pltpu.VMEM((6, 2, L), f32),
        pltpu.VMEM((L, D), bf16),
        pltpu.VMEM((L, 128), f32),
        pltpu.VMEM((L, 128), f32),
        pltpu.VMEM((2, 8, SPAN), f32),
        pltpu.VMEM((16, SPAN), f32),
        pltpu.VMEM((2, LE, HALF), f32),
        pltpu.VMEM((6 + ROWS,) + SMALL, f32),
        dma((15, 4)),
        dma((6,)),
        dma((6,)),
        dma((6,)),
        dma((6,)),
        dma((6,)),
        dma((count, 13)),
        dma((count, 13)),
        dma((count,)),
    ]
    out = pl.pallas_call(
        backward_body,
        out_shape=[
            shape((2, L, HALF), bf16),
            shape((2, L, HALF), f32),
            shape((2, LE, HALF), f32),
        ]
        + [shape((QUAD, PIECE, w), bf16) for w in CHUNKS]
        + [shape(SMALL, f32)],
        in_specs=[any_spec] * 20
        + [vmem] * 3
        + [pl.BlockSpec(memory_space=pltpu.SMEM)],
        out_specs=[any_spec] * (3 + count) + [vmem],
        scratch_shapes=scratch,
        compiler_params=pltpu.CompilerParams(
            collective_id=number, has_side_effects=True, vmem_limit_bytes=VMEM_LIMIT
        ),
        name="backward",
    )(*args, onehot, piece)
    return (out[:3], [o.reshape(BLOCK, o.shape[2]) for o in out[3:-1]], out[-1])


def inverse_rms(v):
    return lax.rsqrt(jnp.mean(v * v, axis=-1, keepdims=True) + EPSILON)


def norm_backward(v, r, gain, dn):
    inner = jnp.sum(dn * gain * v, axis=-1, keepdims=True)
    dv = dn * gain * r - v * (r * r * r) * (inner / D)
    return (dv, jnp.sum(dn * v * r, axis=0))


def gelu_parts(t):
    inner = ROOT_TWO_PI * (t + 0.044715 * t * t * t)
    th = jnp.tanh(inner)
    value = 0.5 * t * (1.0 + th)
    slope = 0.5 * (1.0 + th) + 0.5 * t * (1.0 - th * th) * ROOT_TWO_PI * (
        1.0 + 3.0 * 0.044715 * t * t
    )
    return (value, slope)


def body(
    quads,
    hidden_in,
    encoded,
    cotangent,
    piece_start,
    image_piece_lengths,
    bucket_table,
    self_query,
    self_key,
    self_value,
    self_out,
    rel_weight,
    cross_query,
    cross_key,
    cross_value,
    cross_out,
    ffn_gate,
    ffn_up,
    ffn_down,
    gain_self,
    gain_cross,
    gain_ffn,
    gain_final,
):
    col = lax.axis_index("col")
    row = lax.axis_index("row")
    blocks = (
        jnp.stack(
            [w.reshape(BLOCK, 3, 128) for w in (self_query, self_key, self_value)], axis=2
        ).reshape(BLOCK, 3 * HALF),
        self_out.T,
        cross_query,
        jnp.concatenate([cross_key, cross_value], axis=1),
        cross_out.T,
        jnp.concatenate([ffn_gate, ffn_up], axis=1),
        ffn_down.T,
    )
    gain_block = jnp.stack([gain_self, gain_cross, gain_ffn, gain_final])
    gain_block = jnp.concatenate([gain_block, jnp.zeros_like(gain_block)])
    rel_block = jnp.pad(rel_weight.astype(f32), ((0, 0), (0, 122)))
    turned_table = bucket_table[:SPAN][::-1]
    onehot = (turned_table[None, :] == jnp.arange(BUCKETS, dtype=jnp.int32)[:, None]).astype(bf16)
    starts = lax.dynamic_index_in_dim(piece_start, col, 0, keepdims=False)
    lengths = lax.dynamic_index_in_dim(image_piece_lengths, col, 0, keepdims=False)
    piece = jnp.concatenate([starts, starts + lengths])
    wholes, (x, enc, cot, gains), saved = forward(
        blocks,
        (hidden_in, encoded, cotangent),
        gain_block,
        rel_block,
        onehot,
        piece,
        0,
    )
    t8, qkv, a1, lse1, h1, q2, kv2, a2, lse2, h2 = saved
    made, dh2, gr_gu, gr_down, ffn_gains = feed_forward(h2, cot, gains, wholes[5], wholes[6])
    cut = (2, ROWS, QUAD, PIECE)
    (output, hidden_grad, enc_grad), grads, small = backward(
        (
            dh2,
            gr_gu.reshape(cut + (2048,)),
            gr_down.reshape(cut + (1024,)),
            t8,
            qkv,
            a1,
            lse1,
            h1,
            q2,
            kv2,
            a2,
            lse2,
            x,
            enc,
            *wholes[:5],
            made,
            gains,
            ffn_gains,
        ),
        onehot,
        piece,
        1,
    )
    if quads > 1:
        grads, small = jax.tree.map(
            lambda t: lax.psum(t, "dp") * jnp.asarray(1.0 / QUAD, t.dtype), (grads, small)
        )
    grads = [g.astype(f32) for g in grads]
    gr_gate, gr_up, gr_down, gr_co, gr_cq, gr_ckv, gr_out = grads[:7]
    gr_q, gr_k, gr_v = [
        jnp.concatenate([g[:, 128 * n : 128 * (n + 1)] for g in grads[7:]], axis=1)
        for n in range(3)
    ]
    gain_sums = lax.dynamic_slice_in_dim(small[:4], col * HALF, HALF, 1)
    gr_rel = lax.dynamic_slice(small, (col * 6, D + row * 8), (6, 8)).T
    return (
        output,
        hidden_grad,
        enc_grad,
        gr_q,
        gr_k,
        gr_v,
        gr_out.T,
        gr_rel,
        gr_cq,
        gr_ckv[:, :HALF],
        gr_ckv[:, HALF:],
        gr_co.T,
        gr_gate,
        gr_up,
        gr_down.T,
        gain_sums[0],
        gain_sums[1],
        gain_sums[2],
        gain_sums[3],
    )


def solution(mesh):
    batch = P(("dp", "row"), None, "col")
    inward = P("row", "col")
    outward = P("col", "row")
    gain = P("col")
    weights = (
        (inward,) * 3 + (outward, inward) + (inward,) * 3 + (outward,) + (inward,) * 2 + (outward,)
    )
    placed = (batch,) * 3 + (P(("dp", "row"), None),) * 2 + (P(),) + weights + (gain,) * 4
    return jax.shard_map(
        lambda *args: body(mesh.shape["dp"] // QUAD, *args),
        mesh=mesh,
        in_specs=placed,
        out_specs=(batch,) * 3 + weights + (gain,) * 4,
        check_vma=False,
    )
```

```python
import math

import jax
import jax.numpy as jnp
from jax import lax
from jax.experimental import pallas as pl
from jax.experimental.pallas import tpu as pltpu
from jax.sharding import PartitionSpec as P

D = 768
HALF = 384
L = 1024
LE = 256
BUCKETS = 32
SPAN = 1536
EPSILON = 1e-06
MASKED = -1e30
ROOT_TWO_PI = math.sqrt(2.0 / math.pi)
MESH = pl.DeviceIdType.MESH
ROWS = 4
QUAD = 4
BLOCK = D // ROWS
PIECE = BLOCK // QUAD
f32 = jnp.float32
bf16 = jnp.bfloat16
NT = (((1,), (1,)), ((), ()))
NN = (((1,), (0,)), ((), ()))
TN = (((0,), (0,)), ((), ()))
VMEM_LIMIT = 60 * 2**20


def dot(a, b, dims):
    return lax.dot_general(a, b, dims, preferred_element_type=f32)


def head_of(x, h):
    lane = lax.broadcasted_iota(jnp.int32, x.shape, 1)
    return jnp.where((lane >= 64 * h) & (lane < 64 * h + 64), x, jnp.zeros_like(x))


def transposed(x):
    return x.astype(f32).T.astype(bf16)


def spread_bias(t8_ref, table):
    for h in range(2):
        t = t8_ref[h]
        for m in range(16):
            table[h][8 * m : 8 * m + 8, :] = pltpu.roll(t, 8 * m, 1)


def allowed_rows(piece_ref, base, rows, width):
    s0 = piece_ref[0]
    s1 = piece_ref[1]
    e0 = piece_ref[2]
    e1 = piece_ref[3]
    c = lax.broadcasted_iota(jnp.int32, (1, width), 1) + base
    last = jnp.where(
        (c >= s0) & (c < e0), e0 - 1, jnp.where((c >= s1) & (c < e1), e1 - 1, 0)
    )
    last = jnp.maximum(c, last)
    return lax.broadcasted_iota(jnp.int32, (rows, width), 0) + base <= last


def extent(qb, width):
    return 512 * ((qb * width) // 512 + 1)


def biased_scores(k_ref, q_head, table, h, base, width, ext, ok):
    s = dot(k_ref[:ext, :], q_head, NT)
    bias = jnp.concatenate(
        [table[h][:, pl.ds(base - 128 * g + 512, width)] for g in range(ext // 128)], axis=0
    )
    s = s + bias
    tail = jnp.where(ok, s[base:], MASKED)
    return tail if base == 0 else jnp.concatenate([s[:base], tail], axis=0)


def softmax_cols(s):
    m = jnp.max(s, axis=0, keepdims=True)
    p = jnp.exp(s - m)
    total = jnp.sum(p, axis=0, keepdims=True)
    return (p.astype(bf16), total, m)


def tasks_of(width, group):
    tasks = [(qb, h) for qb in range(L // width) for h in range(2)]
    return [tasks[i : i + group] for i in range(0, len(tasks), group)]


def self_forward_body(piece_ref, q_ref, k_ref, v_ref, t8_ref, o_ref, lse_ref, table):
    width = 256
    vt = transposed(v_ref[...])
    spread_bias(t8_ref, table)
    oks = [
        allowed_rows(piece_ref, qb * width, extent(qb, width) - qb * width, width)
        for qb in range(L // width)
    ]
    outs = {}
    for group in tasks_of(width, 8):
        scored = [
            biased_scores(
                k_ref,
                head_of(q_ref[pl.ds(qb * width, width), :], h),
                table,
                h,
                qb * width,
                width,
                extent(qb, width),
                oks[qb],
            )
            for qb, h in group
        ]
        weights = [softmax_cols(s) for s in scored]
        for (qb, h), (p, total, m) in zip(group, weights):
            mixed = dot(vt[64 * h : 64 * h + 64, : extent(qb, width)], p, NN)
            outs[(qb, h)] = mixed * (1.0 / total)
            lse_ref[0, h : h + 1, pl.ds(qb * width, width)] = m + jnp.log(total)
            if h == 1:
                o_ref[pl.ds(qb * width, width), :] = (
                    jnp.concatenate([outs[(qb, 0)], outs[(qb, 1)]], axis=0).T.astype(bf16)
                )


def head_deltas(a_ref, da_ref):
    prod = (a_ref[...].astype(f32) * da_ref[...].astype(f32)).T
    return [jnp.sum(prod[64 * h : 64 * h + 64], axis=0, keepdims=True) for h in range(2)]


def self_backward_body(
    piece_ref,
    q_ref,
    k_ref,
    v_ref,
    t8_ref,
    a_ref,
    da_ref,
    lse_ref,
    dq_ref,
    dk_ref,
    dv_ref,
    diag_ref,
    table,
    spans,
    dk_sum,
    dv_sum,
):
    width = 256
    delta = head_deltas(a_ref, da_ref)
    kt = transposed(k_ref[...])
    spread_bias(t8_ref, table)
    for h in range(2):
        spans[h][...] = jnp.zeros(spans[h].shape, f32)
    dk_sum[...] = jnp.zeros_like(dk_sum)
    dv_sum[...] = jnp.zeros_like(dv_sum)
    for group in tasks_of(width, 2):
        qb = group[0][0]
        base = qb * width
        ext = extent(qb, width)
        ok = allowed_rows(piece_ref, base, ext - base, width)
        q = q_ref[pl.ds(base, width), :]
        da = da_ref[pl.ds(base, width), :]
        scored = [
            biased_scores(k_ref, head_of(q, h), table, h, base, width, ext, ok) for _, h in group
        ]
        dprobs = [dot(v_ref[:ext, :], head_of(da, h), NT) for _, h in group]
        low = []
        for h in range(2):
            p = jnp.exp(scored[h] - lse_ref[0, h : h + 1, pl.ds(base, width)])
            ds = p * (dprobs[h] - delta[h][:, base : base + width])
            for g in range(ext // 128):
                spans[h][:, pl.ds(base - 128 * g + 512, width)] += ds[128 * g : 128 * g + 128]
            low.append((p.astype(bf16), ds.astype(bf16)))
        dks = [dot(ds, q, NN) for _, ds in low]
        dvs = [dot(p, da, NN) for p, _ in low]
        dqs = [dot(kt[64 * h : 64 * h + 64, :ext], low[h][1], NN) for h in range(2)]
        lane = lax.broadcasted_iota(jnp.int32, (ext, 128), 1)
        dk_sum[:ext] += jnp.where(lane < 64, dks[0], dks[1])
        dv_sum[:ext] += jnp.where(lane < 64, dvs[0], dvs[1])
        dq_ref[pl.ds(base, width), :] = jnp.concatenate(dqs, axis=0).T.astype(bf16)
    dk_ref[...] = dk_sum[...].astype(bf16)
    dv_ref[...] = dv_sum[...].astype(bf16)
    for h in range(2):
        total = spans[h][0:8, :]
        for m in range(1, 16):
            total = total + pltpu.roll(spans[h][8 * m : 8 * m + 8, :], SPAN - 8 * m, 1)
        diag_ref[h] = total


def cross_forward_body(q_ref, k_ref, v_ref, o_ref, lse_ref):
    width = 256
    vt = transposed(v_ref[...])
    outs = {}
    for group in tasks_of(width, 8):
        scored = [
            dot(k_ref[...], head_of(q_ref[pl.ds(qb * width, width), :], h), NT) for qb, h in group
        ]
        weights = [softmax_cols(s) for s in scored]
        for (qb, h), (p, total, m) in zip(group, weights):
            outs[(qb, h)] = dot(vt[64 * h : 64 * h + 64, :], p, NN) * (1.0 / total)
            lse_ref[0, h : h + 1, pl.ds(qb * width, width)] = m + jnp.log(total)
            if h == 1:
                o_ref[pl.ds(qb * width, width), :] = (
                    jnp.concatenate([outs[(qb, 0)], outs[(qb, 1)]], axis=0).T.astype(bf16)
                )


def cross_backward_body(q_ref, k_ref, v_ref, a_ref, da_ref, lse_ref, dq_ref, dk_ref, dv_ref):
    width = 256
    delta = head_deltas(a_ref, da_ref)
    kt = transposed(k_ref[...])
    lane = lax.broadcasted_iota(jnp.int32, (LE, 128), 1)
    outs = {}
    dks = [None, None]
    dvs = [None, None]
    for group in tasks_of(width, 4):
        scored = [
            dot(k_ref[...], head_of(q_ref[pl.ds(qb * width, width), :], h), NT) for qb, h in group
        ]
        dprobs = [
            dot(v_ref[...], head_of(da_ref[pl.ds(qb * width, width), :], h), NT) for qb, h in group
        ]
        low = []
        for (qb, h), s, dp in zip(group, scored, dprobs):
            p = jnp.exp(s - lse_ref[0, h : h + 1, pl.ds(qb * width, width)])
            ds = p * (dp - delta[h][:, qb * width : (qb + 1) * width])
            low.append((p.astype(bf16), ds.astype(bf16)))
        for (qb, h), (p, ds) in zip(group, low):
            dk = dot(ds, q_ref[pl.ds(qb * width, width), :], NN)
            dv = dot(p, da_ref[pl.ds(qb * width, width), :], NN)
            dks[h] = dk if dks[h] is None else dks[h] + dk
            dvs[h] = dv if dvs[h] is None else dvs[h] + dv
            outs[(qb, h)] = dot(kt[64 * h : 64 * h + 64, :], ds, NN)
            if h == 1:
                dq_ref[pl.ds(qb * width, width), :] = (
                    jnp.concatenate([outs[(qb, 0)], outs[(qb, 1)]], axis=0).T.astype(bf16)
                )
    dk_ref[...] = jnp.where(lane < 64, dks[0], dks[1]).astype(bf16)
    dv_ref[...] = jnp.where(lane < 64, dvs[0], dvs[1]).astype(bf16)


def place():
    dp = lax.axis_index("dp")
    return (dp, dp % QUAD, lax.axis_index("row"), lax.axis_index("col"))


def quad_mate(dp, quarter, flip):
    return dp - quarter + (quarter ^ flip)


def greet_all(dp, quarter, row, col):
    barrier = pltpu.get_barrier_semaphore()
    for s in range(1, ROWS):
        pl.semaphore_signal(
            barrier, inc=1, device_id=(dp, (row + s) % ROWS, col), device_id_type=MESH
        )
    for k in range(1, QUAD):
        pl.semaphore_signal(
            barrier, inc=1, device_id=(quad_mate(dp, quarter, k), row, col), device_id_type=MESH
        )
    pl.semaphore_signal(barrier, inc=1, device_id=(dp, row, 1 - col), device_id_type=MESH)
    pl.semaphore_wait(barrier, ROWS + QUAD - 1)


def rms_of(v):
    return lax.rsqrt(jnp.sum(v * v, axis=-1, keepdims=True) * (1.0 / D) + EPSILON)


def norm_back_rows(v, r, gain, dn):
    inner = jnp.sum(dn * gain * v, axis=-1, keepdims=True)
    dv = dn * gain * r - v * (r * r * r) * (inner * (1.0 / D))
    return (dv, jnp.sum(dn * v * r, axis=0, keepdims=True))


class Gathering:
    AHEAD = 3

    def __init__(self, sources, wholes, swaps, rel_pair, sems):
        self.wholes = wholes
        self.dp, self.quarter, self.row, self.col = place()
        self.partner = (self.dp, self.row, 1 - self.col)
        (
            self.z_send,
            self.z_recv,
            self.q_send,
            self.q_recv,
            self.c_send,
            self.c_recv,
            own_sem,
            s_send,
            s_recv,
            s_own,
        ) = sems
        self.started = {}
        self.along = {}
        row, col = self.row, self.col
        self.own = []
        for i, parts in enumerate(sources):
            self.own.append([])
            for n, (src, to) in enumerate(parts):
                copy = pltpu.make_async_copy(
                    src,
                    wholes[i].at[col, self.own_rows(), pl.ds(to, src.shape[1])],
                    own_sem.at[i, n],
                )
                copy.start()
                self.own[i].append(copy)
        self.swap_own = []
        for j, (src, own, dst) in enumerate(swaps):
            copy = pltpu.make_async_copy(src if own is None else src.at[own], dst.at[col], s_own.at[j])
            copy.start()
            self.swap_own.append(copy)

        def rel_at(r):
            return rel_pair[1].at[
                pl.ds(pl.multiple_of(r * 8, 8), 8), pl.ds(pl.multiple_of(col * 128, 128), 128)
            ]

        self.rel_at = rel_at
        count = len(swaps)
        self.rel_own = pltpu.make_async_copy(rel_pair[0], rel_at(row), s_own.at[count])
        self.rel_own.start()
        greet_all(self.dp, self.quarter, row, col)
        self.swap = []
        for j, (src, own, dst) in enumerate(swaps):
            self.swap.append(
                self.remote(
                    src if own is None else src.at[1 - own],
                    dst.at[col],
                    s_send.at[j],
                    s_recv.at[j],
                    self.partner,
                )
            )
        self.rel_sems = (s_send, s_recv, count)
        self.rel_copies = [
            self.remote(
                rel_pair[0],
                rel_at(row),
                s_send.at[count + s],
                s_recv.at[count + s],
                self.partner if s == 0 else (self.dp, (row + s) % ROWS, col),
            )
            for s in range(ROWS)
        ]
        self.q_copies = {}
        self.from_partner = {}
        for i in range(self.AHEAD):
            self.offer(i)

    def own_rows(self):
        return pl.ds(pl.multiple_of(self.row * BLOCK, BLOCK), BLOCK)

    def remote(self, src, dst, send_sem, recv_sem, device, i=-1):
        copy = pltpu.make_async_remote_copy(
            src_ref=src,
            dst_ref=dst,
            send_sem=send_sem,
            recv_sem=recv_sem,
            device_id=device,
            device_id_type=MESH,
        )
        copy.start()
        self.started.setdefault(i, []).append(copy)
        return copy

    def part(self, i, r, q):
        at = pl.multiple_of(r * BLOCK + q * PIECE, PIECE)
        return self.wholes[i].at[self.col, pl.ds(at, PIECE)]

    def offer(self, i):
        for copy in self.own[i]:
            copy.wait()
        row = self.row
        self.along_z(i, row, 0, 2, (row + 2) % ROWS)
        self.along_z(i, row, 1, 1, row + 1, row < ROWS - 1)
        self.along_z(i, row, 2, 3, row - 1, row > 0)
        whole_block = self.wholes[i].at[self.col, self.own_rows()]
        self.from_partner[(i, 0, 0)] = self.remote(
            whole_block,
            whole_block,
            self.c_send.at[i, 0, 0],
            self.c_recv.at[i, 0, 0],
            self.partner,
            i,
        )

    def along_z(self, i, r, slot, far, to, when=None):
        def copy():
            ref = self.part(i, r, self.quarter)
            return pltpu.make_async_remote_copy(
                src_ref=ref,
                dst_ref=ref,
                send_sem=self.z_send.at[i, slot],
                recv_sem=self.z_recv.at[i, far - 1],
                device_id=(self.dp, to, self.col),
                device_id_type=MESH,
            )

        if when is None:
            copy().start()
        else:
            pl.when(when)(lambda: copy().start())
        self.along.setdefault(i, []).append((copy, when))

    def swapped(self, j):
        self.swap_own[j].wait()
        self.swap[j].wait_recv()

    def rel_onward(self):
        s_send, s_recv, base = self.rel_sems
        for s in range(1, ROWS):
            self.rel_copies[s].wait_recv()
            ref = self.rel_at((self.row - s + ROWS) % ROWS)
            slot = base + ROWS - 1 + s
            self.rel_copies.append(
                self.remote(ref, ref, s_send.at[slot], s_recv.at[slot], self.partner)
            )

    def rel_arrived(self):
        self.rel_own.wait()
        self.rel_copies[0].wait_recv()
        for copy in self.rel_copies[ROWS:]:
            copy.wait_recv()

    def hand_over(self, i, s, k, r):
        ref = self.part(i, r, self.quarter ^ k)
        self.from_partner[(i, s, k)] = self.remote(
            ref, ref, self.c_send.at[i, s, k], self.c_recv.at[i, s, k], self.partner, i
        )

    def to_mate(self, i, s, k, slot, ref):
        self.q_copies[(i, s, slot)] = self.remote(
            ref,
            ref,
            self.q_send.at[i, s - 1, slot - 1],
            self.q_recv.at[i, s - 1, slot - 1],
            (quad_mate(self.dp, self.quarter, k), self.row, self.col),
            i,
        )

    def far(self, n):
        low, inner, high = ((3, 1, 1), (2, 3, 2), (1, 2, 3))[n - 1]
        return jnp.where(self.row == 0, low, jnp.where(self.row == ROWS - 1, high, inner))

    def spread(self, i):
        row = self.row
        for n in range(1, ROWS):
            far = self.far(n)
            r = (row - far + ROWS) % ROWS
            ref = self.part(i, r, self.quarter)
            pltpu.make_async_remote_copy(
                src_ref=ref,
                dst_ref=ref,
                send_sem=self.z_send.at[i, 0],
                recv_sem=self.z_recv.at[i, far - 1],
                device_id=self.partner,
                device_id_type=MESH,
            ).wait_recv()
            if n == 3:
                inner = (row == 1) | (row == 2)
                self.along_z(
                    i, r, 3, jnp.where(row == 1, 1, 3), jnp.where(row == 1, 0, 3), inner
                )
            for k in (1, 2):
                self.to_mate(i, n, k, k, ref)
            self.hand_over(i, n, 0, r)
        if i + self.AHEAD < len(self.wholes):
            self.offer(i + self.AHEAD)

    def share(self, i):
        for s in range(1, ROWS):
            r = (self.row - self.far(s) + ROWS) % ROWS
            onward = 1 + (i + s) % 2
            for k in (onward, 3 - onward):
                self.q_copies[(i, s, k)].wait_recv()
                if k == onward:
                    self.to_mate(i, s, 3 - k, 3, self.part(i, r, self.quarter ^ k))
                self.hand_over(i, s, k, r)

    def close(self, i):
        for s in range(1, ROWS):
            self.q_copies[(i, s, 3)].wait_recv()
            self.hand_over(i, s, 3, (self.row - self.far(s) + ROWS) % ROWS)

    def arrived(self, i):
        for s in range(ROWS):
            for k in range(QUAD if s else 1):
                self.from_partner[(i, s, k)].wait_recv()

    def sent(self, i):
        for copy in self.started.pop(i, ()):
            copy.wait_send()
        for copy, when in self.along.pop(i, ()):
            if when is None:
                copy().wait_send()
            else:
                pl.when(when)(lambda copy=copy: copy().wait_send())

    def finish(self):
        for i in sorted({*self.started, *self.along}):
            self.sent(i)


WIDTHS = (3 * HALF, HALF, HALF, 2 * HALF, HALF, 2048, 1024)


def forward_body(*refs):
    hidden_in, encoded, cotangent = refs[:3]
    (s_q, s_k, s_v, s_o, x_q, x_k, x_v, x_o, f_g, f_u, f_d) = refs[3:14]
    gain_in, rel_in, onehot_ref, piece_ref = refs[14:18]
    outs = refs[18:36]
    output, gu_grad, down_grad, gain_sums = refs[36:40]
    refs = refs[40:]
    wholes = refs[: len(WIDTHS)]
    refs = refs[len(WIDTHS) :]
    rel_all, gains, rows_in, enc, cot, qkv, a1, h1, q2, kv2, a2, h2, t8 = refs[:13]
    lse1, lse2, table, dgu_all, save_sem, out_sem, stage_sem = refs[13:20]
    col = lax.axis_index("col")
    sources = (
        [(w.at[:, pl.ds(128 * j, 128)], 128 * (3 * j + n)) for n, w in enumerate((s_q, s_k, s_v)) for j in range(3)],
        [(s_o, 0)],
        [(x_q, 0)],
        [(x_k, 0), (x_v, HALF)],
        [(x_o, 0)],
        [(f_g, 0), (f_u, 1024)],
        [(f_d, 0)],
    )
    comm = Gathering(
        sources,
        wholes,
        (
            (hidden_in, col, rows_in),
            (gain_in, None, gains),
            (encoded, col, enc),
            (cotangent, col, cot),
        ),
        (rel_in, rel_all),
        refs[20:30],
    )
    saving = {}

    def save(slot, src):
        copy = pltpu.make_async_copy(src, outs[slot], save_sem.at[slot])
        copy.start()
        saving[slot] = copy

    def weight(i):
        comm.arrived(i)
        save(9 + i, wholes[i])

    comm.rel_onward()
    comm.spread(0)
    comm.spread(1)
    comm.swapped(0)
    save(14, rows_in)
    comm.swapped(1)
    save(16, gains)
    g_self, g_cross, g_ffn, g_final = [
        jnp.concatenate([gains[0, n : n + 1, :], gains[1, n : n + 1, :]], axis=1) for n in range(4)
    ]
    comm.share(0)
    comm.spread(2)
    step = 256
    blocks_of = [slice(step * b, step * (b + 1)) for b in range(L // step)]
    comm.rel_arrived()
    rel16 = jnp.concatenate([rel_all[:, :6], rel_all[:, 128:134]], axis=1).astype(bf16)
    bias = dot(rel16, onehot_ref[...], TN)
    for n in range(8):
        moved = pltpu.roll(bias, n, 1) if n else bias
        for h in range(12):
            t8[h, n : n + 1, :] = moved[h : h + 1]
    save(0, t8)
    comm.share(1)
    comm.close(0)
    comm.share(2)
    weight(0)

    def x_rows(at):
        return jnp.concatenate([rows_in[0, at, :], rows_in[1, at, :]], axis=1).astype(f32)

    def back_dot(a, i):
        wide = wholes[i].shape[2]
        return dot(a[:, :wide], wholes[i][0], NT) + dot(a[:, wide:], wholes[i][1], NT)

    for n, at in enumerate(blocks_of):
        xb = x_rows(at)
        n1 = (xb * rms_of(xb) * g_self).astype(bf16)
        for c in range(2):
            qkv[at, 3 * HALF * c : 3 * HALF * (c + 1)] = dot(n1, wholes[0][c], NN).astype(bf16)
        if n == 0:
            comm.close(1)
        if n == 1:
            comm.spread(3)
        if n == 2:
            comm.close(2)
        if n == 3:
            comm.share(3)
    save(1, qkv)

    def lane(block):
        return pl.ds(pl.multiple_of(block * 128, 128), 128)

    def self_heads(hp, carry):
        base = (hp // 3) * 9 + (hp % 3) * 3
        self_forward_body(
            piece_ref,
            qkv.at[:, lane(base)],
            qkv.at[:, lane(base + 1)],
            qkv.at[:, lane(base + 2)],
            t8.at[pl.ds(2 * hp, 2)],
            a1.at[:, lane(hp)],
            lse1.at[pl.ds(hp, 1)],
            [table.at[0], table.at[1]],
        )
        return carry

    lax.fori_loop(0, 2, self_heads, 0)
    comm.spread(4)
    comm.close(3)
    weight(1)
    weight(2)
    comm.swapped(2)
    save(15, enc)
    comm.swapped(3)
    lax.fori_loop(2, 4, self_heads, 0)
    comm.share(4)
    comm.spread(5)
    weight(3)
    lax.fori_loop(4, 6, self_heads, 0)
    save(2, a1)
    save(3, lse1)
    comm.close(4)
    comm.spread(6)
    weight(4)
    enc_rows = jnp.concatenate([enc[0], enc[1]], axis=1)
    for c in range(2):
        kv2[:, D * c : D * (c + 1)] = dot(enc_rows, wholes[3][c], NN).astype(bf16)
    save(6, kv2)
    for n, at in enumerate(blocks_of):
        h1b = x_rows(at) + back_dot(a1[at, :], 1)
        h1[at, :] = h1b
        n2 = (h1b * rms_of(h1b) * g_cross).astype(bf16)
        for c in range(2):
            q2[at, HALF * c : HALF * (c + 1)] = dot(n2, wholes[2][c], NN).astype(bf16)
    save(4, h1)
    save(5, q2)

    def cross_heads(hp, carry):
        base = (hp // 3) * 6 + hp % 3
        cross_forward_body(
            q2.at[:, lane(hp)],
            kv2.at[:, lane(base)],
            kv2.at[:, lane(base + 3)],
            a2.at[:, lane(hp)],
            lse2.at[pl.ds(hp, 1)],
        )
        return carry

    comm.share(5)
    lax.fori_loop(0, 2, cross_heads, 0)
    comm.share(6)
    lax.fori_loop(2, 6, cross_heads, 0)
    save(7, a2)
    save(8, lse2)
    comm.close(5)
    for at in blocks_of:
        h2[at, :] = h1[at, :] + back_dot(a2[at, :], 4)
    for i in range(5):
        comm.sent(i)
    for copy in saving.values():
        copy.wait()
    comm.arrived(5)

    n3t = wholes[0].at[0, :, pl.ds(0, L)]
    e3t = wholes[0].at[1, :, pl.ds(0, L)]
    w_gu, w_down = wholes[5], wholes[6]

    def gate_rows(b, carry):
        here = pl.ds(pl.multiple_of(b * step, step), step)
        h2b = h2[here, :]
        n3 = (h2b * rms_of(h2b) * g_ffn).astype(bf16)
        n3t[:, here] = transposed(n3)
        for c in range(4):
            at = (c % 2) * 512
            to = (c // 2) * 2048 + at
            gate = dot(n3, w_gu[c // 2, :, at : at + 512], NN)
            up = dot(n3, w_gu[c // 2, :, at + 1024 : at + 1536], NN)
            act, slope = gelu_parts(gate)
            qkv[here, 512 * c : 512 * (c + 1)] = (act * up).astype(bf16)
            dgu_all[here, to : to + 512] = (up * slope).astype(bf16)
            dgu_all[here, to + 1024 : to + 1536] = act.astype(bf16)
        return carry

    lax.fori_loop(0, 2, gate_rows, 0)
    comm.close(6)
    lax.fori_loop(2, 4, gate_rows, 0)
    comm.arrived(6)

    def ffn_rows(b, carry):
        dg_ffn, dg_final = carry
        here = pl.ds(pl.multiple_of(b * step, step), step)
        h2b = h2[here, :]
        h3 = h2b + back_dot(qkv[here, :2048], 6)
        r4 = rms_of(h3)
        a1[here, :] = (h3 * r4 * g_final).astype(bf16)
        seen = jnp.concatenate([cot[0, here, :], cot[1, here, :]], axis=1).astype(f32)
        dh3, more_final = norm_back_rows(h3, r4, g_final, seen)
        e3 = dh3.astype(bf16)
        e3t[:, here] = transposed(e3)
        for c in range(4):
            low = 512 * (c % 2)
            at = (c // 2) * 2048 + low
            dmid = dot(e3, w_down[c // 2, :, low : low + 512], NN).astype(bf16).astype(f32)
            for to in (at, at + 1024):
                factor = dgu_all[here, to : to + 512].astype(f32)
                dgu_all[here, to : to + 512] = (dmid * factor).astype(bf16)
        dn3 = back_dot(dgu_all[here, :], 5)
        back, more_ffn = norm_back_rows(h2b, rms_of(h2b), g_ffn, dn3)
        h2[here, :] = dh3 + back
        return (dg_ffn + more_ffn, dg_final + more_final)

    zero = jnp.zeros((1, D), f32)
    dg_ffn, dg_final = lax.fori_loop(0, L // step, ffn_rows, (zero, zero))

    def half_of(c):
        return pl.ds(pl.multiple_of(c * HALF, 128), HALF)

    leaving = comm.remote(
        a1.at[:, half_of(1 - col)], output.at[col], out_sem.at[0], out_sem.at[1], comm.partner
    )
    staying = pltpu.make_async_copy(a1.at[:, half_of(col)], output.at[col], out_sem.at[2])
    staying.start()
    dh2_out = pltpu.make_async_copy(h2, outs[-1], out_sem.at[3])
    dh2_out.start()
    gain_sums[...] = jnp.zeros_like(gain_sums)
    gain_sums[2:3, :] = dg_ffn
    gain_sums[3:4, :] = dg_final
    staged = {}

    def stage(n, value, dst):
        slot = n % 2
        if slot in staged:
            staged[slot].wait()
        buffer = wholes[3].at[slot, :, pl.ds(0, 512)]
        buffer[...] = value.astype(bf16)
        staged[slot] = pltpu.make_async_copy(buffer, dst, stage_sem.at[slot])
        staged[slot].start()

    for c in range(8):
        low = slice(512 * (c % 4), 512 * (c % 4 + 1))
        stage(
            c,
            dot(n3t[...], dgu_all[:, 512 * c : 512 * (c + 1)], NN),
            gu_grad.at[c // 4, :, low],
        )
    for c in range(4):
        low = slice(512 * (c % 2), 512 * (c % 2 + 1))
        stage(
            c, dot(e3t[...], qkv[:, 512 * c : 512 * (c + 1)], NN), down_grad.at[c // 2, :, low]
        )
    for copy in staged.values():
        copy.wait()
    staying.wait()
    dh2_out.wait()
    leaving.wait_recv()
    comm.finish()


def forward(args, onehot, piece, number):
    shape = jax.ShapeDtypeStruct
    saved = [
        shape((12, 8, SPAN), f32),
        shape((L, 3 * D), bf16),
        shape((L, D), bf16),
        shape((6, 2, L), f32),
        shape((L, D), f32),
        shape((L, D), bf16),
        shape((LE, 2 * D), bf16),
        shape((L, D), bf16),
        shape((6, 2, L), f32),
    ]
    saved += [shape((2, D, w), bf16) for w in WIDTHS[:5]]
    saved += [shape((2, L, HALF), bf16), shape((2, LE, HALF), bf16), shape((2, 8, HALF), f32)]
    outs = [
        shape((2, L, HALF), bf16),
        shape((2, D, 2048), bf16),
        shape((2, D, 1024), bf16),
        shape((8, D), f32),
    ]
    dma = pltpu.SemaphoreType.DMA
    any_spec = pl.BlockSpec(memory_space=pl.ANY)
    vmem = pl.BlockSpec(memory_space=pltpu.VMEM)
    count = len(WIDTHS)
    scratch = [pltpu.VMEM((2, D, w), bf16) for w in WIDTHS]
    scratch += [
        pltpu.VMEM((BUCKETS, 256), f32),
        pltpu.VMEM((2, 8, HALF), f32),
        pltpu.VMEM((2, L, HALF), bf16),
        pltpu.VMEM((2, LE, HALF), bf16),
        pltpu.VMEM((2, L, HALF), bf16),
        pltpu.VMEM((L, 3 * D), bf16),
        pltpu.VMEM((L, D), bf16),
        pltpu.VMEM((L, D), f32),
        pltpu.VMEM((L, D), bf16),
        pltpu.VMEM((LE, 2 * D), bf16),
        pltpu.VMEM((L, D), bf16),
        pltpu.VMEM((L, D), f32),
        pltpu.VMEM((12, 8, SPAN), f32),
        pltpu.VMEM((6, 2, L), f32),
        pltpu.VMEM((6, 2, L), f32),
        pltpu.VMEM((2, 128, SPAN), f32),
        pltpu.VMEM((L, 4096), bf16),
        dma((17,)),
        dma((4,)),
        dma((2,)),
        dma((count, ROWS)),
        dma((count, ROWS - 1)),
        dma((count, ROWS - 1, QUAD - 1)),
        dma((count, ROWS - 1, QUAD - 1)),
        dma((count, ROWS, QUAD)),
        dma((count, ROWS, QUAD)),
        dma((count, 9)),
        dma((11,)),
        dma((11,)),
        dma((5,)),
    ]
    return pl.pallas_call(
        forward_body,
        out_shape=saved + [shape((L, D), f32)] + outs,
        in_specs=[any_spec] * 16 + [vmem, pl.BlockSpec(memory_space=pltpu.SMEM)],
        out_specs=[any_spec] * (len(saved) + 4) + [vmem],
        scratch_shapes=scratch,
        compiler_params=pltpu.CompilerParams(
            collective_id=number, has_side_effects=True, vmem_limit_bytes=VMEM_LIMIT
        ),
        name="forward",
    )(*args, onehot, piece)


class Summing:
    def __init__(self, widths, pair, first, second, third, final, outs, sems):
        self.widths = widths
        self.pair, self.first, self.second, self.third = pair, first, second, third
        self.final, self.outs = final, outs
        self.sends, self.recvs, self.local_sem = sems
        self.dp, self.quarter, self.row, self.col = place()
        self.partner = (self.dp, self.row, 1 - self.col)
        self.begun = []
        self.pending = {}
        self.kept = []
        greet_all(self.dp, self.quarter, self.row, self.col)

    def remote(self, src, dst, send_sem, recv_sem, device):
        copy = pltpu.make_async_remote_copy(
            src_ref=src,
            dst_ref=dst,
            send_sem=send_sem,
            recv_sem=recv_sem,
            device_id=device,
            device_id_type=MESH,
        )
        copy.start()
        self.begun.append(copy)
        return copy

    def send(self, i, slot, src, dst, device):
        self.pending[(i, slot)] = self.remote(
            src, dst, self.sends.at[i, slot], self.recvs.at[i, slot], device
        )

    def mate(self, k):
        return (quad_mate(self.dp, self.quarter, k), self.row, self.col)

    def offer(self, i, src):
        self.send(i, 0, src, self.pair[i], self.partner)

    def z_first1(self, i, own):
        self.pending[(i, 0)].wait_recv()
        pair = self.pair[i]
        for r in range(ROWS):
            pair[r] = pair[r] + own(r)
        for s in range(1, ROWS):
            to = (self.row + s) % ROWS
            self.send(i, 6 + s, pair.at[to], self.third[i].at[s - 1], (self.dp, to, self.col))

    def z_first2(self, i):
        for s in range(1, ROWS):
            self.pending[(i, 6 + s)].wait_recv()
        block = self.pair[i].at[self.row]
        third = self.third[i]
        for q in range(QUAD):
            total = block[q].astype(f32)
            for s in range(1, ROWS):
                total = total + third[s - 1, q].astype(f32)
            block[q] = total.astype(bf16)
        wide = self.widths[i] // 2
        for h in range(2):
            k = 1 + h
            for j, q in enumerate((self.quarter ^ k, self.quarter ^ 3)):
                self.send(
                    i,
                    1 + 2 * h + j,
                    block.at[q, :, pl.ds(wide * h, wide)],
                    self.first[i].at[h, j],
                    self.mate(k),
                )

    def z_first3(self, i):
        block, first = self.pair[i].at[self.row], self.first[i]
        wide = self.widths[i] // 2
        for h in range(2):
            k = 1 + h
            for j in range(2):
                self.pending[(i, 1 + 2 * h + j)].wait_recv()
            span = pl.ds(wide * h, wide)
            first[h, 1] = first[h, 1] + block[self.quarter ^ 3 ^ k, :, span]
            self.send(i, 5 + h, first.at[h, 1], self.second[i].at[h], self.mate(3 ^ k))
            first[h, 0] = first[h, 0] + block[self.quarter, :, span]

    def z_first4(self, i):
        wide = self.widths[i] // 2
        for h in range(2):
            self.pending[(i, 5 + h)].wait_recv()
            self.final[i][:, wide * h : wide * (h + 1)] = self.second[i][h] + self.first[i][h, 0]
        self.give_back(i)

    def stage1(self, i, own):
        if i in Z_FIRST:
            return self.z_first1(i, own)
        self.pending[(i, 0)].wait_recv()
        pair = self.pair[i]
        for r in range(ROWS):
            pair[r] = pair[r] + own(r)
            if r % 2 == 1:
                k = 1 if r == 1 else 2
                for j, q in enumerate((self.quarter ^ k, self.quarter ^ 3)):
                    self.send(
                        i,
                        r + j,
                        pair.at[pl.ds(r - 1, 2), q],
                        self.first[i].at[pl.ds(r - 1, 2), j],
                        self.mate(k),
                    )

    def stage2(self, i):
        if i in Z_FIRST:
            return self.z_first2(i)
        first, pair = self.first[i], self.pair[i]
        for h in range(2):
            k = 1 if h == 0 else 2
            self.pending[(i, 1 + 2 * h)].wait_recv()
            self.pending[(i, 2 + 2 * h)].wait_recv()
            for r in (2 * h, 2 * h + 1):
                first[r, 1] = first[r, 1] + pair[r, self.quarter ^ 3 ^ k]
            self.send(
                i,
                5 + h,
                first.at[pl.ds(2 * h, 2), 1],
                self.second[i].at[pl.ds(2 * h, 2)],
                self.mate(3 ^ k),
            )
            for r in (2 * h, 2 * h + 1):
                first[r, 0] = first[r, 0] + pair[r, self.quarter]

    def stage3(self, i):
        if i in Z_FIRST:
            return self.z_first3(i)
        second = self.second[i]
        for h in range(2):
            self.pending[(i, 5 + h)].wait_recv()
            for r in (2 * h, 2 * h + 1):
                second[r] = second[r] + self.first[i][r, 0]
        for s in range(1, ROWS):
            to = (self.row + s) % ROWS
            self.send(i, 6 + s, second.at[to], self.third[i].at[s - 1], (self.dp, to, self.col))

    def stage4(self, i):
        if i in Z_FIRST:
            return self.z_first4(i)
        for s in range(1, ROWS):
            self.pending[(i, 6 + s)].wait_recv()
        total = self.second[i][self.row].astype(f32)
        for s in range(1, ROWS):
            total = total + self.third[i][s - 1].astype(f32)
        self.final[i][...] = total.astype(bf16)
        self.give_back(i)

    def give_back(self, i):
        there = self.outs[i].at[self.quarter]
        for k in (1, 2):
            self.send(i, 9 + k, self.final[i], there, self.mate(k))
        copy = pltpu.make_async_copy(self.final[i], there, self.local_sem.at[i])
        copy.start()
        self.kept.append(copy)

    def stage5(self, i):
        onward = 1 + i % 2
        for k in (onward, 3 - onward):
            self.pending[(i, 9 + k)].wait_recv()
            if k == onward:
                ref = self.outs[i].at[self.quarter ^ k]
                self.send(i, 12, ref, ref, self.mate(3 - k))

    def finish(self):
        for i in range(len(self.widths)):
            self.pending[(i, 12)].wait_recv()
        for copy in self.kept:
            copy.wait()
        for copy in self.begun:
            copy.wait_send()


CHUNKS = (1024, 1024, 1024, HALF, HALF, 2 * HALF, HALF, HALF, HALF, HALF)
(F0, F1, F2, CO, CQ, CKV, SO, QA, QB, QC) = range(10)
Z_FIRST = (F0,)
SMALL = (16, 896)


def backward_body(*refs):
    (
        dh2_in,
        g_gu,
        g_down,
        t8_in,
        qkv_in,
        a1_in,
        lse1_in,
        h1_in,
        q2_in,
        kv2_in,
        a2_in,
        lse2_in,
        x_in,
        enc_in,
        w_qkv_in,
        w_out_in,
        w_cq_in,
        w_ckv_in,
        w_co_in,
        gains,
        ffn_gains,
        onehot_ref,
        piece_ref,
    ) = refs[:23]
    count = len(CHUNKS)
    hidden_grad, enc_grad = refs[23:25]
    sums = refs[25 : 25 + count]
    small_out = refs[25 + count]
    refs = refs[26 + count :]
    pair = refs[:count]
    first = refs[count : 2 * count]
    second = refs[2 * count : 3 * count]
    third = refs[3 * count : 4 * count]
    final = refs[4 * count : 5 * count]
    refs = refs[5 * count :]
    gr_co, gr_cq, gr_ckv, gr_out, gr_qkv = refs[:5]
    total, turned, mixed, dmixed, w_big, w_cq, w_out, enc, rows, qkv, t8, lse1, lse2, x = refs[5:19]
    dk_sum, dv_sum, diag, spans_all, eg, small = refs[19:25]
    load_sem, ex_send, ex_recv, ex_local, small_send, small_recv = refs[25:31]
    comm = Summing(CHUNKS, pair, first, second, third, final, sums, refs[31:34])
    col, row, partner = comm.col, comm.row, comm.partner

    def load(slot, *pairs):
        copies = []
        for n, (src, dst) in enumerate(pairs):
            copies.append(pltpu.make_async_copy(src, dst, load_sem.at[slot, n]))
            copies[-1].start()
        return copies

    def wait(copies):
        for copy in copies:
            copy.wait()

    def halves(src, dst, offset=0):
        wide = src.shape[2]
        return [
            (src.at[c], dst.at[:, offset + c * wide : offset + (c + 1) * wide]) for c in range(2)
        ]

    def own_ffn(i):
        src = (g_gu, g_gu, g_down)[i]
        lanes_of = pl.ds(1024 if i == 1 else 0, 1024)
        slot = i % 2
        return load(
            12 + i,
            *[
                (
                    src.at[col, r, :, :, lanes_of],
                    gr_qkv.at[slot * 4 + r, :, :, pl.ds(0, 1024)],
                )
                for r in range(ROWS)
            ],
        )

    comm.offer(F0, g_gu.at[1 - col, :, :, :, pl.ds(0, 1024)])
    comm.offer(F1, g_gu.at[1 - col, :, :, :, pl.ds(1024, 1024)])
    comm.offer(F2, g_down.at[1 - col])
    l_total = load(1, (dh2_in, total))
    l_co = load(2, *halves(w_co_in, w_big, 2 * D))
    l_a2 = load(3, (a2_in, mixed))
    l_own = [own_ffn(0), own_ffn(1)]
    l_q2 = load(4, (q2_in, qkv.at[:, :D]), (kv2_in, qkv.at[:LE, D:]), (lse2_in, lse2))
    l_h1 = load(
        5, *[(h1_in.at[pl.ds(512 * n, 512)], rows.at[:, D * n : D * (n + 1)]) for n in range(2)]
    )
    l_ckv = load(6, *halves(w_ckv_in, w_big))
    l_cq = load(7, *halves(w_cq_in, w_cq))
    l_enc = load(8, *halves(enc_in, enc))
    l_out = load(9, *halves(w_out_in, w_out))
    l_x = load(10, *halves(x_in, x))
    l_t8 = load(11, (t8_in, t8), (lse1_in, lse1))

    step = 256
    blocks_of = [slice(step * b, step * (b + 1)) for b in range(L // step)]
    g_self = jnp.concatenate([gains[0, 0:1, :], gains[1, 0:1, :]], axis=1)
    g_cross = jnp.concatenate([gains[0, 1:2, :], gains[1, 1:2, :]], axis=1)

    def lane(block):
        if isinstance(block, int):
            return pl.ds(block * 128, 128)
        return pl.ds(pl.multiple_of(block * 128, 128), 128)

    def put(dst, value):
        dst[...] = value.astype(bf16).reshape(dst.shape)

    def own_of(ref):
        return lambda r: ref[col, r]

    def own_loaded(i):
        slot = i % 2
        return lambda r: gr_qkv[slot * 4 + r, :, :, pl.ds(0, 1024)]

    wait(l_total)
    for at in blocks_of:
        turned[:, at] = transposed(total[at, :])
    wait(l_co)
    for at in blocks_of:
        dmixed[at, :] = dot(total[at, :].astype(bf16), w_big[:, 2 * D :], NN).astype(bf16)
    wait(l_a2)
    for c in range(2):
        put(gr_co.at[c], dot(turned[...], mixed[:, HALF * c : HALF * (c + 1)], NN))
    comm.offer(CO, gr_co.at[1 - col])
    wait(l_own[0])
    comm.stage1(F0, own_loaded(0))
    wait(l_q2)

    def cross_heads(hp, carry):
        base = 6 + (hp // 3) * 6 + hp % 3
        queries = qkv.at[:, lane(hp)]
        keys = qkv.at[pl.ds(0, LE), lane(base)]
        values = qkv.at[pl.ds(0, LE), lane(base + 3)]
        cross_backward_body(
            queries,
            keys,
            values,
            mixed.at[:, lane(hp)],
            dmixed.at[:, lane(hp)],
            lse2.at[pl.ds(hp, 1)],
            queries,
            keys,
            values,
        )
        return carry

    lax.fori_loop(0, 2, cross_heads, 0)
    wait(l_own[1])
    comm.stage1(F1, own_loaded(1))
    l_own.append(own_ffn(2))
    lax.fori_loop(2, 4, cross_heads, 0)
    wait(l_own[2])
    comm.stage1(F2, own_loaded(2))
    comm.stage1(CO, own_of(gr_co))
    lax.fori_loop(4, 6, cross_heads, 0)
    l_a1 = load(3, (a1_in, mixed))
    comm.stage2(F1)
    wait(l_h1)

    def h1_rows(b):
        return rows[256 * (b % 2) : 256 * (b % 2 + 1), D * (b // 2) : D * (b // 2 + 1)]

    for b, at in enumerate(blocks_of):
        h1b = h1_rows(b)
        turned[:, at] = transposed((h1b * rms_of(h1b) * g_cross).astype(bf16))
    for c in range(2):
        put(gr_cq.at[c], dot(turned[...], qkv[:, HALF * c : HALF * (c + 1)], NN))
    comm.offer(CQ, gr_cq.at[1 - col])
    wait(l_enc)
    enct = transposed(enc[...])
    for c in range(2):
        put(gr_ckv.at[c], dot(enct, qkv[:LE, D + D * c : D + D * (c + 1)], NN))
    comm.offer(CKV, gr_ckv.at[1 - col])
    comm.stage2(F2)
    wait(l_ckv)
    back = dot(qkv[:LE, D:], w_big[:, : 2 * D], NT)
    eg[0] = back[:, :HALF]
    eg[1] = back[:, HALF:]
    ex_eg = comm.remote(eg.at[1 - col], enc_grad.at[col], ex_send.at[1], ex_recv.at[1], partner)
    keep_eg = pltpu.make_async_copy(eg.at[col], enc_grad.at[col], ex_local.at[1])
    keep_eg.start()
    l_qkv = load(2, *halves(w_qkv_in, w_big))
    wait(l_cq)
    wait(l_out)
    comm.stage2(CO)
    dg_cross = jnp.zeros((1, D), f32)
    for b, at in enumerate(blocks_of):
        h1b = h1_rows(b)
        dn2 = dot(qkv[at, :D], w_cq[...], NT)
        dv, dg = norm_back_rows(h1b, rms_of(h1b), g_cross, dn2)
        dg_cross = dg_cross + dg
        dh1 = total[at, :] + dv
        total[at, :] = dh1
        e1 = dh1.astype(bf16)
        turned[:, at] = transposed(e1)
        dmixed[at, :] = dot(e1, w_out[...], NN).astype(bf16)
        if b == 1:
            comm.stage3(F1)
            comm.stage1(CQ, own_of(gr_cq))
    l_q1 = load(4, (qkv_in, qkv))
    comm.stage1(CKV, own_of(gr_ckv))
    wait(l_a1)
    for c in range(2):
        put(gr_out.at[c], dot(turned[...], mixed[:, HALF * c : HALF * (c + 1)], NN))
    comm.offer(SO, gr_out.at[1 - col])
    comm.stage3(F2)
    comm.stage3(CO)
    wait(l_x)
    for at in blocks_of:
        xb = x[at, :].astype(f32)
        turned[:, at] = transposed((xb * rms_of(xb) * g_self).astype(bf16))
    wait(l_t8)
    wait(l_q1)
    table = [rows.at[pl.ds(128 * h, 128)] for h in range(2)]
    spans = [rows.at[pl.ds(256 + 128 * h, 128)] for h in range(2)]
    spans_all[...] = jnp.zeros_like(spans_all)

    def self_heads(hp):
        base = 9 * (hp // 3) + 3 * (hp % 3)
        queries, keys, values = [qkv.at[:, lane(base + n)] for n in range(3)]
        self_backward_body(
            piece_ref,
            queries,
            keys,
            values,
            t8.at[pl.ds(2 * hp, 2)],
            mixed.at[:, lane(hp)],
            dmixed.at[:, lane(hp)],
            lse1.at[pl.ds(hp, 1)],
            queries,
            keys,
            values,
            diag,
            table,
            spans,
            dk_sum,
            dv_sum,
        )
        for h in range(2):
            lined = diag[h, 0:1, :]
            for n in range(1, 8):
                lined = lined + pltpu.roll(diag[h, n : n + 1, :], SPAN - n, 1)
            spans_all[pl.ds(2 * hp + h, 1), :] = lined

    def qkv_grad(j, c):
        return gr_qkv.at[pl.ds(4 * c, 4), :, :, pl.ds(HALF * j, HALF)]

    def grads_of(j):
        for c in range(2):
            at = 3 * HALF * c + HALF * j
            put(qkv_grad(j, c), dot(turned[...], qkv[:, at : at + HALF], NN))
        comm.offer(QA + j, qkv_grad(j, 1 - col))

    def own_qkv(j):
        return lambda r: gr_qkv[4 * col + r, :, :, pl.ds(HALF * j, HALF)]

    self_heads(0)
    comm.stage1(SO, own_of(gr_out))
    comm.stage2(CQ)
    comm.stage2(F0)
    self_heads(3)
    comm.stage2(CKV)
    comm.stage4(F1)
    grads_of(0)
    self_heads(1)
    comm.stage1(QA, own_qkv(0))
    comm.stage2(SO)
    comm.stage3(CQ)
    comm.stage3(CKV)
    comm.stage4(F2)
    comm.stage4(CO)
    comm.stage3(F0)
    self_heads(4)
    comm.stage2(QA)
    comm.stage3(SO)
    comm.stage4(CQ)
    comm.stage5(F1)
    comm.stage4(F0)
    grads_of(1)
    self_heads(2)
    comm.stage1(QB, own_qkv(1))
    comm.stage3(QA)
    comm.stage4(CKV)
    comm.stage5(F2)
    comm.stage5(CO)
    self_heads(5)
    comm.stage2(QB)
    comm.stage4(QA)
    comm.stage4(SO)
    comm.stage5(CQ)
    comm.stage5(CKV)
    comm.stage5(F0)
    grads_of(2)
    comm.stage3(QB)

    wait(l_qkv)
    left = spans_all[...]
    rel = jnp.zeros((16, BUCKETS), f32)
    for _ in range(3):
        high = left.astype(bf16)
        rel = rel + dot(high, onehot_ref[...], NT)
        left = left - high.astype(f32)
    dg_self = jnp.zeros((1, D), f32)
    leaving = []

    def half_of(c):
        return pl.ds(pl.multiple_of(c * HALF, 128), HALF)

    for b, at in enumerate(blocks_of):
        xb = x[at, :].astype(f32)
        dn1 = dot(qkv[at, :], w_big[...], NT)
        dv, dg = norm_back_rows(xb, rms_of(xb), g_self, dn1)
        dg_self = dg_self + dg
        total[at, :] = total[at, :] + dv
        leaving.append(
            comm.remote(
                total.at[at, half_of(1 - col)],
                hidden_grad.at[col, at],
                ex_send.at[2 + b],
                ex_recv.at[2 + b],
                partner,
            )
        )
        kept = pltpu.make_async_copy(
            total.at[at, half_of(col)], hidden_grad.at[col, at], ex_local.at[2 + b]
        )
        kept.start()
        comm.kept.append(kept)
        if b == 0:
            comm.stage1(QC, own_qkv(2))
            comm.stage5(QA)
        if b == 1:
            comm.stage4(QB)
        if b == 2:
            comm.stage2(QC)
            comm.stage5(SO)

    small[0] = jnp.zeros(SMALL, f32)
    small[0, 0:1, :D] = dg_self
    small[0, 1:2, :D] = dg_cross
    small[0, 2:4, :D] = ffn_gains[2:4, :]
    small[0, :, D : D + BUCKETS] = rel
    passing = {}

    def pass_on(slot, src, dst, device):
        passing[slot] = comm.remote(
            small.at[src], small.at[dst], small_send.at[slot], small_recv.at[slot], device
        )

    pass_on(0, 0, 1, partner)
    comm.stage3(QC)
    passing[0].wait_recv()
    small[2] = small[0] + small[1]
    pass_on(1, 2, 3, comm.mate(1))
    comm.stage5(QB)
    passing[1].wait_recv()
    small[4] = small[2] + small[3]
    pass_on(2, 4, 5, comm.mate(2))
    comm.stage4(QC)
    passing[2].wait_recv()
    small[6 + row] = small[4] + small[5]
    for s in range(1, ROWS):
        pass_on(2 + s, 6 + row, 6 + row, (comm.dp, (row + s) % ROWS, col))
    comm.stage5(QC)
    for s in range(1, ROWS):
        passing[2 + s].wait_recv()
    small_out[...] = (small[6] + small[7]) + (small[8] + small[9])
    keep_eg.wait()
    ex_eg.wait_recv()
    for copy in leaving:
        copy.wait_recv()
    comm.finish()


def backward(args, onehot, piece, number):
    shape = jax.ShapeDtypeStruct
    dma = pltpu.SemaphoreType.DMA
    any_spec = pl.BlockSpec(memory_space=pl.ANY)
    vmem = pl.BlockSpec(memory_space=pltpu.VMEM)
    count = len(CHUNKS)
    quarters = (ROWS, QUAD, PIECE)
    scratch = [pltpu.VMEM(quarters + (w,), bf16) for w in CHUNKS]
    for normal, z_first in (
        (lambda w: (ROWS, 2, PIECE, w), lambda w: (2, 2, PIECE, w // 2)),
        (lambda w: (ROWS, PIECE, w), lambda w: (2, PIECE, w // 2)),
        (lambda w: (ROWS - 1, PIECE, w), lambda w: (ROWS - 1, QUAD, PIECE, w)),
    ):
        scratch += [
            pltpu.VMEM((z_first if i in Z_FIRST else normal)(w), bf16)
            for i, w in enumerate(CHUNKS)
        ]
    scratch += [pltpu.VMEM((PIECE, w), bf16) for w in CHUNKS]
    scratch += [
        pltpu.VMEM((2,) + quarters + (HALF,), bf16),
        pltpu.VMEM((2,) + quarters + (HALF,), bf16),
        pltpu.VMEM((2,) + quarters + (2 * HALF,), bf16),
        pltpu.VMEM((2,) + quarters + (HALF,), bf16),
        pltpu.VMEM((2 * ROWS, QUAD, PIECE, 3 * HALF), bf16),
        pltpu.VMEM((L, D), f32),
        pltpu.VMEM((D, L), bf16),
        pltpu.VMEM((L, D), bf16),
        pltpu.VMEM((L, D), bf16),
        pltpu.VMEM((D, 3 * D), bf16),
        pltpu.VMEM((D, D), bf16),
        pltpu.VMEM((D, D), bf16),
        pltpu.VMEM((LE, D), bf16),
        pltpu.VMEM((L // 2, 2 * D), f32),
        pltpu.VMEM((L, 3 * D), bf16),
        pltpu.VMEM((12, 8, SPAN), f32),
        pltpu.VMEM((6, 2, L), f32),
        pltpu.VMEM((6, 2, L), f32),
        pltpu.VMEM((L, D), bf16),
        pltpu.VMEM((L, 128), f32),
        pltpu.VMEM((L, 128), f32),
        pltpu.VMEM((2, 8, SPAN), f32),
        pltpu.VMEM((16, SPAN), f32),
        pltpu.VMEM((2, LE, HALF), f32),
        pltpu.VMEM((6 + ROWS,) + SMALL, f32),
        dma((15, 4)),
        dma((6,)),
        dma((6,)),
        dma((6,)),
        dma((6,)),
        dma((6,)),
        dma((count, 13)),
        dma((count, 13)),
        dma((count,)),
    ]
    out = pl.pallas_call(
        backward_body,
        out_shape=[
            shape((2, L, HALF), f32),
            shape((2, LE, HALF), f32),
        ]
        + [shape((QUAD, PIECE, w), bf16) for w in CHUNKS]
        + [shape(SMALL, f32)],
        in_specs=[any_spec] * 19
        + [vmem] * 3
        + [pl.BlockSpec(memory_space=pltpu.SMEM)],
        out_specs=[any_spec] * (2 + count) + [vmem],
        scratch_shapes=scratch,
        compiler_params=pltpu.CompilerParams(
            collective_id=number, has_side_effects=True, vmem_limit_bytes=VMEM_LIMIT
        ),
        name="backward",
    )(*args, onehot, piece)
    return (out[:2], [o.reshape(BLOCK, o.shape[2]) for o in out[2:-1]], out[-1])


def gelu_parts(t):
    inner = ROOT_TWO_PI * (t + 0.044715 * t * t * t)
    th = jnp.tanh(inner)
    value = 0.5 * t * (1.0 + th)
    slope = 0.5 * (1.0 + th) + 0.5 * t * (1.0 - th * th) * ROOT_TWO_PI * (
        1.0 + 3.0 * 0.044715 * t * t
    )
    return (value, slope)


def body(
    quads,
    hidden_in,
    encoded,
    cotangent,
    piece_start,
    image_piece_lengths,
    bucket_table,
    self_query,
    self_key,
    self_value,
    self_out,
    rel_weight,
    cross_query,
    cross_key,
    cross_value,
    cross_out,
    ffn_gate,
    ffn_up,
    ffn_down,
    gain_self,
    gain_cross,
    gain_ffn,
    gain_final,
):
    col = lax.axis_index("col")
    row = lax.axis_index("row")
    gain_block = jnp.stack([gain_self, gain_cross, gain_ffn, gain_final])
    gain_block = jnp.concatenate([gain_block, jnp.zeros_like(gain_block)])
    rel_block = jnp.pad(rel_weight.astype(f32), ((0, 0), (0, 122)))
    turned_table = bucket_table[:SPAN][::-1]
    onehot = (turned_table[None, :] == jnp.arange(BUCKETS, dtype=jnp.int32)[:, None]).astype(bf16)
    starts = lax.dynamic_index_in_dim(piece_start, col, 0, keepdims=False)
    lengths = lax.dynamic_index_in_dim(image_piece_lengths, col, 0, keepdims=False)
    piece = jnp.concatenate([starts, starts + lengths])
    out = forward(
        (
            hidden_in,
            encoded,
            cotangent,
            self_query,
            self_key,
            self_value,
            self_out.T,
            cross_query,
            cross_key,
            cross_value,
            cross_out.T,
            ffn_gate,
            ffn_up,
            ffn_down.T,
            gain_block,
            rel_block,
        ),
        onehot,
        piece,
        0,
    )
    t8, qkv, a1, lse1, h1, q2, kv2, a2, lse2 = out[:9]
    x, enc, gains, dh2, output, gr_gu, gr_down, ffn_gains = out[14:]
    cut = (2, ROWS, QUAD, PIECE)
    (hidden_grad, enc_grad), grads, small = backward(
        (
            dh2,
            gr_gu.reshape(cut + (2048,)),
            gr_down.reshape(cut + (1024,)),
            t8,
            qkv,
            a1,
            lse1,
            h1,
            q2,
            kv2,
            a2,
            lse2,
            x,
            enc,
            *out[9:14],
            gains,
            ffn_gains,
        ),
        onehot,
        piece,
        1,
    )
    if quads > 1:
        grads, small = jax.tree.map(
            lambda t: lax.psum(t, "dp") * jnp.asarray(1.0 / QUAD, t.dtype), (grads, small)
        )
    grads = [g.astype(f32) for g in grads]
    gr_gate, gr_up, gr_down, gr_co, gr_cq, gr_ckv, gr_out = grads[:7]
    gr_q, gr_k, gr_v = [
        jnp.concatenate([g[:, 128 * n : 128 * (n + 1)] for g in grads[7:]], axis=1)
        for n in range(3)
    ]
    gain_sums = lax.dynamic_slice_in_dim(small[:4], col * HALF, HALF, 1)
    gr_rel = lax.dynamic_slice(small, (col * 6, D + row * 8), (6, 8)).T
    return (
        output,
        hidden_grad,
        enc_grad,
        gr_q,
        gr_k,
        gr_v,
        gr_out.T,
        gr_rel,
        gr_cq,
        gr_ckv[:, :HALF],
        gr_ckv[:, HALF:],
        gr_co.T,
        gr_gate,
        gr_up,
        gr_down.T,
        gain_sums[0],
        gain_sums[1],
        gain_sums[2],
        gain_sums[3],
    )


def solution(mesh):
    batch = P(("dp", "row"), None, "col")
    inward = P("row", "col")
    outward = P("col", "row")
    gain = P("col")
    weights = (
        (inward,) * 3 + (outward, inward) + (inward,) * 3 + (outward,) + (inward,) * 2 + (outward,)
    )
    placed = (batch,) * 3 + (P(("dp", "row"), None),) * 2 + (P(),) + weights + (gain,) * 4
    return jax.shard_map(
        lambda *args: body(mesh.shape["dp"] // QUAD, *args),
        mesh=mesh,
        in_specs=placed,
        out_specs=(batch,) * 3 + weights + (gain,) * 4,
        check_vma=False,
    )
```

```python
import math

import jax
import jax.numpy as jnp
from jax import lax
from jax.experimental import pallas as pl
from jax.experimental.pallas import tpu as pltpu
from jax.sharding import PartitionSpec as P

D = 768
HALF = 384
L = 1024
LE = 256
BUCKETS = 32
SPAN = 1536
EPSILON = 1e-06
MASKED = -1e30
ROOT_TWO_PI = math.sqrt(2.0 / math.pi)
MESH = pl.DeviceIdType.MESH
ROWS = 4
QUAD = 4
BLOCK = D // ROWS
PIECE = BLOCK // QUAD
f32 = jnp.float32
bf16 = jnp.bfloat16
NT = (((1,), (1,)), ((), ()))
NN = (((1,), (0,)), ((), ()))
TN = (((0,), (0,)), ((), ()))
VMEM_LIMIT = 60 * 2**20


def dot(a, b, dims):
    return lax.dot_general(a, b, dims, preferred_element_type=f32)


def head_of(x, h):
    lane = lax.broadcasted_iota(jnp.int32, x.shape, 1)
    return jnp.where((lane >= 64 * h) & (lane < 64 * h + 64), x, jnp.zeros_like(x))


def transposed(x):
    return x.astype(f32).T.astype(bf16)


def spread_bias(t8_ref, table):
    for h in range(2):
        t = t8_ref[h]
        for m in range(16):
            table[h][8 * m : 8 * m + 8, :] = pltpu.roll(t, 8 * m, 1)


def allowed_rows(piece_ref, base, rows, width):
    s0 = piece_ref[0]
    s1 = piece_ref[1]
    e0 = piece_ref[2]
    e1 = piece_ref[3]
    c = lax.broadcasted_iota(jnp.int32, (1, width), 1) + base
    last = jnp.where(
        (c >= s0) & (c < e0), e0 - 1, jnp.where((c >= s1) & (c < e1), e1 - 1, 0)
    )
    last = jnp.maximum(c, last)
    return lax.broadcasted_iota(jnp.int32, (rows, width), 0) + base <= last


def extent(qb, width):
    return 512 * ((qb * width) // 512 + 1)


def biased_scores(k_ref, q_head, table, h, base, width, ext, ok):
    s = dot(k_ref[:ext, :], q_head, NT)
    bias = jnp.concatenate(
        [table[h][:, pl.ds(base - 128 * g + 512, width)] for g in range(ext // 128)], axis=0
    )
    s = s + bias
    tail = jnp.where(ok, s[base:], MASKED)
    return tail if base == 0 else jnp.concatenate([s[:base], tail], axis=0)


def softmax_cols(s):
    m = jnp.max(s, axis=0, keepdims=True)
    p = jnp.exp(s - m)
    total = jnp.sum(p, axis=0, keepdims=True)
    return (p.astype(bf16), total, m)


def tasks_of(width, group):
    tasks = [(qb, h) for qb in range(L // width) for h in range(2)]
    return [tasks[i : i + group] for i in range(0, len(tasks), group)]


def self_forward_body(piece_ref, q_ref, k_ref, v_ref, t8_ref, o_ref, lse_ref, table):
    width = 256
    vt = transposed(v_ref[...])
    spread_bias(t8_ref, table)
    oks = [
        allowed_rows(piece_ref, qb * width, extent(qb, width) - qb * width, width)
        for qb in range(L // width)
    ]
    outs = {}
    for group in tasks_of(width, 8):
        scored = [
            biased_scores(
                k_ref,
                head_of(q_ref[pl.ds(qb * width, width), :], h),
                table,
                h,
                qb * width,
                width,
                extent(qb, width),
                oks[qb],
            )
            for qb, h in group
        ]
        weights = [softmax_cols(s) for s in scored]
        for (qb, h), (p, total, m) in zip(group, weights):
            mixed = dot(vt[64 * h : 64 * h + 64, : extent(qb, width)], p, NN)
            outs[(qb, h)] = mixed * (1.0 / total)
            lse_ref[0, h : h + 1, pl.ds(qb * width, width)] = m + jnp.log(total)
            if h == 1:
                o_ref[pl.ds(qb * width, width), :] = (
                    jnp.concatenate([outs[(qb, 0)], outs[(qb, 1)]], axis=0).T.astype(bf16)
                )


def head_deltas(a_ref, da_ref):
    prod = (a_ref[...].astype(f32) * da_ref[...].astype(f32)).T
    return [jnp.sum(prod[64 * h : 64 * h + 64], axis=0, keepdims=True) for h in range(2)]


def self_backward_body(
    piece_ref,
    q_ref,
    k_ref,
    v_ref,
    t8_ref,
    a_ref,
    da_ref,
    lse_ref,
    dq_ref,
    dk_ref,
    dv_ref,
    diag_ref,
    table,
    spans,
    dk_sum,
    dv_sum,
):
    width = 256
    delta = head_deltas(a_ref, da_ref)
    kt = transposed(k_ref[...])
    spread_bias(t8_ref, table)
    for h in range(2):
        spans[h][...] = jnp.zeros(spans[h].shape, f32)
    dk_sum[...] = jnp.zeros_like(dk_sum)
    dv_sum[...] = jnp.zeros_like(dv_sum)
    for group in tasks_of(width, 2):
        qb = group[0][0]
        base = qb * width
        ext = extent(qb, width)
        ok = allowed_rows(piece_ref, base, ext - base, width)
        q = q_ref[pl.ds(base, width), :]
        da = da_ref[pl.ds(base, width), :]
        scored = [
            biased_scores(k_ref, head_of(q, h), table, h, base, width, ext, ok) for _, h in group
        ]
        dprobs = [dot(v_ref[:ext, :], head_of(da, h), NT) for _, h in group]
        low = []
        for h in range(2):
            p = jnp.exp(scored[h] - lse_ref[0, h : h + 1, pl.ds(base, width)])
            ds = p * (dprobs[h] - delta[h][:, base : base + width])
            for g in range(ext // 128):
                spans[h][:, pl.ds(base - 128 * g + 512, width)] += ds[128 * g : 128 * g + 128]
            low.append((p.astype(bf16), ds.astype(bf16)))
        dks = [dot(ds, q, NN) for _, ds in low]
        dvs = [dot(p, da, NN) for p, _ in low]
        dqs = [dot(kt[64 * h : 64 * h + 64, :ext], low[h][1], NN) for h in range(2)]
        lane = lax.broadcasted_iota(jnp.int32, (ext, 128), 1)
        dk_sum[:ext] += jnp.where(lane < 64, dks[0], dks[1])
        dv_sum[:ext] += jnp.where(lane < 64, dvs[0], dvs[1])
        dq_ref[pl.ds(base, width), :] = jnp.concatenate(dqs, axis=0).T.astype(bf16)
    dk_ref[...] = dk_sum[...].astype(bf16)
    dv_ref[...] = dv_sum[...].astype(bf16)
    for h in range(2):
        total = spans[h][0:8, :]
        for m in range(1, 16):
            total = total + pltpu.roll(spans[h][8 * m : 8 * m + 8, :], SPAN - 8 * m, 1)
        diag_ref[h] = total


def cross_forward_body(q_ref, k_ref, v_ref, o_ref, lse_ref):
    width = 256
    vt = transposed(v_ref[...])
    outs = {}
    for group in tasks_of(width, 8):
        scored = [
            dot(k_ref[...], head_of(q_ref[pl.ds(qb * width, width), :], h), NT) for qb, h in group
        ]
        weights = [softmax_cols(s) for s in scored]
        for (qb, h), (p, total, m) in zip(group, weights):
            outs[(qb, h)] = dot(vt[64 * h : 64 * h + 64, :], p, NN) * (1.0 / total)
            lse_ref[0, h : h + 1, pl.ds(qb * width, width)] = m + jnp.log(total)
            if h == 1:
                o_ref[pl.ds(qb * width, width), :] = (
                    jnp.concatenate([outs[(qb, 0)], outs[(qb, 1)]], axis=0).T.astype(bf16)
                )


def cross_backward_body(q_ref, k_ref, v_ref, a_ref, da_ref, lse_ref, dq_ref, dk_ref, dv_ref):
    width = 256
    delta = head_deltas(a_ref, da_ref)
    kt = transposed(k_ref[...])
    lane = lax.broadcasted_iota(jnp.int32, (LE, 128), 1)
    outs = {}
    dks = [None, None]
    dvs = [None, None]
    for group in tasks_of(width, 4):
        scored = [
            dot(k_ref[...], head_of(q_ref[pl.ds(qb * width, width), :], h), NT) for qb, h in group
        ]
        dprobs = [
            dot(v_ref[...], head_of(da_ref[pl.ds(qb * width, width), :], h), NT) for qb, h in group
        ]
        low = []
        for (qb, h), s, dp in zip(group, scored, dprobs):
            p = jnp.exp(s - lse_ref[0, h : h + 1, pl.ds(qb * width, width)])
            ds = p * (dp - delta[h][:, qb * width : (qb + 1) * width])
            low.append((p.astype(bf16), ds.astype(bf16)))
        for (qb, h), (p, ds) in zip(group, low):
            dk = dot(ds, q_ref[pl.ds(qb * width, width), :], NN)
            dv = dot(p, da_ref[pl.ds(qb * width, width), :], NN)
            dks[h] = dk if dks[h] is None else dks[h] + dk
            dvs[h] = dv if dvs[h] is None else dvs[h] + dv
            outs[(qb, h)] = dot(kt[64 * h : 64 * h + 64, :], ds, NN)
            if h == 1:
                dq_ref[pl.ds(qb * width, width), :] = (
                    jnp.concatenate([outs[(qb, 0)], outs[(qb, 1)]], axis=0).T.astype(bf16)
                )
    dk_ref[...] = jnp.where(lane < 64, dks[0], dks[1]).astype(bf16)
    dv_ref[...] = jnp.where(lane < 64, dvs[0], dvs[1]).astype(bf16)


def place():
    dp = lax.axis_index("dp")
    return (dp, dp % QUAD, lax.axis_index("row"), lax.axis_index("col"))


def quad_mate(dp, quarter, flip):
    return dp - quarter + (quarter ^ flip)


def greet_all(dp, quarter, row, col):
    barrier = pltpu.get_barrier_semaphore()
    for s in range(1, ROWS):
        pl.semaphore_signal(
            barrier, inc=1, device_id=(dp, (row + s) % ROWS, col), device_id_type=MESH
        )
    for k in range(1, QUAD):
        pl.semaphore_signal(
            barrier, inc=1, device_id=(quad_mate(dp, quarter, k), row, col), device_id_type=MESH
        )
    pl.semaphore_signal(barrier, inc=1, device_id=(dp, row, 1 - col), device_id_type=MESH)
    pl.semaphore_wait(barrier, ROWS + QUAD - 1)


def rms_of(v):
    return lax.rsqrt(jnp.sum(v * v, axis=-1, keepdims=True) * (1.0 / D) + EPSILON)


def norm_back_rows(v, r, gain, dn):
    inner = jnp.sum(dn * gain * v, axis=-1, keepdims=True)
    dv = dn * gain * r - v * (r * r * r) * (inner * (1.0 / D))
    return (dv, jnp.sum(dn * v * r, axis=0, keepdims=True))


class Gathering:
    AHEAD = 5

    def __init__(self, sources, wholes, swaps, rel_pair, sems):
        self.wholes = wholes
        self.items = ITEMS
        self.dp, self.quarter, self.row, self.col = place()
        self.partner = (self.dp, self.row, 1 - self.col)
        (
            self.z_send,
            self.z_recv,
            self.q_send,
            self.q_recv,
            self.c_send,
            self.c_recv,
            own_sem,
            s_send,
            s_recv,
            s_own,
        ) = sems
        self.started = {}
        self.along = {}
        row, col = self.row, self.col
        self.own = []
        for i, parts in enumerate(sources):
            self.own.append([])
            for n, (src, to) in enumerate(parts):
                copy = pltpu.make_async_copy(
                    src,
                    self.lanes_of(i, self.own_rows(), to, src.shape[1]),
                    own_sem.at[i, n],
                )
                copy.start()
                self.own[i].append(copy)
        self.swap_own = []
        for j, (src, own, dst) in enumerate(swaps):
            copy = pltpu.make_async_copy(src if own is None else src.at[own], dst.at[col], s_own.at[j])
            copy.start()
            self.swap_own.append(copy)

        def rel_at(r):
            return rel_pair[1].at[
                pl.ds(pl.multiple_of(r * 8, 8), 8), pl.ds(pl.multiple_of(col * 128, 128), 128)
            ]

        self.rel_at = rel_at
        count = len(swaps)
        self.rel_own = pltpu.make_async_copy(rel_pair[0], rel_at(row), s_own.at[count])
        self.rel_own.start()
        greet_all(self.dp, self.quarter, row, col)
        self.swap = []
        for j, (src, own, dst) in enumerate(swaps):
            self.swap.append(
                self.remote(
                    src if own is None else src.at[1 - own],
                    dst.at[col],
                    s_send.at[j],
                    s_recv.at[j],
                    self.partner,
                )
            )
        self.rel_sems = (s_send, s_recv, count)
        self.rel_copies = [
            self.remote(
                rel_pair[0],
                rel_at(row),
                s_send.at[count + s],
                s_recv.at[count + s],
                self.partner if s == 0 else (self.dp, (row + s) % ROWS, col),
            )
            for s in range(ROWS)
        ]
        self.q_copies = {}
        self.from_partner = {}
        for i in range(self.AHEAD):
            self.offer(i)

    def lanes_of(self, i, rows, offset=0, width=None):
        array, low, wide = self.items[i]
        return self.wholes[array].at[self.col, rows, pl.ds(low + offset, width or wide)]

    def own_rows(self):
        return pl.ds(pl.multiple_of(self.row * BLOCK, BLOCK), BLOCK)

    def remote(self, src, dst, send_sem, recv_sem, device, i=-1):
        copy = pltpu.make_async_remote_copy(
            src_ref=src,
            dst_ref=dst,
            send_sem=send_sem,
            recv_sem=recv_sem,
            device_id=device,
            device_id_type=MESH,
        )
        copy.start()
        self.started.setdefault(i, []).append(copy)
        return copy

    def part(self, i, r, q):
        at = pl.multiple_of(r * BLOCK + q * PIECE, PIECE)
        return self.lanes_of(i, pl.ds(at, PIECE))

    def offer(self, i):
        for copy in self.own[i]:
            copy.wait()
        row = self.row
        self.along_z(i, row, 0, 2, (row + 2) % ROWS)
        self.along_z(i, row, 1, 1, row + 1, row < ROWS - 1)
        self.along_z(i, row, 2, 3, row - 1, row > 0)
        whole_block = self.lanes_of(i, self.own_rows())
        self.from_partner[(i, 0, 0)] = self.remote(
            whole_block,
            whole_block,
            self.c_send.at[i, 0, 0],
            self.c_recv.at[i, 0, 0],
            self.partner,
            i,
        )

    def along_z(self, i, r, slot, far, to, when=None):
        def copy():
            ref = self.part(i, r, self.quarter)
            return pltpu.make_async_remote_copy(
                src_ref=ref,
                dst_ref=ref,
                send_sem=self.z_send.at[i, slot],
                recv_sem=self.z_recv.at[i, far - 1],
                device_id=(self.dp, to, self.col),
                device_id_type=MESH,
            )

        if when is None:
            copy().start()
        else:
            pl.when(when)(lambda: copy().start())
        self.along.setdefault(i, []).append((copy, when))

    def swapped(self, j):
        self.swap_own[j].wait()
        self.swap[j].wait_recv()

    def rel_onward(self):
        s_send, s_recv, base = self.rel_sems
        for s in range(1, ROWS):
            self.rel_copies[s].wait_recv()
            ref = self.rel_at((self.row - s + ROWS) % ROWS)
            slot = base + ROWS - 1 + s
            self.rel_copies.append(
                self.remote(ref, ref, s_send.at[slot], s_recv.at[slot], self.partner)
            )

    def rel_arrived(self):
        self.rel_own.wait()
        self.rel_copies[0].wait_recv()
        for copy in self.rel_copies[ROWS:]:
            copy.wait_recv()

    def hand_over(self, i, s, k, r):
        ref = self.part(i, r, self.quarter ^ k)
        self.from_partner[(i, s, k)] = self.remote(
            ref, ref, self.c_send.at[i, s, k], self.c_recv.at[i, s, k], self.partner, i
        )

    def to_mate(self, i, s, k, slot, ref):
        self.q_copies[(i, s, slot)] = self.remote(
            ref,
            ref,
            self.q_send.at[i, s - 1, slot - 1],
            self.q_recv.at[i, s - 1, slot - 1],
            (quad_mate(self.dp, self.quarter, k), self.row, self.col),
            i,
        )

    def far(self, n):
        low, inner, high = ((3, 1, 1), (2, 3, 2), (1, 2, 3))[n - 1]
        return jnp.where(self.row == 0, low, jnp.where(self.row == ROWS - 1, high, inner))

    def spread(self, i):
        row = self.row
        for n in range(1, ROWS):
            far = self.far(n)
            r = (row - far + ROWS) % ROWS
            ref = self.part(i, r, self.quarter)
            pltpu.make_async_remote_copy(
                src_ref=ref,
                dst_ref=ref,
                send_sem=self.z_send.at[i, 0],
                recv_sem=self.z_recv.at[i, far - 1],
                device_id=self.partner,
                device_id_type=MESH,
            ).wait_recv()
            if n == 3:
                inner = (row == 1) | (row == 2)
                self.along_z(
                    i, r, 3, jnp.where(row == 1, 1, 3), jnp.where(row == 1, 0, 3), inner
                )
            for k in (1, 2):
                self.to_mate(i, n, k, k, ref)
            self.hand_over(i, n, 0, r)
        if i + self.AHEAD < len(self.items):
            self.offer(i + self.AHEAD)

    def share(self, i):
        for s in range(1, ROWS):
            r = (self.row - self.far(s) + ROWS) % ROWS
            onward = 1 + (i + s) % 2
            for k in (onward, 3 - onward):
                self.q_copies[(i, s, k)].wait_recv()
                if k == onward:
                    self.to_mate(i, s, 3 - k, 3, self.part(i, r, self.quarter ^ k))
                self.hand_over(i, s, k, r)

    def close(self, i):
        for s in range(1, ROWS):
            self.q_copies[(i, s, 3)].wait_recv()
            self.hand_over(i, s, 3, (self.row - self.far(s) + ROWS) % ROWS)

    def arrived(self, i):
        for s in range(ROWS):
            for k in range(QUAD if s else 1):
                self.from_partner[(i, s, k)].wait_recv()

    def sent(self, i):
        for copy in self.started.pop(i, ()):
            copy.wait_send()
        for copy, when in self.along.pop(i, ()):
            if when is None:
                copy().wait_send()
            else:
                pl.when(when)(lambda copy=copy: copy().wait_send())

    def finish(self):
        for i in sorted({*self.started, *self.along}):
            self.sent(i)


WIDTHS = (3 * HALF, HALF, HALF, 2 * HALF, HALF, 2048, 1024)
ITEMS = tuple((0, HALF * j, HALF) for j in range(3)) + tuple(
    (i, 0, w) for i, w in enumerate(WIDTHS) if i
)


def forward_body(*refs):
    hidden_in, encoded, cotangent = refs[:3]
    (s_q, s_k, s_v, s_o, x_q, x_k, x_v, x_o, f_g, f_u, f_d) = refs[3:14]
    gain_in, rel_in, onehot_ref, piece_ref = refs[14:18]
    outs = refs[18:36]
    output, gu_grad, down_grad, gain_sums = refs[36:40]
    refs = refs[40:]
    wholes = refs[: len(WIDTHS)]
    refs = refs[len(WIDTHS) :]
    rel_all, gains, rows_in, enc, cot, qkv, a1, h1, q2, kv2, a2, h2, t8 = refs[:13]
    lse1, lse2, table, dgu_all, save_sem, out_sem, stage_sem = refs[13:20]
    col = lax.axis_index("col")
    sources = (
        *[
            [(w.at[:, pl.ds(128 * j, 128)], 128 * n) for n, w in enumerate((s_q, s_k, s_v))]
            for j in range(3)
        ],
        [(s_o, 0)],
        [(x_q, 0)],
        [(x_k, 0), (x_v, HALF)],
        [(x_o, 0)],
        [(f_g, 0), (f_u, 1024)],
        [(f_d, 0)],
    )
    comm = Gathering(
        sources,
        wholes,
        (
            (hidden_in, col, rows_in),
            (gain_in, None, gains),
            (encoded, col, enc),
            (cotangent, col, cot),
        ),
        (rel_in, rel_all),
        refs[20:30],
    )
    saving = {}

    def save(slot, src):
        copy = pltpu.make_async_copy(src, outs[slot], save_sem.at[slot])
        copy.start()
        saving[slot] = copy

    def weight(i):
        for n, item in enumerate(ITEMS):
            if item[0] == i:
                comm.arrived(n)
        save(9 + i, wholes[i])

    comm.spread(0)
    comm.spread(1)
    comm.rel_onward()
    comm.spread(2)
    comm.share(0)
    comm.swapped(0)
    save(14, rows_in)
    comm.swapped(1)
    save(16, gains)
    g_self, g_cross, g_ffn, g_final = [
        jnp.concatenate([gains[0, n : n + 1, :], gains[1, n : n + 1, :]], axis=1) for n in range(4)
    ]
    comm.share(1)
    comm.share(2)
    comm.spread(3)
    step = 256
    blocks_of = [slice(step * b, step * (b + 1)) for b in range(L // step)]
    comm.rel_arrived()
    rel16 = jnp.concatenate([rel_all[:, :6], rel_all[:, 128:134]], axis=1).astype(bf16)
    bias = dot(rel16, onehot_ref[...], TN)
    for n in range(8):
        moved = pltpu.roll(bias, n, 1) if n else bias
        for h in range(12):
            t8[h, n : n + 1, :] = moved[h : h + 1]
    save(0, t8)
    comm.close(0)
    comm.close(1)
    comm.spread(4)
    comm.close(2)
    comm.share(3)
    weight(0)

    def x_rows(at):
        return jnp.concatenate([rows_in[0, at, :], rows_in[1, at, :]], axis=1).astype(f32)

    def back_dot(a, i):
        wide = wholes[i].shape[2]
        return dot(a[:, :wide], wholes[i][0], NT) + dot(a[:, wide:], wholes[i][1], NT)

    for n, at in enumerate(blocks_of):
        xb = x_rows(at)
        n1 = (xb * rms_of(xb) * g_self).astype(bf16)
        for c in range(2):
            qkv[at, 3 * HALF * c : 3 * HALF * (c + 1)] = dot(n1, wholes[0][c], NN).astype(bf16)
        if n == 0:
            comm.close(3)
            comm.share(4)
        if n == 1:
            comm.spread(5)
        if n == 2:
            comm.close(4)
        if n == 3:
            comm.share(5)
    save(1, qkv)

    def lane(block):
        return pl.ds(pl.multiple_of(block * 128, 128), 128)

    def self_heads(hp, carry):
        base = (hp // 3) * 9 + (hp % 3) * 3
        self_forward_body(
            piece_ref,
            qkv.at[:, lane(base)],
            qkv.at[:, lane(base + 1)],
            qkv.at[:, lane(base + 2)],
            t8.at[pl.ds(2 * hp, 2)],
            a1.at[:, lane(hp)],
            lse1.at[pl.ds(hp, 1)],
            [table.at[0], table.at[1]],
        )
        return carry

    lax.fori_loop(0, 2, self_heads, 0)
    comm.spread(6)
    comm.close(5)
    weight(1)
    weight(2)
    comm.swapped(2)
    save(15, enc)
    comm.swapped(3)
    lax.fori_loop(2, 4, self_heads, 0)
    comm.share(6)
    comm.spread(7)
    weight(3)
    lax.fori_loop(4, 6, self_heads, 0)
    save(2, a1)
    save(3, lse1)
    comm.close(6)
    comm.spread(8)
    weight(4)
    enc_rows = jnp.concatenate([enc[0], enc[1]], axis=1)
    for c in range(2):
        kv2[:, D * c : D * (c + 1)] = dot(enc_rows, wholes[3][c], NN).astype(bf16)
    save(6, kv2)
    for n, at in enumerate(blocks_of):
        h1b = x_rows(at) + back_dot(a1[at, :], 1)
        h1[at, :] = h1b
        n2 = (h1b * rms_of(h1b) * g_cross).astype(bf16)
        for c in range(2):
            q2[at, HALF * c : HALF * (c + 1)] = dot(n2, wholes[2][c], NN).astype(bf16)
    save(4, h1)
    save(5, q2)

    def cross_heads(hp, carry):
        base = (hp // 3) * 6 + hp % 3
        cross_forward_body(
            q2.at[:, lane(hp)],
            kv2.at[:, lane(base)],
            kv2.at[:, lane(base + 3)],
            a2.at[:, lane(hp)],
            lse2.at[pl.ds(hp, 1)],
        )
        return carry

    comm.share(7)
    lax.fori_loop(0, 2, cross_heads, 0)
    comm.share(8)
    lax.fori_loop(2, 6, cross_heads, 0)
    save(7, a2)
    save(8, lse2)
    comm.close(7)
    for at in blocks_of:
        h2[at, :] = h1[at, :] + back_dot(a2[at, :], 4)
    for i in range(7):
        comm.sent(i)
    for copy in saving.values():
        copy.wait()
    comm.arrived(7)

    n3t = wholes[0].at[0, :, pl.ds(0, L)]
    e3t = wholes[0].at[1, :, pl.ds(0, L)]
    w_gu, w_down = wholes[5], wholes[6]

    def gate_rows(b, carry):
        here = pl.ds(pl.multiple_of(b * step, step), step)
        h2b = h2[here, :]
        n3 = (h2b * rms_of(h2b) * g_ffn).astype(bf16)
        n3t[:, here] = transposed(n3)
        for c in range(4):
            at = (c % 2) * 512
            to = (c // 2) * 2048 + at
            gate = dot(n3, w_gu[c // 2, :, at : at + 512], NN)
            up = dot(n3, w_gu[c // 2, :, at + 1024 : at + 1536], NN)
            act, slope = gelu_parts(gate)
            qkv[here, 512 * c : 512 * (c + 1)] = (act * up).astype(bf16)
            dgu_all[here, to : to + 512] = (up * slope).astype(bf16)
            dgu_all[here, to + 1024 : to + 1536] = act.astype(bf16)
        return carry

    lax.fori_loop(0, 2, gate_rows, 0)
    comm.close(8)
    lax.fori_loop(2, 4, gate_rows, 0)
    comm.arrived(8)

    def ffn_rows(b, carry):
        dg_ffn, dg_final = carry
        here = pl.ds(pl.multiple_of(b * step, step), step)
        h2b = h2[here, :]
        h3 = h2b + back_dot(qkv[here, :2048], 6)
        r4 = rms_of(h3)
        a1[here, :] = (h3 * r4 * g_final).astype(bf16)
        seen = jnp.concatenate([cot[0, here, :], cot[1, here, :]], axis=1).astype(f32)
        dh3, more_final = norm_back_rows(h3, r4, g_final, seen)
        e3 = dh3.astype(bf16)
        e3t[:, here] = transposed(e3)
        for c in range(4):
            low = 512 * (c % 2)
            at = (c // 2) * 2048 + low
            dmid = dot(e3, w_down[c // 2, :, low : low + 512], NN).astype(bf16).astype(f32)
            for to in (at, at + 1024):
                factor = dgu_all[here, to : to + 512].astype(f32)
                dgu_all[here, to : to + 512] = (dmid * factor).astype(bf16)
        dn3 = back_dot(dgu_all[here, :], 5)
        back, more_ffn = norm_back_rows(h2b, rms_of(h2b), g_ffn, dn3)
        h2[here, :] = dh3 + back
        return (dg_ffn + more_ffn, dg_final + more_final)

    zero = jnp.zeros((1, D), f32)
    dg_ffn, dg_final = lax.fori_loop(0, L // step, ffn_rows, (zero, zero))

    def half_of(c):
        return pl.ds(pl.multiple_of(c * HALF, 128), HALF)

    leaving = comm.remote(
        a1.at[:, half_of(1 - col)], output.at[col], out_sem.at[0], out_sem.at[1], comm.partner
    )
    staying = pltpu.make_async_copy(a1.at[:, half_of(col)], output.at[col], out_sem.at[2])
    staying.start()
    dh2_out = pltpu.make_async_copy(h2, outs[-1], out_sem.at[3])
    dh2_out.start()
    gain_sums[...] = jnp.zeros_like(gain_sums)
    gain_sums[2:3, :] = dg_ffn
    gain_sums[3:4, :] = dg_final
    staged = {}

    def stage(n, value, dst):
        slot = n % 2
        if slot in staged:
            staged[slot].wait()
        buffer = wholes[3].at[slot, :, pl.ds(0, 512)]
        buffer[...] = value.astype(bf16)
        staged[slot] = pltpu.make_async_copy(buffer, dst, stage_sem.at[slot])
        staged[slot].start()

    for c in range(8):
        low = slice(512 * (c % 4), 512 * (c % 4 + 1))
        stage(
            c,
            dot(n3t[...], dgu_all[:, 512 * c : 512 * (c + 1)], NN),
            gu_grad.at[c // 4, :, low],
        )
    for c in range(4):
        low = slice(512 * (c % 2), 512 * (c % 2 + 1))
        stage(
            c, dot(e3t[...], qkv[:, 512 * c : 512 * (c + 1)], NN), down_grad.at[c // 2, :, low]
        )
    for copy in staged.values():
        copy.wait()
    staying.wait()
    dh2_out.wait()
    leaving.wait_recv()
    comm.finish()


def forward(args, onehot, piece, number):
    shape = jax.ShapeDtypeStruct
    saved = [
        shape((12, 8, SPAN), f32),
        shape((L, 3 * D), bf16),
        shape((L, D), bf16),
        shape((6, 2, L), f32),
        shape((L, D), f32),
        shape((L, D), bf16),
        shape((LE, 2 * D), bf16),
        shape((L, D), bf16),
        shape((6, 2, L), f32),
    ]
    saved += [shape((2, D, w), bf16) for w in WIDTHS[:5]]
    saved += [shape((2, L, HALF), bf16), shape((2, LE, HALF), bf16), shape((2, 8, HALF), f32)]
    outs = [
        shape((2, L, HALF), bf16),
        shape((2, D, 2048), bf16),
        shape((2, D, 1024), bf16),
        shape((8, D), f32),
    ]
    dma = pltpu.SemaphoreType.DMA
    any_spec = pl.BlockSpec(memory_space=pl.ANY)
    vmem = pl.BlockSpec(memory_space=pltpu.VMEM)
    count = len(ITEMS)
    scratch = [pltpu.VMEM((2, D, w), bf16) for w in WIDTHS]
    scratch += [
        pltpu.VMEM((BUCKETS, 256), f32),
        pltpu.VMEM((2, 8, HALF), f32),
        pltpu.VMEM((2, L, HALF), bf16),
        pltpu.VMEM((2, LE, HALF), bf16),
        pltpu.VMEM((2, L, HALF), bf16),
        pltpu.VMEM((L, 3 * D), bf16),
        pltpu.VMEM((L, D), bf16),
        pltpu.VMEM((L, D), f32),
        pltpu.VMEM((L, D), bf16),
        pltpu.VMEM((LE, 2 * D), bf16),
        pltpu.VMEM((L, D), bf16),
        pltpu.VMEM((L, D), f32),
        pltpu.VMEM((12, 8, SPAN), f32),
        pltpu.VMEM((6, 2, L), f32),
        pltpu.VMEM((6, 2, L), f32),
        pltpu.VMEM((2, 128, SPAN), f32),
        pltpu.VMEM((L, 4096), bf16),
        dma((17,)),
        dma((4,)),
        dma((2,)),
        dma((count, ROWS)),
        dma((count, ROWS - 1)),
        dma((count, ROWS - 1, QUAD - 1)),
        dma((count, ROWS - 1, QUAD - 1)),
        dma((count, ROWS, QUAD)),
        dma((count, ROWS, QUAD)),
        dma((count, 3)),
        dma((11,)),
        dma((11,)),
        dma((5,)),
    ]
    return pl.pallas_call(
        forward_body,
        out_shape=saved + [shape((L, D), f32)] + outs,
        in_specs=[any_spec] * 16 + [vmem, pl.BlockSpec(memory_space=pltpu.SMEM)],
        out_specs=[any_spec] * (len(saved) + 4) + [vmem],
        scratch_shapes=scratch,
        compiler_params=pltpu.CompilerParams(
            collective_id=number, has_side_effects=True, vmem_limit_bytes=VMEM_LIMIT
        ),
        name="forward",
    )(*args, onehot, piece)


class Summing:
    def __init__(self, widths, pair, first, second, third, final, outs, sems):
        self.widths = widths
        self.pair, self.first, self.second, self.third = pair, first, second, third
        self.final, self.outs = final, outs
        self.sends, self.recvs, self.local_sem = sems
        self.dp, self.quarter, self.row, self.col = place()
        self.partner = (self.dp, self.row, 1 - self.col)
        self.begun = []
        self.pending = {}
        self.kept = []
        greet_all(self.dp, self.quarter, self.row, self.col)

    def remote(self, src, dst, send_sem, recv_sem, device):
        copy = pltpu.make_async_remote_copy(
            src_ref=src,
            dst_ref=dst,
            send_sem=send_sem,
            recv_sem=recv_sem,
            device_id=device,
            device_id_type=MESH,
        )
        copy.start()
        self.begun.append(copy)
        return copy

    def send(self, i, slot, src, dst, device):
        self.pending[(i, slot)] = self.remote(
            src, dst, self.sends.at[i, slot], self.recvs.at[i, slot], device
        )

    def mate(self, k):
        return (quad_mate(self.dp, self.quarter, k), self.row, self.col)

    def offer(self, i, src):
        self.send(i, 0, src, self.pair[i], self.partner)

    def z_first1(self, i, own):
        self.pending[(i, 0)].wait_recv()
        pair = self.pair[i]
        for r in range(ROWS):
            pair[r] = pair[r] + own(r)
        for s in range(1, ROWS):
            to = (self.row + s) % ROWS
            self.send(i, 6 + s, pair.at[to], self.third[i].at[s - 1], (self.dp, to, self.col))

    def z_first2(self, i):
        for s in range(1, ROWS):
            self.pending[(i, 6 + s)].wait_recv()
        block = self.pair[i].at[self.row]
        third = self.third[i]
        for q in range(QUAD):
            total = block[q].astype(f32)
            for s in range(1, ROWS):
                total = total + third[s - 1, q].astype(f32)
            block[q] = total.astype(bf16)
        wide = self.widths[i] // 2
        for h in range(2):
            k = 1 + h
            for j, q in enumerate((self.quarter ^ k, self.quarter ^ 3)):
                self.send(
                    i,
                    1 + 2 * h + j,
                    block.at[q, :, pl.ds(wide * h, wide)],
                    self.first[i].at[h, j],
                    self.mate(k),
                )

    def z_first3(self, i):
        block, first = self.pair[i].at[self.row], self.first[i]
        wide = self.widths[i] // 2
        for h in range(2):
            k = 1 + h
            for j in range(2):
                self.pending[(i, 1 + 2 * h + j)].wait_recv()
            span = pl.ds(wide * h, wide)
            first[h, 1] = first[h, 1] + block[self.quarter ^ 3 ^ k, :, span]
            self.send(i, 5 + h, first.at[h, 1], self.second[i].at[h], self.mate(3 ^ k))
            first[h, 0] = first[h, 0] + block[self.quarter, :, span]

    def z_first4(self, i):
        wide = self.widths[i] // 2
        for h in range(2):
            self.pending[(i, 5 + h)].wait_recv()
            self.final[i][:, wide * h : wide * (h + 1)] = self.second[i][h] + self.first[i][h, 0]
        self.give_back(i)

    def stage1(self, i, own):
        if i in Z_FIRST:
            return self.z_first1(i, own)
        self.pending[(i, 0)].wait_recv()
        pair = self.pair[i]
        for r in range(ROWS):
            pair[r] = pair[r] + own(r)
            if r % 2 == 1:
                k = 1 if r == 1 else 2
                for j, q in enumerate((self.quarter ^ k, self.quarter ^ 3)):
                    self.send(
                        i,
                        r + j,
                        pair.at[pl.ds(r - 1, 2), q],
                        self.first[i].at[pl.ds(r - 1, 2), j],
                        self.mate(k),
                    )

    def stage2(self, i):
        if i in Z_FIRST:
            return self.z_first2(i)
        first, pair = self.first[i], self.pair[i]
        for h in range(2):
            k = 1 if h == 0 else 2
            self.pending[(i, 1 + 2 * h)].wait_recv()
            self.pending[(i, 2 + 2 * h)].wait_recv()
            for r in (2 * h, 2 * h + 1):
                first[r, 1] = first[r, 1] + pair[r, self.quarter ^ 3 ^ k]
            self.send(
                i,
                5 + h,
                first.at[pl.ds(2 * h, 2), 1],
                self.second[i].at[pl.ds(2 * h, 2)],
                self.mate(3 ^ k),
            )
            for r in (2 * h, 2 * h + 1):
                first[r, 0] = first[r, 0] + pair[r, self.quarter]

    def stage3(self, i):
        if i in Z_FIRST:
            return self.z_first3(i)
        second = self.second[i]
        for h in range(2):
            self.pending[(i, 5 + h)].wait_recv()
            for r in (2 * h, 2 * h + 1):
                second[r] = second[r] + self.first[i][r, 0]
        for s in range(1, ROWS):
            to = (self.row + s) % ROWS
            self.send(i, 6 + s, second.at[to], self.third[i].at[s - 1], (self.dp, to, self.col))

    def stage4(self, i):
        if i in Z_FIRST:
            return self.z_first4(i)
        for s in range(1, ROWS):
            self.pending[(i, 6 + s)].wait_recv()
        total = self.second[i][self.row].astype(f32)
        for s in range(1, ROWS):
            total = total + self.third[i][s - 1].astype(f32)
        self.final[i][...] = total.astype(bf16)
        self.give_back(i)

    def give_back(self, i):
        there = self.outs[i].at[self.quarter]
        for k in (1, 2):
            self.send(i, 9 + k, self.final[i], there, self.mate(k))
        copy = pltpu.make_async_copy(self.final[i], there, self.local_sem.at[i])
        copy.start()
        self.kept.append(copy)

    def stage5(self, i):
        onward = 1 + i % 2
        for k in (onward, 3 - onward):
            self.pending[(i, 9 + k)].wait_recv()
            if k == onward:
                ref = self.outs[i].at[self.quarter ^ k]
                self.send(i, 12, ref, ref, self.mate(3 - k))

    def finish(self):
        for i in range(len(self.widths)):
            self.pending[(i, 12)].wait_recv()
        for copy in self.kept:
            copy.wait()
        for copy in self.begun:
            copy.wait_send()


CHUNKS = (1024, 1024, 1024, HALF, HALF, 2 * HALF, HALF, HALF, HALF, HALF)
(F0, F1, F2, CO, CQ, CKV, SO, QA, QB, QC) = range(10)
Z_FIRST = (F0,)
SMALL = (16, 896)


def backward_body(*refs):
    (
        dh2_in,
        g_gu,
        g_down,
        t8_in,
        qkv_in,
        a1_in,
        lse1_in,
        h1_in,
        q2_in,
        kv2_in,
        a2_in,
        lse2_in,
        x_in,
        enc_in,
        w_qkv_in,
        w_out_in,
        w_cq_in,
        w_ckv_in,
        w_co_in,
        gains,
        ffn_gains,
        onehot_ref,
        piece_ref,
    ) = refs[:23]
    count = len(CHUNKS)
    hidden_grad, enc_grad = refs[23:25]
    sums = refs[25 : 25 + count]
    small_out = refs[25 + count]
    refs = refs[26 + count :]
    pair = refs[:count]
    first = refs[count : 2 * count]
    second = refs[2 * count : 3 * count]
    third = refs[3 * count : 4 * count]
    final = refs[4 * count : 5 * count]
    refs = refs[5 * count :]
    gr_co, gr_cq, gr_ckv, gr_out, gr_qkv = refs[:5]
    total, turned, mixed, dmixed, w_big, w_cq, w_out, enc, rows, qkv, t8, lse1, lse2, x = refs[5:19]
    dk_sum, dv_sum, diag, spans_all, eg, small = refs[19:25]
    load_sem, ex_send, ex_recv, ex_local, small_send, small_recv = refs[25:31]
    comm = Summing(CHUNKS, pair, first, second, third, final, sums, refs[31:34])
    col, row, partner = comm.col, comm.row, comm.partner

    def load(slot, *pairs):
        copies = []
        for n, (src, dst) in enumerate(pairs):
            copies.append(pltpu.make_async_copy(src, dst, load_sem.at[slot, n]))
            copies[-1].start()
        return copies

    def wait(copies):
        for copy in copies:
            copy.wait()

    def halves(src, dst, offset=0):
        wide = src.shape[2]
        return [
            (src.at[c], dst.at[:, offset + c * wide : offset + (c + 1) * wide]) for c in range(2)
        ]

    def own_ffn(i):
        src = (g_gu, g_gu, g_down)[i]
        lanes_of = pl.ds(1024 if i == 1 else 0, 1024)
        slot = i % 2
        return load(
            12 + i,
            *[
                (
                    src.at[col, r, :, :, lanes_of],
                    gr_qkv.at[slot * 4 + r, :, :, pl.ds(0, 1024)],
                )
                for r in range(ROWS)
            ],
        )

    comm.offer(F0, g_gu.at[1 - col, :, :, :, pl.ds(0, 1024)])
    comm.offer(F1, g_gu.at[1 - col, :, :, :, pl.ds(1024, 1024)])
    comm.offer(F2, g_down.at[1 - col])
    l_total = load(1, (dh2_in, total))
    l_co = load(2, *halves(w_co_in, w_big, 2 * D))
    l_a2 = load(3, (a2_in, mixed))
    l_own = [own_ffn(0), own_ffn(1)]
    l_q2 = load(4, (q2_in, qkv.at[:, :D]), (kv2_in, qkv.at[:LE, D:]), (lse2_in, lse2))
    l_h1 = load(
        5, *[(h1_in.at[pl.ds(512 * n, 512)], rows.at[:, D * n : D * (n + 1)]) for n in range(2)]
    )
    l_ckv = load(6, *halves(w_ckv_in, w_big))
    l_cq = load(7, *halves(w_cq_in, w_cq))
    l_enc = load(8, *halves(enc_in, enc))
    l_out = load(9, *halves(w_out_in, w_out))
    l_x = load(10, *halves(x_in, x))
    l_t8 = load(11, (t8_in, t8), (lse1_in, lse1))

    step = 256
    blocks_of = [slice(step * b, step * (b + 1)) for b in range(L // step)]
    g_self = jnp.concatenate([gains[0, 0:1, :], gains[1, 0:1, :]], axis=1)
    g_cross = jnp.concatenate([gains[0, 1:2, :], gains[1, 1:2, :]], axis=1)

    def lane(block):
        if isinstance(block, int):
            return pl.ds(block * 128, 128)
        return pl.ds(pl.multiple_of(block * 128, 128), 128)

    def put(dst, value):
        dst[...] = value.astype(bf16).reshape(dst.shape)

    def own_of(ref):
        return lambda r: ref[col, r]

    def own_loaded(i):
        slot = i % 2
        return lambda r: gr_qkv[slot * 4 + r, :, :, pl.ds(0, 1024)]

    wait(l_total)
    for at in blocks_of:
        turned[:, at] = transposed(total[at, :])
    wait(l_co)
    for at in blocks_of:
        dmixed[at, :] = dot(total[at, :].astype(bf16), w_big[:, 2 * D :], NN).astype(bf16)
    wait(l_a2)
    for c in range(2):
        put(gr_co.at[c], dot(turned[...], mixed[:, HALF * c : HALF * (c + 1)], NN))
    comm.offer(CO, gr_co.at[1 - col])
    wait(l_own[0])
    comm.stage1(F0, own_loaded(0))
    wait(l_q2)

    def cross_heads(hp, carry):
        base = 6 + (hp // 3) * 6 + hp % 3
        queries = qkv.at[:, lane(hp)]
        keys = qkv.at[pl.ds(0, LE), lane(base)]
        values = qkv.at[pl.ds(0, LE), lane(base + 3)]
        cross_backward_body(
            queries,
            keys,
            values,
            mixed.at[:, lane(hp)],
            dmixed.at[:, lane(hp)],
            lse2.at[pl.ds(hp, 1)],
            queries,
            keys,
            values,
        )
        return carry

    lax.fori_loop(0, 2, cross_heads, 0)
    wait(l_own[1])
    comm.stage1(F1, own_loaded(1))
    l_own.append(own_ffn(2))
    lax.fori_loop(2, 4, cross_heads, 0)
    wait(l_own[2])
    comm.stage1(F2, own_loaded(2))
    comm.stage1(CO, own_of(gr_co))
    lax.fori_loop(4, 6, cross_heads, 0)
    l_a1 = load(3, (a1_in, mixed))
    comm.stage2(F1)
    wait(l_h1)

    def h1_rows(b):
        return rows[256 * (b % 2) : 256 * (b % 2 + 1), D * (b // 2) : D * (b // 2 + 1)]

    for b, at in enumerate(blocks_of):
        h1b = h1_rows(b)
        turned[:, at] = transposed((h1b * rms_of(h1b) * g_cross).astype(bf16))
    for c in range(2):
        put(gr_cq.at[c], dot(turned[...], qkv[:, HALF * c : HALF * (c + 1)], NN))
    comm.offer(CQ, gr_cq.at[1 - col])
    wait(l_enc)
    enct = transposed(enc[...])
    for c in range(2):
        put(gr_ckv.at[c], dot(enct, qkv[:LE, D + D * c : D + D * (c + 1)], NN))
    comm.offer(CKV, gr_ckv.at[1 - col])
    comm.stage2(F2)
    wait(l_ckv)
    back = dot(qkv[:LE, D:], w_big[:, : 2 * D], NT)
    eg[0] = back[:, :HALF]
    eg[1] = back[:, HALF:]
    ex_eg = comm.remote(eg.at[1 - col], enc_grad.at[col], ex_send.at[1], ex_recv.at[1], partner)
    keep_eg = pltpu.make_async_copy(eg.at[col], enc_grad.at[col], ex_local.at[1])
    keep_eg.start()
    l_qkv = load(2, *halves(w_qkv_in, w_big))
    wait(l_cq)
    wait(l_out)
    comm.stage2(CO)
    dg_cross = jnp.zeros((1, D), f32)
    for b, at in enumerate(blocks_of):
        h1b = h1_rows(b)
        dn2 = dot(qkv[at, :D], w_cq[...], NT)
        dv, dg = norm_back_rows(h1b, rms_of(h1b), g_cross, dn2)
        dg_cross = dg_cross + dg
        dh1 = total[at, :] + dv
        total[at, :] = dh1
        e1 = dh1.astype(bf16)
        turned[:, at] = transposed(e1)
        dmixed[at, :] = dot(e1, w_out[...], NN).astype(bf16)
        if b == 1:
            comm.stage3(F1)
            comm.stage1(CQ, own_of(gr_cq))
    l_q1 = load(4, (qkv_in, qkv))
    comm.stage1(CKV, own_of(gr_ckv))
    wait(l_a1)
    for c in range(2):
        put(gr_out.at[c], dot(turned[...], mixed[:, HALF * c : HALF * (c + 1)], NN))
    comm.offer(SO, gr_out.at[1 - col])
    comm.stage3(F2)
    comm.stage3(CO)
    wait(l_x)
    for at in blocks_of:
        xb = x[at, :].astype(f32)
        turned[:, at] = transposed((xb * rms_of(xb) * g_self).astype(bf16))
    wait(l_t8)
    wait(l_q1)
    table = [rows.at[pl.ds(128 * h, 128)] for h in range(2)]
    spans = [rows.at[pl.ds(256 + 128 * h, 128)] for h in range(2)]
    spans_all[...] = jnp.zeros_like(spans_all)

    def self_heads(hp):
        base = 9 * (hp // 3) + 3 * (hp % 3)
        queries, keys, values = [qkv.at[:, lane(base + n)] for n in range(3)]
        self_backward_body(
            piece_ref,
            queries,
            keys,
            values,
            t8.at[pl.ds(2 * hp, 2)],
            mixed.at[:, lane(hp)],
            dmixed.at[:, lane(hp)],
            lse1.at[pl.ds(hp, 1)],
            queries,
            keys,
            values,
            diag,
            table,
            spans,
            dk_sum,
            dv_sum,
        )
        for h in range(2):
            lined = diag[h, 0:1, :]
            for n in range(1, 8):
                lined = lined + pltpu.roll(diag[h, n : n + 1, :], SPAN - n, 1)
            spans_all[pl.ds(2 * hp + h, 1), :] = lined

    def qkv_grad(j, c):
        return gr_qkv.at[pl.ds(4 * c, 4), :, :, pl.ds(HALF * j, HALF)]

    def grads_of(j):
        for c in range(2):
            at = 3 * HALF * c + HALF * j
            put(qkv_grad(j, c), dot(turned[...], qkv[:, at : at + HALF], NN))
        comm.offer(QA + j, qkv_grad(j, 1 - col))

    def own_qkv(j):
        return lambda r: gr_qkv[4 * col + r, :, :, pl.ds(HALF * j, HALF)]

    self_heads(0)
    comm.stage1(SO, own_of(gr_out))
    comm.stage2(CQ)
    comm.stage2(F0)
    self_heads(3)
    comm.stage2(CKV)
    comm.stage4(F1)
    grads_of(0)
    self_heads(1)
    comm.stage1(QA, own_qkv(0))
    comm.stage2(SO)
    comm.stage3(CQ)
    comm.stage3(CKV)
    comm.stage4(F2)
    comm.stage4(CO)
    comm.stage3(F0)
    self_heads(4)
    comm.stage2(QA)
    comm.stage3(SO)
    comm.stage4(CQ)
    comm.stage5(F1)
    comm.stage4(F0)
    grads_of(1)
    self_heads(2)
    comm.stage1(QB, own_qkv(1))
    comm.stage3(QA)
    comm.stage4(CKV)
    comm.stage5(F2)
    comm.stage5(CO)
    self_heads(5)
    comm.stage2(QB)
    comm.stage4(QA)
    comm.stage4(SO)
    comm.stage5(CQ)
    comm.stage5(CKV)
    comm.stage5(F0)
    grads_of(2)
    comm.stage3(QB)

    wait(l_qkv)
    left = spans_all[...]
    rel = jnp.zeros((16, BUCKETS), f32)
    for _ in range(3):
        high = left.astype(bf16)
        rel = rel + dot(high, onehot_ref[...], NT)
        left = left - high.astype(f32)
    dg_self = jnp.zeros((1, D), f32)
    leaving = []

    def half_of(c):
        return pl.ds(pl.multiple_of(c * HALF, 128), HALF)

    for b, at in enumerate(blocks_of):
        xb = x[at, :].astype(f32)
        dn1 = dot(qkv[at, :], w_big[...], NT)
        dv, dg = norm_back_rows(xb, rms_of(xb), g_self, dn1)
        dg_self = dg_self + dg
        total[at, :] = total[at, :] + dv
        leaving.append(
            comm.remote(
                total.at[at, half_of(1 - col)],
                hidden_grad.at[col, at],
                ex_send.at[2 + b],
                ex_recv.at[2 + b],
                partner,
            )
        )
        kept = pltpu.make_async_copy(
            total.at[at, half_of(col)], hidden_grad.at[col, at], ex_local.at[2 + b]
        )
        kept.start()
        comm.kept.append(kept)
        if b == 0:
            comm.stage1(QC, own_qkv(2))
            comm.stage5(QA)
        if b == 1:
            comm.stage4(QB)
        if b == 2:
            comm.stage2(QC)
            comm.stage5(SO)

    small[0] = jnp.zeros(SMALL, f32)
    small[0, 0:1, :D] = dg_self
    small[0, 1:2, :D] = dg_cross
    small[0, 2:4, :D] = ffn_gains[2:4, :]
    small[0, :, D : D + BUCKETS] = rel
    passing = {}

    def pass_on(slot, src, dst, device):
        passing[slot] = comm.remote(
            small.at[src], small.at[dst], small_send.at[slot], small_recv.at[slot], device
        )

    pass_on(0, 0, 1, partner)
    comm.stage3(QC)
    passing[0].wait_recv()
    small[2] = small[0] + small[1]
    pass_on(1, 2, 3, comm.mate(1))
    comm.stage5(QB)
    passing[1].wait_recv()
    small[4] = small[2] + small[3]
    pass_on(2, 4, 5, comm.mate(2))
    comm.stage4(QC)
    passing[2].wait_recv()
    small[6 + row] = small[4] + small[5]
    for s in range(1, ROWS):
        pass_on(2 + s, 6 + row, 6 + row, (comm.dp, (row + s) % ROWS, col))
    comm.stage5(QC)
    for s in range(1, ROWS):
        passing[2 + s].wait_recv()
    small_out[...] = (small[6] + small[7]) + (small[8] + small[9])
    keep_eg.wait()
    ex_eg.wait_recv()
    for copy in leaving:
        copy.wait_recv()
    comm.finish()


def backward(args, onehot, piece, number):
    shape = jax.ShapeDtypeStruct
    dma = pltpu.SemaphoreType.DMA
    any_spec = pl.BlockSpec(memory_space=pl.ANY)
    vmem = pl.BlockSpec(memory_space=pltpu.VMEM)
    count = len(CHUNKS)
    quarters = (ROWS, QUAD, PIECE)
    scratch = [pltpu.VMEM(quarters + (w,), bf16) for w in CHUNKS]
    for normal, z_first in (
        (lambda w: (ROWS, 2, PIECE, w), lambda w: (2, 2, PIECE, w // 2)),
        (lambda w: (ROWS, PIECE, w), lambda w: (2, PIECE, w // 2)),
        (lambda w: (ROWS - 1, PIECE, w), lambda w: (ROWS - 1, QUAD, PIECE, w)),
    ):
        scratch += [
            pltpu.VMEM((z_first if i in Z_FIRST else normal)(w), bf16)
            for i, w in enumerate(CHUNKS)
        ]
    scratch += [pltpu.VMEM((PIECE, w), bf16) for w in CHUNKS]
    scratch += [
        pltpu.VMEM((2,) + quarters + (HALF,), bf16),
        pltpu.VMEM((2,) + quarters + (HALF,), bf16),
        pltpu.VMEM((2,) + quarters + (2 * HALF,), bf16),
        pltpu.VMEM((2,) + quarters + (HALF,), bf16),
        pltpu.VMEM((2 * ROWS, QUAD, PIECE, 3 * HALF), bf16),
        pltpu.VMEM((L, D), f32),
        pltpu.VMEM((D, L), bf16),
        pltpu.VMEM((L, D), bf16),
        pltpu.VMEM((L, D), bf16),
        pltpu.VMEM((D, 3 * D), bf16),
        pltpu.VMEM((D, D), bf16),
        pltpu.VMEM((D, D), bf16),
        pltpu.VMEM((LE, D), bf16),
        pltpu.VMEM((L // 2, 2 * D), f32),
        pltpu.VMEM((L, 3 * D), bf16),
        pltpu.VMEM((12, 8, SPAN), f32),
        pltpu.VMEM((6, 2, L), f32),
        pltpu.VMEM((6, 2, L), f32),
        pltpu.VMEM((L, D), bf16),
        pltpu.VMEM((L, 128), f32),
        pltpu.VMEM((L, 128), f32),
        pltpu.VMEM((2, 8, SPAN), f32),
        pltpu.VMEM((16, SPAN), f32),
        pltpu.VMEM((2, LE, HALF), f32),
        pltpu.VMEM((6 + ROWS,) + SMALL, f32),
        dma((15, 4)),
        dma((6,)),
        dma((6,)),
        dma((6,)),
        dma((6,)),
        dma((6,)),
        dma((count, 13)),
        dma((count, 13)),
        dma((count,)),
    ]
    out = pl.pallas_call(
        backward_body,
        out_shape=[
            shape((2, L, HALF), f32),
            shape((2, LE, HALF), f32),
        ]
        + [shape((QUAD, PIECE, w), bf16) for w in CHUNKS]
        + [shape(SMALL, f32)],
        in_specs=[any_spec] * 19
        + [vmem] * 3
        + [pl.BlockSpec(memory_space=pltpu.SMEM)],
        out_specs=[any_spec] * (2 + count) + [vmem],
        scratch_shapes=scratch,
        compiler_params=pltpu.CompilerParams(
            collective_id=number, has_side_effects=True, vmem_limit_bytes=VMEM_LIMIT
        ),
        name="backward",
    )(*args, onehot, piece)
    return (out[:2], [o.reshape(BLOCK, o.shape[2]) for o in out[2:-1]], out[-1])


def gelu_parts(t):
    inner = ROOT_TWO_PI * (t + 0.044715 * t * t * t)
    th = jnp.tanh(inner)
    value = 0.5 * t * (1.0 + th)
    slope = 0.5 * (1.0 + th) + 0.5 * t * (1.0 - th * th) * ROOT_TWO_PI * (
        1.0 + 3.0 * 0.044715 * t * t
    )
    return (value, slope)


def body(
    quads,
    hidden_in,
    encoded,
    cotangent,
    piece_start,
    image_piece_lengths,
    bucket_table,
    self_query,
    self_key,
    self_value,
    self_out,
    rel_weight,
    cross_query,
    cross_key,
    cross_value,
    cross_out,
    ffn_gate,
    ffn_up,
    ffn_down,
    gain_self,
    gain_cross,
    gain_ffn,
    gain_final,
):
    col = lax.axis_index("col")
    row = lax.axis_index("row")
    gain_block = jnp.tile(
        jnp.concatenate([gain_self, gain_cross, gain_ffn, gain_final]).reshape(4, HALF), (2, 1)
    )
    rel_block = jnp.pad(rel_weight.astype(f32), ((0, 0), (0, 122)))
    turned_table = bucket_table[:SPAN][::-1]
    onehot = (turned_table[None, :] == jnp.arange(BUCKETS, dtype=jnp.int32)[:, None]).astype(bf16)
    starts = lax.dynamic_index_in_dim(piece_start, col, 0, keepdims=False)
    lengths = lax.dynamic_index_in_dim(image_piece_lengths, col, 0, keepdims=False)
    piece = jnp.concatenate([starts, starts + lengths])
    out = forward(
        (
            hidden_in,
            encoded,
            cotangent,
            self_query,
            self_key,
            self_value,
            self_out.T,
            cross_query,
            cross_key,
            cross_value,
            cross_out.T,
            ffn_gate,
            ffn_up,
            ffn_down.T,
            gain_block,
            rel_block,
        ),
        onehot,
        piece,
        0,
    )
    t8, qkv, a1, lse1, h1, q2, kv2, a2, lse2 = out[:9]
    x, enc, gains, dh2, output, gr_gu, gr_down, ffn_gains = out[14:]
    cut = (2, ROWS, QUAD, PIECE)
    (hidden_grad, enc_grad), grads, small = backward(
        (
            dh2,
            gr_gu.reshape(cut + (2048,)),
            gr_down.reshape(cut + (1024,)),
            t8,
            qkv,
            a1,
            lse1,
            h1,
            q2,
            kv2,
            a2,
            lse2,
            x,
            enc,
            *out[9:14],
            gains,
            ffn_gains,
        ),
        onehot,
        piece,
        1,
    )
    if quads > 1:
        grads, small = jax.tree.map(
            lambda t: lax.psum(t, "dp") * jnp.asarray(1.0 / QUAD, t.dtype), (grads, small)
        )
    grads = [g.astype(f32) for g in grads]
    gr_gate, gr_up, gr_down, gr_co, gr_cq, gr_ckv, gr_out = grads[:7]
    gr_q, gr_k, gr_v = [
        jnp.concatenate([g[:, 128 * n : 128 * (n + 1)] for g in grads[7:]], axis=1)
        for n in range(3)
    ]
    gain_sums = lax.dynamic_slice_in_dim(small[:4], col * HALF, HALF, 1)
    gr_rel = lax.dynamic_slice(small, (col * 6, D + row * 8), (6, 8)).T
    return (
        output,
        hidden_grad,
        enc_grad,
        gr_q,
        gr_k,
        gr_v,
        gr_out.T,
        gr_rel,
        gr_cq,
        gr_ckv[:, :HALF],
        gr_ckv[:, HALF:],
        gr_co.T,
        gr_gate,
        gr_up,
        gr_down.T,
        gain_sums[0],
        gain_sums[1],
        gain_sums[2],
        gain_sums[3],
    )


def solution(mesh):
    batch = P(("dp", "row"), None, "col")
    inward = P("row", "col")
    outward = P("col", "row")
    gain = P("col")
    weights = (
        (inward,) * 3 + (outward, inward) + (inward,) * 3 + (outward,) + (inward,) * 2 + (outward,)
    )
    placed = (batch,) * 3 + (P(("dp", "row"), None),) * 2 + (P(),) + weights + (gain,) * 4
    return jax.shard_map(
        lambda *args: body(mesh.shape["dp"] // QUAD, *args),
        mesh=mesh,
        in_specs=placed,
        out_specs=(batch,) * 3 + weights + (gain,) * 4,
        check_vma=False,
    )
```
